32 devices in a mesh: replica: 16 (over z, y, core), fsdp: 2 (over x).
Axes of the slice: x: 2, y: 2, z: 4, core: 2. Of those that a mesh axis runs over, the one named last changes fastest.
Arguments:
- inputs: bfloat16 [16384, 1024], P(('replica', 'fsdp')), may hold values from -6 to 6
- segments: int32 [16, 1024], P('replica', 'fsdp'), may hold values from 0 to 66, as said below
- cotangent: bfloat16 [16384, 1024], P(('replica', 'fsdp')), may hold values from -6 to 6
- mixer_gain: bfloat16 [1024], P('fsdp'), may hold values from 0.5 to 1.5
- query_map: bfloat16 [1024, 512], P('fsdp'), may hold values from -0.1875 to 0.1875
- key_map: bfloat16 [1024, 512], P('fsdp'), may hold values from -0.1875 to 0.1875
- value_map: bfloat16 [1024, 1024], P('fsdp'), may hold values from -0.1875 to 0.1875
- swish_map: bfloat16 [1024, 1024], P('fsdp'), may hold values from -0.1875 to 0.1875
- squeeze: bfloat16 [1024, 16], P('fsdp'), may hold values from -0.1875 to 0.1875
- expand: bfloat16 [16, 512], P(None, 'fsdp'), may hold values from -1.5 to 1.5
- forget_bias: bfloat16 [512], P('fsdp'), may hold values from -2 to 6
- head_gain: bfloat16 [256], P('fsdp'), may hold values from 0.5 to 1.5
- readout: bfloat16 [1024, 1024], P('fsdp'), may hold values from -0.25 to 0.25
- feed_gain: bfloat16 [1024], P('fsdp'), may hold values from 0.5 to 1.5
- gate_map: bfloat16 [1024, 2816], P('fsdp'), may hold values from -0.1875 to 0.1875
- up_map: bfloat16 [1024, 2816], P('fsdp'), may hold values from -0.1875 to 0.1875
- down_map: bfloat16 [2816, 1024], P('fsdp'), may hold values from -0.21875 to 0.21875
Outputs:
- output: bfloat16 [16384, 1024], P(('replica', 'fsdp'))
- grad_input: bfloat16 [16384, 1024], P(('replica', 'fsdp'))
- grad_mixer: float32 [1024], P('fsdp')
- grad_query: float32 [1024, 512], P('fsdp')
- grad_key: float32 [1024, 512], P('fsdp')
- grad_value: float32 [1024, 1024], P('fsdp')
- grad_swish: float32 [1024, 1024], P('fsdp')
- grad_squeeze: float32 [1024, 16], P('fsdp')
- grad_expand: float32 [16, 512], P(None, 'fsdp')
- grad_bias: float32 [512], P('fsdp')
- grad_heads: float32 [256], P('fsdp')
- grad_readout: float32 [1024, 1024], P('fsdp')
- grad_feed: float32 [1024], P('fsdp')
- grad_gate: float32 [1024, 2816], P('fsdp')
- grad_up: float32 [1024, 2816], P('fsdp')
- grad_down: float32 [2816, 1024], P('fsdp')
The draws below stay inside these ranges and needn't reach their ends.
Inputs may be any that keep to these rules, and one draw needn't show every extreme that they name: `segments`: along each sequence the document numbers start at 0 and rise by 0 or 1 from token to token; in every sequence one document begins among the first 512 tokens and ends among the last 512, and the last token's number is 66.
All inputs are finite; a program needn't handle non-finite values.
Results may differ from the reference program's by a relative error of at most 0.035.
Values may be sent and summed in bfloat16 or wider, within the bound.
No kernel may reach another device: no remote copies, remote signals or barrier semaphores. Data moves between devices by JAX's collectives and lax.ppermute only.
A program may use at most 192 MiB of HBM per device.

```python
import jax
import jax.numpy as jnp
from jax import lax

D = 1024
HEADS = 4
DK = 128
DV = 256
RANK = 16
FF = 2816
SPAN = 64
TOK_DEV = 512
SEQ = 1024
NSEQ = 16
TOKENS = 16384


def draw_segments(key, part):
    key = jax.random.fold_in(key, 11)
    keys = jax.random.split(key, 3)
    places = jnp.arange(SEQ, dtype=jnp.int32)[None, :]
    half = TOK_DEV // 2
    begin = jax.random.randint(keys[0], (NSEQ, 1), half, TOK_DEV)
    finish = jax.random.randint(keys[1], (NSEQ, 1), SEQ - TOK_DEV + 1, SEQ - half + 1)
    outside = (places > 0) & (places < begin) | (places > finish)
    scores = jax.random.randint(keys[2], (NSEQ, SEQ), 0, 2 ** 30 // SEQ) * SEQ + places
    scores = jnp.where(outside, scores, -1)
    picked = lax.top_k(scores, TOK_DEV // 8)[1].astype(jnp.int32)
    rows = jnp.arange(NSEQ, dtype=jnp.int32)[:, None]
    starts = jnp.zeros((NSEQ, SEQ), jnp.int32).at[rows, picked].set(1)
    ends = ((places == begin) | (places == finish)).astype(jnp.int32)
    starts = jnp.maximum(starts, ends)
    return jnp.cumsum(starts, axis=1).astype(jnp.int32)


def block_levels(own_key, dims, pieces, least, largest):
    level = 1.0
    for axis_at, shards_of in pieces:
        steps = jax.random.uniform(jax.random.fold_in(jax.random.fold_in(own_key, 6), axis_at), (shards_of,), jnp.float32, least / len(pieces), largest / len(pieces))
        level = level * jnp.repeat(jnp.exp(steps), dims[axis_at] // shards_of).reshape((-1,) + (1,) * (len(dims) - 1 - axis_at))
    return level


def normal_values(own_key, shape, scale, most, cuts=(), held_as=jnp.bfloat16):
    drawn = scale * jax.random.normal(own_key, shape, jnp.float32)
    if cuts:
        drawn = drawn * block_levels(own_key, shape, cuts, -0.22, 0.18)
    return jnp.clip(drawn, -most, most).astype(held_as)


def setup_inputs(seed: int = 0) -> dict:
    seeds = jax.random.split(jax.random.key(seed), 18)
    inputs = normal_values(seeds[0], (TOKENS, D), 1.0, 6.0, ((0, 32),))
    segments = draw_segments(jax.random.fold_in(seeds[17], 71), 0)
    cotangent = normal_values(seeds[2], (TOKENS, D), 1.0, 6.0, ((0, 32),))
    mixer_gain = jnp.clip(1.0 + 0.1 * jax.random.normal(seeds[3], (D,), jnp.float32), 0.5, 1.5).astype(jnp.bfloat16)
    query_map = normal_values(seeds[4], (D, HEADS * DK), D ** -0.5, 0.1875, ((0, 2),))
    key_map = normal_values(seeds[5], (D, HEADS * DK), D ** -0.5, 0.1875, ((0, 2),))
    value_map = normal_values(seeds[6], (D, HEADS * DV), D ** -0.5, 0.1875, ((0, 2),))
    swish_map = normal_values(seeds[7], (D, HEADS * DV), D ** -0.5, 0.1875, ((0, 2),))
    squeeze = normal_values(seeds[8], (D, RANK), D ** -0.5, 0.1875, ((0, 2),))
    expand = normal_values(seeds[9], (RANK, HEADS * DK), RANK ** -0.5, 1.5, ((1, 2),))
    forget_bias = jnp.clip(-2.0 + 8.0 * jax.random.uniform(seeds[10], (HEADS * DK,), jnp.float32) ** block_levels(seeds[10], (HEADS * DK,), ((0, 2),), -0.2, 0.2), -2.0, 6.0).astype(jnp.bfloat16)
    head_gain = jnp.clip(1.0 + 0.1 * jax.random.normal(seeds[11], (DV,), jnp.float32), 0.5, 1.5).astype(jnp.bfloat16)
    readout = normal_values(seeds[12], (HEADS * DV, D), (HEADS * DV // 2) ** -0.5, 0.25, ((0, 2),))
    feed_gain = jnp.clip(1.0 + 0.1 * jax.random.normal(seeds[13], (D,), jnp.float32), 0.5, 1.5).astype(jnp.bfloat16)
    gate_map = normal_values(seeds[14], (D, FF), D ** -0.5, 0.1875, ((0, 2),))
    up_map = normal_values(seeds[15], (D, FF), D ** -0.5, 0.1875, ((0, 2),))
    down_map = normal_values(seeds[16], (FF, D), (FF // 4) ** -0.5, 0.21875, ((0, 2),))
    return {"inputs": inputs, "segments": segments, "cotangent": cotangent, "mixer_gain": mixer_gain, "query_map": query_map, "key_map": key_map, "value_map": value_map, "swish_map": swish_map, "squeeze": squeeze, "expand": expand, "forget_bias": forget_bias, "head_gain": head_gain, "readout": readout, "feed_gain": feed_gain, "gate_map": gate_map, "up_map": up_map, "down_map": down_map}


EPSILON = 1e-06
HEAD_FLOOR = 16.0
GATE_NORM = 16.0
HIGH = lax.Precision.HIGHEST

@jax.custom_vjp
def low(v):
    return lax.optimization_barrier(v.astype(jnp.bfloat16)).astype(jnp.float32)

@jax.custom_vjp
def low_back(v):
    return v

def low_keep(v):
    return (low(v), None)

def low_pass(kept, grad):
    return (grad,)

def back_keep(v):
    return (v, None)

def back_low(kept, grad):
    return (low(grad),)
low.defvjp(low_keep, low_pass)
low_back.defvjp(back_keep, back_low)

def matmul(left, right):
    return jnp.dot(left, right, precision=HIGH, preferred_element_type=jnp.float32)

def rms_scale(values, gain):
    mean_sq = lax.optimization_barrier(jnp.mean(values * values, axis=-1, keepdims=True))
    return values * lax.rsqrt(mean_sq + EPSILON) * gain

def head_scale(values, gain):
    mean_sq = lax.optimization_barrier(jnp.mean(values * values, axis=-1, keepdims=True))
    return values * lax.rsqrt(mean_sq + HEAD_FLOOR) * gain

def block_step(carry, block):
    state, last = carry
    queries, keys, values, decay, marks = block
    cumul = jnp.cumsum(decay, axis=0)
    width = marks.shape[0]
    places = jnp.arange(width, dtype=jnp.int32)
    causal = (places[:, None] >= places[None, :]) & (marks[:, None] == marks[None, :])
    lifted = queries * jnp.exp(cumul)
    lowered = keys * jnp.exp(-cumul)
    scores = jnp.einsum('thc,shc->hts', lifted, lowered, precision=HIGH)
    scores = jnp.where(causal[None], scores, 0.0)
    within = jnp.einsum('hts,shv->thv', scores, values, precision=HIGH)
    carried = jnp.where((marks == last)[:, None, None], lifted, 0.0)
    across = jnp.einsum('thc,hcv->thv', carried, state, precision=HIGH)
    tail = jnp.where((marks == marks[-1])[:, None, None], jnp.exp(cumul[-1][None] - cumul) * keys, 0.0)
    keeping = jnp.where(marks[-1] == last, jnp.exp(cumul[-1]), 0.0)
    state = keeping[:, :, None] * state + jnp.einsum('shc,shv->hcv', tail, values, precision=HIGH)
    return ((state, marks[-1].astype(jnp.int32)), within + across)

def recurrence(queries, keys, values, decay, marks):
    length = marks.shape[0]
    count = length // SPAN
    blocks = (queries.reshape(count, SPAN, HEADS, DK), keys.reshape(count, SPAN, HEADS, DK), values.reshape(count, SPAN, HEADS, DV), decay.reshape(count, SPAN, HEADS, DK), marks.reshape(count, SPAN))
    start = (jnp.zeros((HEADS, DK, DV), queries.dtype), marks[0].astype(jnp.int32))
    final, mixed = lax.scan(jax.checkpoint(block_step), start, blocks)
    return mixed.reshape(length, HEADS, DV)

def forward(params, tokens, marks):
    mixer_gain, query_map, key_map, value_map, swish_map, squeeze, expand, forget_bias, head_gain, readout, feed_gain, gate_map, up_map, down_map = params
    length = tokens.shape[0]
    normed = low(rms_scale(tokens, mixer_gain))
    queries = low_back(low(matmul(normed, query_map))).reshape(length, HEADS, DK)
    keys = low_back(low(matmul(normed, key_map))).reshape(length, HEADS, DK)
    values = low_back(low(matmul(normed, value_map))).reshape(length, HEADS, DV)
    narrow = low_back(low(matmul(normed, squeeze)))
    decay_pre = low_back(matmul(narrow, expand)) + forget_bias
    decay = (jax.nn.log_sigmoid(decay_pre) / GATE_NORM).reshape(length, HEADS, DK)
    swish_pre = low_back(matmul(normed, swish_map)).reshape(length, HEADS, DV)
    mixed = recurrence(queries, keys, values, decay, marks)
    gated = low(head_scale(mixed, head_gain) * jax.nn.silu(swish_pre)).reshape(length, HEADS * DV)
    hidden = tokens + low_back(matmul(gated, readout))
    second = low(rms_scale(hidden, feed_gain))
    gate = low_back(matmul(second, gate_map))
    upward = low_back(matmul(second, up_map))
    inner = low(jax.nn.silu(gate) * upward)
    return hidden + low_back(matmul(inner, down_map))

def reference(inputs, segments, cotangent, mixer_gain, query_map, key_map, value_map, swish_map, squeeze, expand, forget_bias, head_gain, readout, feed_gain, gate_map, up_map, down_map):
    params = tuple((weight.astype(jnp.float32) for weight in (mixer_gain, query_map, key_map, value_map, swish_map, squeeze, expand, forget_bias, head_gain, readout, feed_gain, gate_map, up_map, down_map)))
    rows = inputs.astype(jnp.float32).reshape(NSEQ, SEQ, D)
    tangents = cotangent.astype(jnp.float32).reshape(NSEQ, SEQ, D)
    labels = segments.astype(jnp.int32)

    def one_sequence(total, item):
        tokens, tangent, marks = item

        def apply(token_rows, weights):
            return forward(weights, token_rows, marks)
        result, pullback = jax.vjp(apply, tokens, params)
        grad_tokens, grad_params = pullback(tangent)
        total = jax.tree.map(lambda first, second: first + second, total, grad_params)
        return (total, (result, grad_tokens))
    zeros = jax.tree.map(jnp.zeros_like, params)
    total, (results, grad_rows) = lax.scan(one_sequence, zeros, (rows, tangents, labels))
    return (results.reshape(TOKENS, D).astype(jnp.bfloat16), grad_rows.reshape(TOKENS, D).astype(jnp.bfloat16), total[0], total[1], total[2], total[3], total[4], total[5], total[6], total[7], total[8], total[9], total[10], total[11], total[12], total[13])
```

```python
import functools

import jax
import jax.numpy as jnp
from jax import lax
from jax.experimental import pallas as pl
from jax.experimental.pallas import tpu as pltpu
from jax.sharding import PartitionSpec as P

HEADS = 4
DK = 128
DV = 256
SPAN = 64
WIDE = 2 * SPAN

EPSILON = 1e-06
HEAD_FLOOR = 16.0
GATE_NORM = 16.0

F32 = jnp.float32
BF16 = jnp.bfloat16
VMEM_BYTES = 56 * 1024 * 1024

ROW_EXPAND = 16
ROW_MIXER = 32
ROW_FEED = 33
ROW_MIXED = 34
SMALL_ROWS = 48
LANE_EXPAND = 16
LANE_MIXER = 32
LANE_FEED = 33
LANE_BIAS = 34
LANE_HEADS = 35


def nn(a, b):
    return lax.dot_general(a, b, (((1,), (0,)), ((), ())), preferred_element_type=F32)


def nt(a, b):
    return lax.dot_general(a, b, (((1,), (1,)), ((), ())), preferred_element_type=F32)


def tn(a, b):
    return lax.dot_general(a, b, (((0,), (0,)), ((), ())), preferred_element_type=F32)


def sigmoid(v):
    return 1.0 / (1.0 + jnp.exp(-v))


def call(kernel, out_shape, **kw):
    return pl.pallas_call(
        kernel,
        out_shape=out_shape,
        compiler_params=pltpu.CompilerParams(vmem_limit_bytes=VMEM_BYTES),
        **kw,
    )


def sds(shape, dtype):
    return jax.ShapeDtypeStruct(shape, dtype)


SMEM = pl.BlockSpec(memory_space=pltpu.SMEM)
VMEM = pl.BlockSpec(memory_space=pltpu.VMEM)


def split_sum(ones, values):
    high = values.astype(BF16)
    rest = values - high.astype(F32)
    middle = rest.astype(BF16)
    low = (rest - middle.astype(F32)).astype(BF16)
    return nn(ones, high) + nn(ones, middle) + nn(ones, low)


def lower_ones(size):
    rows = lax.broadcasted_iota(jnp.int32, (size, size), 0)
    cols = lax.broadcasted_iota(jnp.int32, (size, size), 1)
    return (rows >= cols).astype(F32).astype(BF16)


def upper_ones(size):
    rows = lax.broadcasted_iota(jnp.int32, (size, size), 0)
    cols = lax.broadcasted_iota(jnp.int32, (size, size), 1)
    return (rows <= cols).astype(F32).astype(BF16)


def log_decay(pre):
    return (jnp.minimum(pre, 0.0) - jnp.log1p(jnp.exp(-jnp.abs(pre)))) / GATE_NORM


def row_of(small_ref, row):
    return small_ref[ROW_MIXER:SMALL_ROWS, :].astype(F32)[row - ROW_MIXER : row - ROW_MIXER + 1, :]


def expand_of(small_ref):
    half = small_ref.shape[1] // 2
    quarter = half // 2
    part = small_ref[ROW_EXPAND:ROW_MIXER, :]
    return jnp.concatenate([part[:, :quarter], part[:, half : half + quarter]], axis=1)


def bias_of(small_ref):
    half = small_ref.shape[1] // 2
    quarter = half // 2
    row = row_of(small_ref, ROW_MIXED)
    return jnp.concatenate([row[:, :quarter], row[:, half : half + quarter]], axis=1)


def head_gain_of(small_ref):
    half = small_ref.shape[1] // 2
    at = half // 2
    count = DV // 2
    row = row_of(small_ref, ROW_MIXED)
    return jnp.concatenate([row[:, at : at + count], row[:, half + at : half + at + count]], axis=1)


def place_rows(who_ref, full_ref, own, pieces):
    x = who_ref[0]
    q = who_ref[1]
    half = own.shape[0]
    rows = pieces[0].shape[0]
    full_ref[pl.ds(pl.multiple_of(x * half, half), half), :] = own
    for k in range(4):
        at = (1 - x) * half + (q ^ k) * rows
        full_ref[pl.ds(pl.multiple_of(at, rows), rows), :] = pieces[k]


def place_grads(who_ref, keep_ref, send_ref, scratch_ref, row, cols, rows=32):
    x = who_ref[0]
    me = who_ref[2]
    half = scratch_ref.shape[0] // 2
    for core, out_ref in ((0, keep_ref), (1, send_ref)):
        for xx in range(2):
            for yy in range(2):
                for zz in range(4):
                    block = me ^ (core * 8 + yy * 4 + zz)
                    at = pl.multiple_of((x ^ xx) * half + block * rows, rows)
                    out_ref[xx, yy, zz, row : row + rows, cols] = scratch_ref[pl.ds(at, rows), :]


def project_kernel(
    who, x, small, q_own, k_own, v_own, r0, r1, r2, r3, normed, qkv, pre, narrow_out, full
):
    j = pl.program_id(0)

    @pl.when(j == 0)
    def _():
        tokens = x[...].astype(F32)
        mean_sq = jnp.mean(tokens * tokens, axis=-1, keepdims=True)
        normed[...] = (
            tokens * lax.rsqrt(mean_sq + EPSILON) * row_of(small, ROW_MIXER)
        ).astype(BF16)
        narrow = nt(normed[...], small[0:ROW_EXPAND, :]).astype(BF16)
        narrow_out[...] = narrow
        pre[...] = nn(narrow, expand_of(small)) + bias_of(small)

    pieces = [r[...] for r in (r0, r1, r2, r3)]

    @pl.when(j < 2)
    def _():
        place_rows(who, full, q_own[...], pieces)

    @pl.when((j >= 2) & (j < 4))
    def _():
        place_rows(who, full, k_own[...], pieces)

    @pl.when(j >= 4)
    def _():
        place_rows(who, full, v_own[...], pieces)

    qkv[...] = nn(normed[...], full[...]).astype(BF16)


def project(who, x, small, q_own, k_own, v_own, pieces):
    t, d = x.shape
    half = d // 2
    kd = HEADS * DK
    vd = HEADS * DV
    width = 2 * kd + vd
    const = lambda j: (0, 0)
    qn = kd // 256
    vn = vd // 256
    return call(
        project_kernel,
        (sds((t, d), BF16), sds((t, width), BF16), sds((t, kd), F32), sds((t, 16), BF16)),
        grid=(width // 256,),
        in_specs=[
            SMEM,
            pl.BlockSpec((t, d), const),
            pl.BlockSpec(small.shape, const),
            pl.BlockSpec((half, 256), lambda j: (0, jnp.minimum(j, qn - 1))),
            pl.BlockSpec((half, 256), lambda j: (0, jnp.clip(j - qn, 0, qn - 1))),
            pl.BlockSpec((half, 256), lambda j: (0, jnp.clip(j - 2 * qn, 0, vn - 1))),
        ]
        + [pl.BlockSpec((half // 4, 256), lambda j: (0, j))] * 4,
        out_specs=(
            pl.BlockSpec((t, d), const),
            pl.BlockSpec((t, 256), lambda j: (0, j)),
            pl.BlockSpec((t, kd), const),
            pl.BlockSpec((t, 16), const),
        ),
        scratch_shapes=[pltpu.VMEM((d, 256), BF16)],
    )(who, x, small, q_own, k_own, v_own, *pieces)


def swish_kernel(who, normed, own, r0, r1, r2, r3, out, full):
    place_rows(who, full, own[...], [r[...] for r in (r0, r1, r2, r3)])
    out[...] = nn(normed[...], full[...])


def swish_project(who, normed, own, pieces):
    t, d = normed.shape
    half = d // 2
    vd = HEADS * DV
    return call(
        swish_kernel,
        sds((t, vd), F32),
        grid=(vd // 256,),
        in_specs=[
            SMEM,
            pl.BlockSpec((t, d), lambda j: (0, 0)),
            pl.BlockSpec((half, 256), lambda j: (0, j)),
        ]
        + [pl.BlockSpec((half // 4, 256), lambda j: (0, j))] * 4,
        out_specs=pl.BlockSpec((t, 256), lambda j: (0, j)),
        scratch_shapes=[pltpu.VMEM((d, 256), BF16)],
    )(who, normed, own, *pieces)


def mark_at(mrow, place):
    return mrow[0:1, place : place + 1]


def state_kernel(qkv, pre, mcol, mrow, payload, passing):
    t = pre.shape[0]
    kd = HEADS * DK
    ones = lower_ones(WIDE)
    states = [jnp.zeros((DV, DK), F32) for _ in range(HEADS)]
    total = jnp.zeros((1, kd), F32)
    for i in range(t // WIDE):
        rows = slice(i * WIDE, (i + 1) * WIDE)
        cumul = split_sum(ones, log_decay(pre[rows, :]))
        end = cumul[WIDE - 1 : WIDE, :]
        total = total + end
        last = mark_at(mrow, (i + 1) * WIDE - 1)
        keys = qkv[rows, kd : 2 * kd].astype(F32)
        tail = jnp.where(mcol[rows, :] == last, keys * jnp.exp(end - cumul), 0.0).astype(BF16)
        if i:
            keep = jnp.where(mark_at(mrow, i * WIDE - 1) == last, jnp.exp(end), 0.0)
        for h in range(HEADS):
            c = slice(h * DK, (h + 1) * DK)
            values = qkv[rows, 2 * kd + h * DV : 2 * kd + (h + 1) * DV]
            update = tn(values, tail[:, c])
            states[h] = states[h] * keep[:, c] + update if i else update
    for h in range(HEADS):
        payload[h * DV : (h + 1) * DV, :] = states[h].astype(BF16)
    last = mark_at(mrow, t - 1)
    payload[HEADS * DV :, :] = jnp.broadcast_to(last, (16, DK)).astype(BF16)
    passes = jnp.where(mark_at(mrow, 0) == last, jnp.exp(total), 0.0)
    passing[...] = jnp.broadcast_to(passes, passing.shape)


def local_state(qkv, pre, mcol, mrow):
    return call(
        state_kernel,
        (sds((HEADS * DV + 16, DK), BF16), sds((8, HEADS * DK), F32)),
    )(qkv, pre, mcol, mrow)


def mixer_kernel(
    who, x, small, qkv, pre, swish, mcol, mrow, payload, own, r0, r1, r2, r3,
    mixed_out, states_out, gated_out, hidden_out, second_out, full,
):
    t, d = x.shape
    kd = HEADS * DK
    ones = lower_ones(WIDE)
    causal_rows = lax.broadcasted_iota(jnp.int32, (WIDE, WIDE), 0)
    causal_cols = lax.broadcasted_iota(jnp.int32, (WIDE, WIDE), 1)
    states = [payload[h * DV : (h + 1) * DV, :].astype(F32) for h in range(HEADS)]
    before = payload[HEADS * DV :, :].astype(F32)[0:1, 0:1]
    place_rows(who, full, own[...], [r[...] for r in (r0, r1, r2, r3)])
    for i in range(t // WIDE):
        rows = slice(i * WIDE, (i + 1) * WIDE)
        marks = mcol[rows, :]
        last = mark_at(mrow, (i + 1) * WIDE - 1)
        cumul = split_sum(ones, log_decay(pre[rows, :]))
        middle = cumul[SPAN - 1 : SPAN, :]
        end = cumul[WIDE - 1 : WIDE, :]
        queries = qkv[rows, 0:kd].astype(F32)
        keys = qkv[rows, kd : 2 * kd].astype(F32)
        lifted = (queries * jnp.exp(cumul - middle)).astype(BF16)
        lowered = (keys * jnp.exp(middle - cumul)).astype(BF16)
        carried = jnp.where(marks == before, queries * jnp.exp(cumul), 0.0).astype(BF16)
        tail = jnp.where(marks == last, keys * jnp.exp(end - cumul), 0.0).astype(BF16)
        keep = jnp.where(before == last, jnp.exp(end), 0.0)
        causal = (causal_rows >= causal_cols) & (marks == mrow[0:1, rows])
        for h in range(HEADS):
            c = slice(h * DK, (h + 1) * DK)
            values = qkv[rows, 2 * kd + h * DV : 2 * kd + (h + 1) * DV]
            low_state = states[h].astype(BF16)
            states_out[i, h] = low_state
            scores = jnp.where(causal, nt(lifted[:, c], lowered[:, c]), 0.0).astype(BF16)
            mixed_out[rows, h * DV : (h + 1) * DV] = nn(scores, values) + nt(
                carried[:, c], low_state
            )
            states[h] = states[h] * keep[:, c] + tn(values, tail[:, c])
        before = last
    gain = head_gain_of(small)
    for h in range(HEADS):
        c = slice(h * DV, (h + 1) * DV)
        mixed = mixed_out[:, c]
        scale = lax.rsqrt(jnp.mean(mixed * mixed, axis=-1, keepdims=True) + HEAD_FLOOR)
        pre_gate = swish[:, c]
        gated_out[:, c] = (mixed * scale * gain * (pre_gate * sigmoid(pre_gate))).astype(BF16)
    hidden = x[...].astype(F32) + nn(gated_out[...], full[...])
    hidden_out[...] = hidden
    mean_sq = jnp.mean(hidden * hidden, axis=-1, keepdims=True)
    second_out[...] = (
        hidden * lax.rsqrt(mean_sq + EPSILON) * row_of(small, ROW_FEED)
    ).astype(BF16)


def mixer(who, x, small, qkv, pre, swish, mcol, mrow, payload, own, pieces):
    t, d = x.shape
    vd = HEADS * DV
    quarter = own.shape[0] // 4
    right = pl.BlockSpec((quarter, d), lambda i: (0, 1))
    whole = lambda a: pl.BlockSpec(a.shape, lambda i: (0,) * a.ndim)
    outs = (
        sds((t, vd), F32),
        sds((t // WIDE, HEADS, DV, DK), BF16),
        sds((t, vd), BF16),
        sds((t, d), F32),
        sds((t, d), BF16),
    )
    ins = (x, small, qkv, pre, swish, mcol, mrow, payload, own)
    return call(
        mixer_kernel,
        outs,
        grid=(1,),
        in_specs=[SMEM] + [whole(a) for a in ins] + [right] * 4,
        out_specs=tuple(whole(a) for a in outs),
        scratch_shapes=[pltpu.VMEM((vd, d), BF16)],
    )(who, *ins, *pieces)


def feed_kernel(
    who, second, cot, g0, g1, u0, u1, down, r0, r1, r2, r3, *rest, first, blocks
):
    if first:
        total_out, total_ds, keep, send, wg, wu, wd, sec_t, cot_t, sg_, su_, sd_ = rest
    else:
        in_out, in_ds, total_out, total_ds, keep, send, wg, wu, wd, sec_t, cot_t, sg_, su_, sd_ = rest
    j = pl.program_id(0)

    @pl.when(j == 0)
    def _():
        if first:
            total_out[...] = jnp.zeros_like(total_out)
            total_ds[...] = jnp.zeros_like(total_ds)
        else:
            total_out[...] = in_out[...]
            total_ds[...] = in_ds[...]
        sec_t[...] = second[...].T
        cot_t[...] = cot[...].T

    x = who[0]
    q = who[1]
    half = g0.shape[0]
    rows = pl.ds(pl.multiple_of(x * half, half), half)
    wg[rows, 0:128] = g0[...]
    wg[rows, 128:256] = g1[...]
    wu[rows, 0:128] = u0[...]
    wu[rows, 128:256] = u1[...]
    wd[pl.ds(pl.multiple_of(x * 128, 128), 128), :] = down[...]
    for k, r in enumerate((r0, r1, r2, r3)):
        at = q ^ k
        rows = pl.ds(pl.multiple_of((1 - x) * half + at * 128, 128), 128)
        wg[rows, :] = r[:, 0:256]
        wu[rows, :] = r[:, 256:512]
        wd[pl.ds(pl.multiple_of((1 - x) * 128, 128), 128), pl.ds(pl.multiple_of(at * 256, 256), 256)] = r[:, 512:768]
    gate = nn(second[...], wg[...])
    upward = nn(second[...], wu[...])
    d_inner = nt(cot[...], wd[...])
    sig = sigmoid(gate)
    silu = gate * sig
    inner = (silu * upward).astype(BF16)
    d_gate = (d_inner * upward * sig * (1.0 + gate * (1.0 - sig))).astype(BF16)
    d_up = (d_inner * silu).astype(BF16)
    total_out[...] += nn(inner, wd[...])
    total_ds[...] += nt(d_gate, wg[...]) + nt(d_up, wu[...])
    sg_[...] = nn(sec_t[...], d_gate).astype(BF16)
    su_[...] = nn(sec_t[...], d_up).astype(BF16)
    grad_down = tn(inner, cot[...]).astype(BF16)
    for part in range(2):
        for cb in range(4):
            at = part * half + cb * 128
            sd_[at : at + 128, :] = grad_down[part * 128 : (part + 1) * 128, cb * 256 : (cb + 1) * 256]
    cols = slice(0, 256)
    place_grads(who, keep, send, sg_, 0, cols)
    place_grads(who, keep, send, su_, 32, cols)
    place_grads(who, keep, send, sd_, 64, cols)


def feed(who, second, cot, gate_own, up_own, down_own, pieces, totals, start, blocks):
    t, d = second.shape
    half = d // 2
    ff = gate_own.shape[1]
    halves = ff // 256
    const = lambda j: (0, 0)
    first = totals is None
    left = pl.BlockSpec((half, 128), lambda j: (0, start + j))
    right = pl.BlockSpec((half, 128), lambda j: (0, halves + start + j))
    full = pl.BlockSpec((t, d), const)
    grads = pl.BlockSpec((2, 2, 4, 96, 256), lambda j: (0, 0, 0, 0, j))
    grads_shape = sds((2, 2, 4, 96, blocks * 256), BF16)
    return call(
        functools.partial(feed_kernel, first=first, blocks=blocks),
        (sds((t, d), F32), sds((t, d), F32), grads_shape, grads_shape),
        grid=(blocks,),
        in_specs=[
            SMEM, full, full, left, right, left, right,
            pl.BlockSpec((128, d), lambda j: (start + j, 0)),
        ]
        + [pl.BlockSpec((half // 4, 768), lambda j: (0, j))] * 4
        + ([] if first else [full, full]),
        out_specs=(full, full, grads, grads),
        scratch_shapes=[
            pltpu.VMEM((d, 256), BF16),
            pltpu.VMEM((d, 256), BF16),
            pltpu.VMEM((256, d), BF16),
            pltpu.VMEM((d, t), BF16),
            pltpu.VMEM((d, t), BF16),
            pltpu.VMEM((d, 256), BF16),
            pltpu.VMEM((d, 256), BF16),
            pltpu.VMEM((d, 256), BF16),
        ],
    )(
        who, second, cot, gate_own, gate_own, up_own, up_own, down_own, *pieces,
        *(() if first else totals),
    )


def pack_kernel(who, g0, g1, u0, u1, down, out):
    out[:, 0:128] = g0[...]
    out[:, 128:256] = g1[...]
    out[:, 256:384] = u0[...]
    out[:, 384:512] = u1[...]
    out[:, 512:768] = down[...]


def pack_feed(who, gate_own, up_own, down_own, start, blocks):
    half, ff = gate_own.shape
    halves = ff // 256
    quarter = half // 4
    left = pl.BlockSpec((quarter, 128), lambda j, w: (w[1], start + j))
    right = pl.BlockSpec((quarter, 128), lambda j, w: (w[1], halves + start + j))
    return pl.pallas_call(
        pack_kernel,
        out_shape=sds((quarter, blocks * 768), BF16),
        grid_spec=pltpu.PrefetchScalarGridSpec(
            num_scalar_prefetch=1,
            grid=(blocks,),
            in_specs=[
                left, right, left, right,
                pl.BlockSpec((128, down_own.shape[1] // 4), lambda j, w: (start + j, w[1])),
            ],
            out_specs=pl.BlockSpec((quarter, 768), lambda j, w: (0, j)),
        ),
    )(who, gate_own, gate_own, up_own, up_own, down_own)


def mixer_back_kernel(
    who, small, d_second, hidden, cot, swish, mixed, qkv, pre, mcol, payload,
    own, r0, r1, r2, r3,
    d_hidden_out, low_out, d_swish_out, d_mixed_out, rows_out, back_out, full, d_gated,
):
    t, d = hidden.shape
    kd = HEADS * DK
    place_rows(who, full, own[...], [r[...] for r in (r0, r1, r2, r3)])
    values = hidden[...]
    upstream = d_second[...]
    scale = lax.rsqrt(jnp.mean(values * values, axis=-1, keepdims=True) + EPSILON)
    rows_out[...] = jnp.zeros_like(rows_out)
    rows_out[0:1, :] = jnp.sum(upstream * values * scale, axis=0, keepdims=True)
    scaled = upstream * row_of(small, ROW_FEED)
    mean = jnp.mean(scaled * values, axis=-1, keepdims=True)
    d_hidden = cot[...].astype(F32) + scale * scaled - values * (scale * scale * scale * mean)
    d_hidden_out[...] = d_hidden
    low_out[...] = d_hidden.astype(BF16)
    d_gated[...] = nt(low_out[...], full[...])
    gain = head_gain_of(small)
    grad_heads = jnp.zeros((1, DV), F32)
    for h in range(HEADS):
        c = slice(h * DV, (h + 1) * DV)
        values = mixed[:, c]
        scale = lax.rsqrt(jnp.mean(values * values, axis=-1, keepdims=True) + HEAD_FLOOR)
        pre_gate = swish[:, c]
        sig = sigmoid(pre_gate)
        up = d_gated[:, c]
        unit = values * scale
        d_swish_out[:, c] = (up * unit * gain * sig * (1.0 + pre_gate * (1.0 - sig))).astype(BF16)
        err = up * pre_gate * sig
        grad_heads = grad_heads + jnp.sum(err * unit, axis=0, keepdims=True)
        scaled = err * gain
        mean = jnp.mean(scaled * unit, axis=-1, keepdims=True)
        d_mixed_out[:, c] = (scale * (scaled - unit * mean)).astype(BF16)
    rows_out[1:2, 0:DV] = grad_heads
    ones = lower_ones(WIDE)
    before = payload[HEADS * DV :, :].astype(F32)[0:1, 0:1]
    base = jnp.zeros((1, kd), F32)
    sums = [jnp.zeros((DV, DK), F32) for _ in range(HEADS)]
    for i in range(t // WIDE):
        rows = slice(i * WIDE, (i + 1) * WIDE)
        cumul = split_sum(ones, log_decay(pre[rows, :])) + base
        base = cumul[WIDE - 1 : WIDE, :]
        queries = qkv[rows, 0:kd].astype(F32)
        carried = jnp.where(mcol[rows, :] == before, queries * jnp.exp(cumul), 0.0).astype(BF16)
        for h in range(HEADS):
            sums[h] = sums[h] + tn(
                d_mixed_out[rows, h * DV : (h + 1) * DV], carried[:, h * DK : (h + 1) * DK]
            )
    for h in range(HEADS):
        back_out[h * DV : (h + 1) * DV, :] = sums[h].astype(BF16)


def mixer_back(who, small, d_second, hidden, cot, swish, mixed, qkv, pre, mcol, payload, own, pieces):
    t, d = hidden.shape
    vd = HEADS * DV
    quarter = own.shape[0] // 4
    right = pl.BlockSpec((quarter, d), lambda i: (0, 1))
    whole = lambda a: pl.BlockSpec(a.shape, lambda i: (0,) * len(a.shape))
    outs = (
        sds((t, d), F32),
        sds((t, d), BF16),
        sds((t, vd), BF16),
        sds((t, vd), BF16),
        sds((8, d), F32),
        sds((HEADS * DV, DK), BF16),
    )
    ins = (small, d_second, hidden, cot, swish, mixed, qkv, pre, mcol, payload, own)
    return call(
        mixer_back_kernel,
        outs,
        grid=(1,),
        in_specs=[SMEM] + [whole(a) for a in ins] + [right] * 4,
        out_specs=tuple(whole(a) for a in outs),
        scratch_shapes=[pltpu.VMEM((vd, d), BF16), pltpu.VMEM((t, vd), F32)],
    )(who, *ins, *pieces)


def gate_grads_kernel(who, normed, d_swish, gated, low, keep, send, scratch, left_t):
    j = pl.program_id(0)
    count = d_swish.shape[1]
    half = pl.num_programs(0) // 2

    @pl.when(j == 0)
    def _():
        left_t[...] = normed[...].T

    @pl.when(j == half)
    def _():
        left_t[...] = gated[...].T

    @pl.when(j < half)
    def _():
        scratch[...] = nn(left_t[...], d_swish[...]).astype(BF16)

    @pl.when(j >= half)
    def _():
        scratch[...] = nn(left_t[...], low[...]).astype(BF16)

    place_grads(who, keep, send, scratch, 0, slice(0, 256))


def gate_grads(who, normed, d_swish, gated, low):
    t, d = normed.shape
    n = d_swish.shape[1] // 256
    const = lambda j: (0, 0)
    shape = sds((2, 2, 4, 32, 2 * n * 256), BF16)
    spec = pl.BlockSpec((2, 2, 4, 32, 256), lambda j: (0, 0, 0, 0, j))
    return call(
        gate_grads_kernel,
        (shape, shape),
        grid=(2 * n,),
        in_specs=[
            SMEM,
            pl.BlockSpec((t, d), const),
            pl.BlockSpec((t, 256), lambda j: (0, jnp.minimum(j, n - 1))),
            pl.BlockSpec((t, d), const),
            pl.BlockSpec((t, 256), lambda j: (0, jnp.maximum(j - n, 0))),
        ],
        out_specs=(spec, spec),
        scratch_shapes=[pltpu.VMEM((d, 256), BF16), pltpu.VMEM((d, t), BF16)],
    )(who, normed, d_swish, gated, low)


def recurrence_back_kernel(
    small, qkv, pre, d_mixed, mcol, mrow, payload, states, entering,
    d_qkv, d_pre_out, d_narrow_out, bias_out,
):
    t = pre.shape[0]
    kd = HEADS * DK
    ones = lower_ones(WIDE)
    reverse = upper_ones(WIDE)
    causal_rows = lax.broadcasted_iota(jnp.int32, (WIDE, WIDE), 0)
    causal_cols = lax.broadcasted_iota(jnp.int32, (WIDE, WIDE), 1)
    grads = [entering[h * DV : (h + 1) * DV, :].astype(F32) for h in range(HEADS)]
    bias_sum = jnp.zeros((1, kd), F32)
    for i in reversed(range(t // WIDE)):
        rows = slice(i * WIDE, (i + 1) * WIDE)
        marks = mcol[rows, :]
        last = mark_at(mrow, (i + 1) * WIDE - 1)
        if i:
            before = mark_at(mrow, i * WIDE - 1)
        else:
            before = payload[HEADS * DV :, :].astype(F32)[0:1, 0:1]
        pre_here = pre[rows, :]
        cumul = split_sum(ones, log_decay(pre_here))
        middle = cumul[SPAN - 1 : SPAN, :]
        end = cumul[WIDE - 1 : WIDE, :]
        queries = qkv[rows, 0:kd].astype(F32)
        keys = qkv[rows, kd : 2 * kd].astype(F32)
        lift = jnp.exp(cumul - middle)
        sink = jnp.exp(middle - cumul)
        rise = jnp.where(marks == before, jnp.exp(cumul), 0.0)
        fall = jnp.where(marks == last, jnp.exp(end - cumul), 0.0)
        lifted = (queries * lift).astype(BF16)
        lowered = (keys * sink).astype(BF16)
        carried = (queries * rise).astype(BF16)
        tail = (keys * fall).astype(BF16)
        keep = jnp.where(before == last, jnp.exp(end), 0.0)
        causal = (causal_rows >= causal_cols) & (marks == mrow[0:1, rows])
        slopes = []
        ends = []
        for h in range(HEADS):
            c = slice(h * DK, (h + 1) * DK)
            values = qkv[rows, 2 * kd + h * DV : 2 * kd + (h + 1) * DV]
            up = d_mixed[rows, h * DV : (h + 1) * DV]
            state = states[i, h]
            grad = grads[h]
            low_grad = grad.astype(BF16)
            scores = jnp.where(causal, nt(lifted[:, c], lowered[:, c]), 0.0).astype(BF16)
            d_scores = jnp.where(causal, nt(up, values), 0.0).astype(BF16)
            d_lifted = nn(d_scores, lowered[:, c])
            d_lowered = tn(d_scores, lifted[:, c])
            d_carried = nn(up, state)
            d_tail = nn(values, low_grad)
            d_values = tn(scores, up) + nt(tail[:, c], low_grad)
            d_qkv[rows, c] = (d_lifted * lift[:, c] + d_carried * rise[:, c]).astype(BF16)
            d_qkv[rows, kd + h * DK : kd + (h + 1) * DK] = (
                d_lowered * sink[:, c] + d_tail * fall[:, c]
            ).astype(BF16)
            d_qkv[rows, 2 * kd + h * DV : 2 * kd + (h + 1) * DV] = d_values.astype(BF16)
            tail_term = tail[:, c].astype(F32) * d_tail
            slopes.append(
                lifted[:, c].astype(F32) * d_lifted
                - lowered[:, c].astype(F32) * d_lowered
                + carried[:, c].astype(F32) * d_carried
                - tail_term
            )
            kept = keep[:, c] * grad
            ends.append(
                jnp.sum(tail_term, axis=0, keepdims=True)
                + jnp.sum(kept * state.astype(F32), axis=0, keepdims=True)
            )
            grads[h] = kept + tn(up, carried[:, c])
        d_decay = split_sum(reverse, jnp.concatenate(slopes, axis=1)) + jnp.concatenate(ends, axis=1)
        d_pre = d_decay * sigmoid(-pre_here) / GATE_NORM
        bias_sum = bias_sum + jnp.sum(d_pre, axis=0, keepdims=True)
        d_pre_out[rows, :] = d_pre.astype(BF16)
    bias_out[...] = jnp.broadcast_to(bias_sum, bias_out.shape)
    d_narrow_out[...] = nt(d_pre_out[...], expand_of(small)).astype(BF16)


def recurrence_back(small, qkv, pre, d_mixed, mcol, mrow, payload, states, entering):
    t, width = qkv.shape
    return call(
        recurrence_back_kernel,
        (
            sds((t, width), BF16),
            sds(pre.shape, BF16),
            sds((t, 16), BF16),
            sds((8, HEADS * DK), F32),
        ),
    )(small, qkv, pre, d_mixed, mcol, mrow, payload, states, entering)


def input_back_kernel(
    who, x, small, d_hidden, d_qkv, d_swish, d_narrow, q_own, k_own, v_own, s_own,
    a0, a1, a2, a3, b0, b1, b2, b3, grad_input, mixer_out, total, full,
):
    j = pl.program_id(0)
    steps = pl.num_programs(0)

    @pl.when(j == 0)
    def _():
        total[...] = nn(d_narrow[...], small[0:ROW_EXPAND, :])

    first = [r[...] for r in (a0, a1, a2, a3)]

    @pl.when(j < 2)
    def _():
        place_rows(who, full, q_own[...], first)

    @pl.when((j >= 2) & (j < 4))
    def _():
        place_rows(who, full, k_own[...], first)

    @pl.when((j >= 4) & (j < 8))
    def _():
        place_rows(who, full, v_own[...], first)

    @pl.when(j >= 8)
    def _():
        place_rows(who, full, s_own[...], [r[...] for r in (b0, b1, b2, b3)])

    @pl.when(j < 8)
    def _():
        total[...] += nt(d_qkv[...], full[...])

    @pl.when(j >= 8)
    def _():
        total[...] += nt(d_swish[...], full[...])

    @pl.when(j == steps - 1)
    def _():
        values = x[...].astype(F32)
        upstream = total[...]
        scale = lax.rsqrt(jnp.mean(values * values, axis=-1, keepdims=True) + EPSILON)
        unit = values * scale
        mixer_out[...] = jnp.broadcast_to(
            jnp.sum(upstream * unit, axis=0, keepdims=True), mixer_out.shape
        )
        scaled = upstream * row_of(small, ROW_MIXER)
        mean = jnp.mean(scaled * unit, axis=-1, keepdims=True)
        grad_input[...] = (d_hidden[...] + scale * (scaled - unit * mean)).astype(BF16)


def input_back(who, x, small, d_hidden, d_qkv, d_swish, d_narrow, owns, pieces, gate_pieces):
    t, d = x.shape
    half = d // 2
    kd = HEADS * DK
    vd = HEADS * DV
    qn = kd // 256
    vn = vd // 256
    wn = 2 * qn + vn
    const = lambda j: (0, 0)
    col = lambda low, count: (lambda j: (0, jnp.clip(j - low, 0, count - 1)))
    return call(
        input_back_kernel,
        (sds((t, d), BF16), sds((8, d), F32)),
        grid=(wn + vn,),
        in_specs=[
            SMEM,
            pl.BlockSpec((t, d), const),
            pl.BlockSpec(small.shape, const),
            pl.BlockSpec((t, d), const),
            pl.BlockSpec((t, 256), col(0, wn)),
            pl.BlockSpec((t, 256), col(wn, vn)),
            pl.BlockSpec((t, 16), const),
            pl.BlockSpec((half, 256), col(0, qn)),
            pl.BlockSpec((half, 256), col(qn, qn)),
            pl.BlockSpec((half, 256), col(2 * qn, vn)),
            pl.BlockSpec((half, 256), col(wn, vn)),
        ]
        + [pl.BlockSpec((half // 4, 256), col(0, wn))] * 4
        + [pl.BlockSpec((half // 4, 256), col(wn, vn))] * 4,
        out_specs=(pl.BlockSpec((t, d), const), pl.BlockSpec((8, d), const)),
        scratch_shapes=[pltpu.VMEM((t, d), F32), pltpu.VMEM((d, 256), BF16)],
    )(who, x, small, d_hidden, d_qkv, d_swish, d_narrow, *owns, *pieces, *gate_pieces)


def pair_grads_kernel(who, normed, d_qkv, keep, send, scratch, left_t):
    j = pl.program_id(0)

    @pl.when(j == 0)
    def _():
        left_t[...] = normed[...].T

    scratch[...] = nn(left_t[...], d_qkv[...]).astype(BF16)
    place_grads(who, keep, send, scratch, 0, slice(0, 256))


def pair_grads(who, normed, d_qkv):
    t, d = normed.shape
    n = 2 * HEADS * DK // 256
    shape = sds((2, 2, 4, 32, n * 256), BF16)
    spec = pl.BlockSpec((2, 2, 4, 32, 256), lambda j: (0, 0, 0, 0, j))
    return call(
        pair_grads_kernel,
        (shape, shape),
        grid=(n,),
        in_specs=[
            SMEM,
            pl.BlockSpec((t, d), lambda j: (0, 0)),
            pl.BlockSpec((t, 256), lambda j: (0, j)),
        ],
        out_specs=(spec, spec),
        scratch_shapes=[pltpu.VMEM((d, 256), BF16), pltpu.VMEM((d, t), BF16)],
    )(who, normed, d_qkv)


def value_grads_kernel(
    who, normed, d_values, d_narrow, narrow, d_pre, rows_in, bias_in, mixer_in,
    keep, send, scratch, strip, left_t, rows,
):
    t, d = normed.shape
    half = d // 2
    kd = HEADS * DK
    n = d_values.shape[1] // 256
    left_t[...] = normed[...].T
    for j in range(n):
        c = slice(j * 256, (j + 1) * 256)
        scratch[...] = nn(left_t[...], d_values[:, c]).astype(BF16)
        place_grads(who, keep, send, scratch, 0, c)
    rows[...] = jnp.zeros_like(rows)
    rows[LANE_MIXER : LANE_MIXER + 1, :] = mixer_in[0:1, :]
    rows[LANE_FEED : LANE_FEED + 1, :] = rows_in[0:1, :]
    part = kd // 2
    rows[LANE_BIAS : LANE_BIAS + 1, 0:part] = bias_in[0:1, 0:part]
    rows[LANE_BIAS : LANE_BIAS + 1, half : half + part] = bias_in[0:1, part:kd]
    part = DV // 2
    rows[LANE_HEADS : LANE_HEADS + 1, 0:part] = rows_in[1:2, 0:part]
    rows[LANE_HEADS : LANE_HEADS + 1, half : half + part] = rows_in[1:2, part:DV]
    columns = rows[...].T
    squeeze = nn(left_t[...], d_narrow[...])
    expand = tn(d_pre[...], narrow[...])
    part = kd // 2
    strip[...] = columns.astype(BF16)
    strip[:, 0:16] = squeeze.astype(BF16)
    strip[0:part, LANE_EXPAND : LANE_EXPAND + 16] = expand[0:part].astype(BF16)
    strip[half : half + part, LANE_EXPAND : LANE_EXPAND + 16] = expand[part:kd].astype(BF16)
    place_grads(who, keep, send, strip, 0, slice(n * 256, n * 256 + 128))


def value_grads(who, normed, d_qkv, d_narrow, narrow, d_pre, rows_in, bias_in, mixer_in):
    t, d = normed.shape
    vd = HEADS * DV
    shape = sds((2, 2, 4, 32, vd + 128), BF16)
    whole = lambda a: pl.BlockSpec(a.shape, lambda i: (0,) * len(a.shape))
    ins = (normed, d_qkv, d_narrow, narrow, d_pre, rows_in, bias_in, mixer_in)
    specs = [whole(a) for a in ins]
    specs[1] = pl.BlockSpec((t, vd), lambda i: (0, (2 * HEADS * DK) // vd))
    return call(
        value_grads_kernel,
        (shape, shape),
        grid=(1,),
        in_specs=[SMEM] + specs,
        out_specs=(whole(shape), whole(shape)),
        scratch_shapes=[
            pltpu.VMEM((d, 256), BF16),
            pltpu.VMEM((d, 128), BF16),
            pltpu.VMEM((d, t), BF16),
            pltpu.VMEM((128, d), F32),
        ],
    )(who, *ins)


def settle(who, parts, out_refs_of):
    me = who[2]
    for k, part in enumerate(parts):
        for zz in range(4):
            out_refs_of(me ^ (k * 4 + zz), part, zz)


def feed_settle_kernel(who, a, b, c, d, *rest, first):
    gate, up, down = rest if first else rest[3:]
    h = pl.program_id(1)
    me = who[2]
    for k, part in enumerate((a, b, c, d)):
        for zz in range(4):
            block = me ^ (k * 4 + zz)
            rows = pl.ds(pl.multiple_of(block * 32, 32), 32)
            gate[rows, :] = part[zz, 0:32, :].astype(F32)
            up[rows, :] = part[zz, 32:64, :].astype(F32)
            at = pl.ds(pl.multiple_of((block % 4) * 32, 32), 32)
            cols = pl.ds(pl.multiple_of((block // 4) * 256 + h * 128, 128), 128)
            down[at, cols] = part[zz, 64:96, :].astype(F32)


def feed_settle(who, parts, before, start, blocks, half, ff, d):
    halves = ff // 256
    first = before is None
    shapes = (sds((half, ff), F32), sds((half, ff), F32), sds((ff // 2, d), F32))
    wide = pl.BlockSpec((half, 128), lambda j, h: (0, h * halves + start + j))
    tall = pl.BlockSpec((128, d), lambda j, h: (start + j, 0))
    any_spec = pl.BlockSpec(memory_space=pl.ANY)
    return call(
        functools.partial(feed_settle_kernel, first=first),
        shapes,
        grid=(blocks, 2),
        in_specs=[SMEM]
        + [pl.BlockSpec((4, 96, 128), lambda j, h: (0, 0, 2 * j + h))] * 4
        + ([] if first else [any_spec] * 3),
        out_specs=(wide, wide, tall),
        input_output_aliases={} if first else {5: 0, 6: 1, 7: 2},
    )(who, *parts, *(() if first else before))


def pair_settle_kernel(who, a, b, c, d, left, right):
    me = who[2]
    count = left.shape[1]
    for k, part in enumerate((a, b, c, d)):
        for zz in range(4):
            rows = pl.ds(pl.multiple_of((me ^ (k * 4 + zz)) * 32, 32), 32)
            left[rows, :] = part[zz, :, 0:count].astype(F32)
            right[rows, :] = part[zz, :, count:].astype(F32)


def pair_settle(who, parts, half):
    count = parts[0].shape[2] // 2
    shape = sds((half, count), F32)
    return call(pair_settle_kernel, (shape, shape), in_specs=[SMEM] + [VMEM] * 4)(who, *parts)


def added(*terms):
    total = terms[0].astype(F32)
    for term in terms[1:]:
        total = total + term.astype(F32)
    return total.astype(BF16)


def swap(v, bit):
    count = lax.axis_size("replica")
    return lax.ppermute(v, "replica", [(i, i ^ bit) for i in range(count)])


def cross(v):
    return lax.ppermute(v, "fsdp", [(0, 1), (1, 0)])


def spread(piece):
    first = cross(piece)
    second = swap(first, 2)
    return (first, swap(first, 1), second, swap(second, 1))


def reduced(keep, send):
    got = swap(send, 1)
    over = cross(added(keep[1], got[1]))
    side = swap(added(keep[0, 1], got[0, 1], over[1]), 2)
    parts = [added(keep[0, 0, j], got[0, 0, j], over[0, j], side[j]) for j in range(4)]
    deep = [swap(parts[j], 4 * j) for j in range(1, 4)]
    own = added(parts[0], *deep)
    line = jnp.stack([own] + [swap(own, 4 * j) for j in range(1, 4)])
    beside = swap(line, 2)
    return (line, beside, swap(line, 1), swap(beside, 1))


def natural(keep, send):
    both = jnp.stack([keep, send])
    both = jnp.moveaxis(both, 0, 1)
    return both.reshape((2, 16) + keep.shape[3:])


def total_over(v, dim):
    v = lax.psum_scatter(v.astype(BF16), "fsdp", scatter_dimension=dim, tiled=True)
    return lax.psum(v, "replica").astype(F32)


def chain_join(earlier, later):
    factor_early, state_early, first_early, last_early = earlier
    factor_late, state_late, first_late, last_late = later
    joined = (first_late == last_early) | (last_early < 0) | (first_late < 0)
    linked = jnp.where(joined, factor_late, 0.0)
    return (
        linked * factor_early,
        linked[:, None] * state_early + state_late,
        jnp.where(first_early < 0, first_late, first_early),
        jnp.where(last_late < 0, last_early, last_late),
    )


def chained(payload, passing, first_mark):
    place = lax.axis_index("fsdp")
    own = (
        passing[0].reshape(HEADS, DK).astype(BF16),
        payload,
        first_mark.astype(BF16),
    )
    factors, payloads, firsts = [lax.all_gather(a, "fsdp") for a in own]
    rows = HEADS * DV

    def one(turn, carry):
        pick = lambda a: lax.dynamic_index_in_dim(a, turn, 0, False).astype(F32)
        factor, block, first = pick(factors), pick(payloads), pick(firsts)
        later = (factor, block[:rows].reshape(HEADS, DV, DK), first, block[rows, :1])
        earlier_factor, state, earlier_first, earlier_last = carry
        joined = (later[2] == earlier_last) | (earlier_last < 0)
        linked = jnp.where(joined, later[0], 0.0)
        return (
            linked * earlier_factor,
            linked[:, None, :] * state + later[1],
            jnp.where(earlier_first < 0, later[2], earlier_first),
            later[3],
        )

    none = -jnp.ones((1,), F32)
    start = (jnp.ones((HEADS, DK), F32), jnp.zeros((HEADS, DV, DK), F32), none, none)
    done = lax.fori_loop(0, place, one, start)
    marks = jnp.broadcast_to(done[3][:, None], (16, DK))
    return jnp.concatenate([done[1].reshape(rows, DK), marks]).astype(BF16)


def chained_back(back, passing, linked):
    count = lax.axis_size("fsdp")
    ahead = count - 1 - lax.axis_index("fsdp")
    factor = jnp.where(linked, passing[0], 0.0).reshape(HEADS, DK).astype(BF16)
    factors, backs = [lax.all_gather(a, "fsdp") for a in (factor, back)]

    def one(turn, grad):
        source = count - 1 - turn
        pick = lambda a: lax.dynamic_index_in_dim(a, source, 0, False).astype(F32)
        return pick(backs).reshape(HEADS, DV, DK) + pick(factors)[:, None, :] * grad

    grad = lax.fori_loop(0, ahead, one, jnp.zeros((HEADS, DV, DK), F32))
    return grad.reshape(HEADS * DV, DK).astype(BF16)


def on_device(
    inputs, segments, cotangent, mixer_gain, query_map, key_map, value_map, swish_map, squeeze,
    expand, forget_bias, head_gain, readout, feed_gain, gate_map, up_map, down_map,
):
    shards = lax.axis_size("fsdp")
    copies = lax.axis_size("replica")
    paired = shards == 2 and copies == 16
    t, d = inputs.shape
    kd, vd = HEADS * DK, HEADS * DV
    half = d // 2
    quarter = half // 4
    marks = segments[0].astype(F32)
    mcol, mrow = marks[:, None], marks[None, :]

    if paired:
        place = lax.axis_index("replica")
        core, side, deep = place % 2, (place // 2) % 2, place // 4
        x = lax.axis_index("fsdp")
        q = side * 2 + core
        who = jnp.stack([x, q, core * 8 + side * 4 + deep]).astype(jnp.int32)
    else:
        who = jnp.zeros((3,), jnp.int32)
        x = q = 0
        gather = lambda a, dim=0: lax.all_gather(a, "fsdp", axis=dim, tiled=True)
        query_map, key_map, value_map, swish_map, readout, gate_map, up_map, down_map = [
            gather(a)
            for a in (query_map, key_map, value_map, swish_map, readout, gate_map, up_map, down_map)
        ]
        mixer_gain, feed_gain, forget_bias, head_gain, squeeze = [
            gather(a) for a in (mixer_gain, feed_gain, forget_bias, head_gain, squeeze)
        ]
        expand = gather(expand, 1)

    def small_half(k):
        cut = lambda a, dim=0: lax.slice_in_dim(a, k * (a.shape[dim] // 2), (k + 1) * (a.shape[dim] // 2), axis=dim)
        return packed(cut(squeeze), cut(expand, 1), cut(mixer_gain), cut(feed_gain), cut(forget_bias), cut(head_gain))

    def packed(squeeze, expand, mixer_gain, feed_gain, forget_bias, head_gain):
        wide = lambda a: jnp.pad(a, ((0, 0), (0, half - a.shape[1])))
        mixed = jnp.concatenate([forget_bias, head_gain])[None]
        rows = [squeeze.T, wide(expand), mixer_gain[None], feed_gain[None], wide(mixed)]
        block = jnp.concatenate(rows)
        return jnp.pad(block, ((0, SMALL_ROWS - block.shape[0]), (0, 0)))

    ff = gate_map.shape[1]
    halves = ff // 256
    counts = chunk_blocks(halves)
    starts = [sum(counts[:i]) for i in range(len(counts))]

    def quarter_rows(a, k):
        return lax.dynamic_slice_in_dim(a, k * quarter, quarter, 0)

    if paired:
        small_own = packed(squeeze, expand, mixer_gain, feed_gain, forget_bias, head_gain)
        small_other = cross(small_own)
        small = jnp.concatenate(
            [jnp.where(x == 0, small_own, small_other), jnp.where(x == 0, small_other, small_own)],
            axis=1,
        )
        share = lambda maps: spread(jnp.concatenate([quarter_rows(a, q) for a in maps], axis=1))
        qkv_pieces = share((query_map, key_map, value_map))
        gate_pieces = share((swish_map, readout))
        feed_pieces = [
            spread(pack_feed(who, gate_map, up_map, down_map, s, n))
            for s, n in zip(starts, counts)
        ]
    else:
        small = jnp.concatenate([small_half(0), small_half(1)], axis=1)
        lower = lambda a: a[: a.shape[0] // 2]
        upper = lambda a: a[a.shape[0] // 2 :]
        share = lambda maps: tuple(
            jnp.concatenate([quarter_rows(upper(a), k) for a in maps], axis=1) for k in range(4)
        )
        qkv_pieces = share((query_map, key_map, value_map))
        gate_pieces = share((swish_map, readout))
        others = (upper(gate_map), upper(up_map), upper(down_map))
        feed_pieces = [
            tuple(
                pack_feed(jnp.full((3,), k, jnp.int32), *others, s, n) for k in range(4)
            )
            for s, n in zip(starts, counts)
        ]
        query_map, key_map, value_map, swish_map, readout, gate_map, up_map, down_map = [
            lower(a)
            for a in (query_map, key_map, value_map, swish_map, readout, gate_map, up_map, down_map)
        ]

    normed, qkv, pre, narrow = project(
        who, inputs, small, query_map, key_map, value_map, qkv_pieces
    )
    local, passing = local_state(qkv, pre, mcol, mrow)
    if paired:
        payload = lax.ppermute(local, "fsdp", [(0, 1)])
    else:
        payload = chained(local, passing, marks[:1])
    swish = swish_project(who, normed, swish_map, gate_pieces)
    mixed, states, gated, hidden, second = mixer(
        who, inputs, small, qkv, pre, swish, mcol, mrow, payload, readout, gate_pieces
    )

    totals = None
    feed_grads = []
    for s, n, pieces in zip(starts, counts, feed_pieces):
        *totals, keep, send = feed(
            who, second, cotangent, gate_map, up_map, down_map, pieces, totals, s, n
        )
        feed_grads.append((keep, send))
    output = (hidden + totals[0]).astype(BF16)

    d_hidden, low, d_swish, d_mixed, rows, back = mixer_back(
        who, small, totals[1], hidden, cotangent, swish, mixed, qkv, pre, mcol, payload,
        readout, gate_pieces,
    )
    if paired:
        entering = lax.ppermute(back, "fsdp", [(1, 0)])
    else:
        linked = marks[0] == payload[HEADS * DV, 0].astype(F32)
        entering = chained_back(back, passing, linked)
    gate_grad = gate_grads(who, normed, d_swish, gated, low)
    d_qkv, d_pre, d_narrow, bias_row = recurrence_back(
        small, qkv, pre, d_mixed, mcol, mrow, payload, states, entering
    )
    pair_grad = pair_grads(who, normed, d_qkv)
    grad_input, mixer_row = input_back(
        who, inputs, small, d_hidden, d_qkv, d_swish, d_narrow,
        (query_map, key_map, value_map, swish_map), qkv_pieces, gate_pieces,
    )
    value_grad = value_grads(
        who, normed, d_qkv, d_narrow, narrow, d_pre, rows, bias_row, mixer_row
    )

    if paired:
        feeds = None
        for (keep, send), s, n in zip(feed_grads, starts, counts):
            feeds = feed_settle(who, reduced(keep, send), feeds, s, n, half, ff, d)
        grad_gate, grad_up, grad_down = feeds
        grad_swish, grad_readout = pair_settle(who, reduced(*gate_grad), half)
        grad_query, grad_key = pair_settle(who, reduced(*pair_grad), half)
        parts = reduced(*value_grad)
        grad_value, strip = value_settle(who, parts, half)
        return (
            output, grad_input, strip[:, LANE_MIXER], grad_query, grad_key, grad_value, grad_swish,
            strip[:, :16], strip[: kd // 2, LANE_EXPAND : LANE_EXPAND + 16].T,
            strip[: kd // 2, LANE_BIAS], strip[: DV // 2, LANE_HEADS], grad_readout,
            strip[:, LANE_FEED], grad_gate, grad_up, grad_down,
        )

    gates, ups, downs = [], [], []
    for (keep, send), n in zip(feed_grads, counts):
        block = natural(keep, send)
        sides = lambda k: block[:, :, 32 * k : 32 * (k + 1), :].reshape(d, n, 2, 128)
        gates.append(sides(0))
        ups.append(sides(1))
        part = block[:, :, 64:96, :].reshape(2, 4, 128, n, 256)
        downs.append(part.transpose(0, 3, 2, 1, 4).reshape(2, n * 128, d))
    whole = lambda parts: jnp.concatenate(parts, axis=1).transpose(0, 2, 1, 3).reshape(d, ff)
    grad_gate, grad_up = whole(gates), whole(ups)
    grad_down = jnp.concatenate(downs, axis=1).reshape(ff, d)
    flat = lambda pair: natural(*pair).reshape(d, -1)
    gate_flat, pair_flat, value_flat = flat(gate_grad), flat(pair_grad), flat(value_grad)
    strip = value_flat[:, vd:]
    joined = lambda lane, count: jnp.concatenate(
        [strip[:count, lane], strip[half : half + count, lane]]
    )
    part = kd // 2
    grad_expand = jnp.concatenate([strip[:part, 16:32], strip[half : half + part, 16:32]]).T
    results = (
        joined(LANE_MIXER, half), pair_flat[:, :kd], pair_flat[:, kd:], value_flat[:, :vd],
        gate_flat[:, :vd], strip[:, :16], grad_expand, joined(LANE_BIAS, part),
        joined(LANE_HEADS, DV // 2), gate_flat[:, vd:], joined(LANE_FEED, half),
        grad_gate, grad_up, grad_down,
    )
    return (output, grad_input) + tuple(
        total_over(a, 1 if i == 6 else 0) for i, a in enumerate(results)
    )


def value_settle_kernel(who, a, b, c, d, left, right):
    me = who[2]
    count = left.shape[1]
    for k, part in enumerate((a, b, c, d)):
        for zz in range(4):
            rows = pl.ds(pl.multiple_of((me ^ (k * 4 + zz)) * 32, 32), 32)
            left[rows, :] = part[zz, :, 0:count].astype(F32)
            right[rows, :] = part[zz, :, count:].astype(F32)


def value_settle(who, parts, half):
    vd = HEADS * DV
    shapes = (sds((half, vd), F32), sds((half, 128), F32))
    return call(value_settle_kernel, shapes, in_specs=[SMEM] + [VMEM] * 4)(who, *parts)


def chunk_blocks(halves):
    parts = 3
    base, extra = divmod(halves, parts)
    return [base + (1 if i >= parts - extra else 0) for i in range(parts)]


def solution(mesh):
    placed = (
        P(("replica", "fsdp"), None),
        P("replica", "fsdp"),
        P(("replica", "fsdp"), None),
        P("fsdp"),
        P("fsdp", None),
        P("fsdp", None),
        P("fsdp", None),
        P("fsdp", None),
        P("fsdp", None),
        P(None, "fsdp"),
        P("fsdp"),
        P("fsdp"),
        P("fsdp", None),
        P("fsdp"),
        P("fsdp", None),
        P("fsdp", None),
        P("fsdp", None),
    )
    return jax.shard_map(
        on_device,
        mesh=mesh,
        in_specs=placed,
        out_specs=(
            P(("replica", "fsdp"), None),
            P(("replica", "fsdp"), None),
            P("fsdp"),
            P("fsdp", None),
            P("fsdp", None),
            P("fsdp", None),
            P("fsdp", None),
            P("fsdp", None),
            P(None, "fsdp"),
            P("fsdp"),
            P("fsdp"),
            P("fsdp", None),
            P("fsdp"),
            P("fsdp", None),
            P("fsdp", None),
            P("fsdp", None),
        ),
        check_vma=False,
    )
```

```python
import functools

import jax
import jax.numpy as jnp
from jax import lax
from jax.experimental import pallas as pl
from jax.experimental.pallas import tpu as pltpu
from jax.sharding import PartitionSpec as P

HEADS = 4
DK = 128
DV = 256
SPAN = 64
WIDE = 2 * SPAN

EPSILON = 1e-06
HEAD_FLOOR = 16.0
GATE_NORM = 16.0

F32 = jnp.float32
BF16 = jnp.bfloat16
VMEM_BYTES = 56 * 1024 * 1024

ROW_EXPAND = 16
ROW_MIXER = 32
ROW_FEED = 33
ROW_MIXED = 34
SMALL_ROWS = 48
LANE_EXPAND = 16
LANE_FEED = 32
LANE_BIAS = 33
LANE_HEADS = 34


def nn(a, b):
    return lax.dot_general(a, b, (((1,), (0,)), ((), ())), preferred_element_type=F32)


def nt(a, b):
    return lax.dot_general(a, b, (((1,), (1,)), ((), ())), preferred_element_type=F32)


def tn(a, b):
    return lax.dot_general(a, b, (((0,), (0,)), ((), ())), preferred_element_type=F32)


def sigmoid(v):
    return 1.0 / (1.0 + jnp.exp(-v))


def cost(us):
    return pl.CostEstimate(
        flops=int(us * 1e7), bytes_accessed=int(us * 3.6e4), transcendentals=0
    )


def call(kernel, out_shape, us=5, **kw):
    return pl.pallas_call(
        kernel,
        out_shape=out_shape,
        cost_estimate=cost(us),
        compiler_params=pltpu.CompilerParams(vmem_limit_bytes=VMEM_BYTES),
        **kw,
    )


def sds(shape, dtype):
    return jax.ShapeDtypeStruct(shape, dtype)


SMEM = pl.BlockSpec(memory_space=pltpu.SMEM)
VMEM = pl.BlockSpec(memory_space=pltpu.VMEM)


def split_sum(ones, values):
    high = values.astype(BF16)
    rest = values - high.astype(F32)
    middle = rest.astype(BF16)
    low = (rest - middle.astype(F32)).astype(BF16)
    return nn(ones, high) + nn(ones, middle) + nn(ones, low)


def lower_ones(size):
    rows = lax.broadcasted_iota(jnp.int32, (size, size), 0)
    cols = lax.broadcasted_iota(jnp.int32, (size, size), 1)
    return (rows >= cols).astype(F32).astype(BF16)


def upper_ones(size):
    rows = lax.broadcasted_iota(jnp.int32, (size, size), 0)
    cols = lax.broadcasted_iota(jnp.int32, (size, size), 1)
    return (rows <= cols).astype(F32).astype(BF16)


def log_decay(pre):
    return (jnp.minimum(pre, 0.0) - jnp.log1p(jnp.exp(-jnp.abs(pre)))) / GATE_NORM


def row_of(small_ref, row):
    return small_ref[ROW_MIXER:SMALL_ROWS, :].astype(F32)[row - ROW_MIXER : row - ROW_MIXER + 1, :]


def expand_of(small_ref):
    half = small_ref.shape[1] // 2
    quarter = half // 2
    part = small_ref[ROW_EXPAND:ROW_MIXER, :]
    return jnp.concatenate([part[:, :quarter], part[:, half : half + quarter]], axis=1)


def bias_of(small_ref):
    half = small_ref.shape[1] // 2
    quarter = half // 2
    row = row_of(small_ref, ROW_MIXED)
    return jnp.concatenate([row[:, :quarter], row[:, half : half + quarter]], axis=1)


def head_gain_of(small_ref):
    half = small_ref.shape[1] // 2
    at = half // 2
    count = DV // 2
    row = row_of(small_ref, ROW_MIXED)
    return jnp.concatenate([row[:, at : at + count], row[:, half + at : half + at + count]], axis=1)


def place_rows(who_ref, full_ref, own, pieces):
    x = who_ref[0]
    q = who_ref[1]
    half = own.shape[0]
    rows = pieces[0].shape[0]
    full_ref[pl.ds(pl.multiple_of(x * half, half), half), :] = own
    for k in range(4):
        at = (1 - x) * half + (q ^ k) * rows
        full_ref[pl.ds(pl.multiple_of(at, rows), rows), :] = pieces[k]


def place_grads(who_ref, keep_ref, send_ref, scratch_ref, row, cols, rows=32):
    x = who_ref[0]
    me = who_ref[2]
    half = scratch_ref.shape[0] // 2
    for core, out_ref in ((0, keep_ref), (1, send_ref)):
        for xx in range(2):
            for yy in range(2):
                for zz in range(4):
                    block = me ^ (core * 8 + yy * 4 + zz)
                    at = pl.multiple_of((x ^ xx) * half + block * rows, rows)
                    out_ref[xx, yy, zz, row : row + rows, cols] = scratch_ref[pl.ds(at, rows), :]


def project_kernel(
    who, x, small, k_own, v_own, r0, r1, r2, r3, normed, kv, pre, narrow_out, full
):
    j = pl.program_id(0)

    @pl.when(j == 0)
    def _():
        tokens = x[...].astype(F32)
        mean_sq = jnp.mean(tokens * tokens, axis=-1, keepdims=True)
        normed[...] = (
            tokens * lax.rsqrt(mean_sq + EPSILON) * row_of(small, ROW_MIXER)
        ).astype(BF16)
        narrow = nt(normed[...], small[0:ROW_EXPAND, :]).astype(BF16)
        narrow_out[...] = narrow
        pre[...] = nn(narrow, expand_of(small)) + bias_of(small)

    pieces = [r[...] for r in (r0, r1, r2, r3)]

    @pl.when(j < 2)
    def _():
        place_rows(who, full, k_own[...], pieces)

    @pl.when(j >= 2)
    def _():
        place_rows(who, full, v_own[...], pieces)

    kv[...] = nn(normed[...], full[...]).astype(BF16)


def project(who, x, small, k_own, v_own, pieces):
    t, d = x.shape
    half = d // 2
    kd = HEADS * DK
    vd = HEADS * DV
    width = kd + vd
    const = lambda j: (0, 0)
    qn = kd // 256
    vn = vd // 256
    return call(
        project_kernel,
        (sds((t, d), BF16), sds((t, width), BF16), sds((t, kd), F32), sds((t, 16), BF16)),
        grid=(width // 256,),
        in_specs=[
            SMEM,
            pl.BlockSpec((t, d), const),
            pl.BlockSpec(small.shape, const),
            pl.BlockSpec((half, 256), lambda j: (0, jnp.minimum(j, qn - 1))),
            pl.BlockSpec((half, 256), lambda j: (0, jnp.clip(j - qn, 0, vn - 1))),
        ]
        + [pl.BlockSpec((half // 4, 256), lambda j: (0, j))] * 4,
        out_specs=(
            pl.BlockSpec((t, d), const),
            pl.BlockSpec((t, 256), lambda j: (0, j)),
            pl.BlockSpec((t, kd), const),
            pl.BlockSpec((t, 16), const),
        ),
        scratch_shapes=[pltpu.VMEM((d, 256), BF16)],
    )(who, x, small, k_own, v_own, *pieces)


def swish_kernel(who, normed, q_own, s_own, r0, r1, r2, r3, queries, swish, full):
    j = pl.program_id(0)
    pieces = [r[...] for r in (r0, r1, r2, r3)]

    @pl.when(j < 2)
    def _():
        place_rows(who, full, q_own[...], pieces)
        queries[...] = nn(normed[...], full[...]).astype(BF16)

    @pl.when(j >= 2)
    def _():
        place_rows(who, full, s_own[...], pieces)
        swish[...] = nn(normed[...], full[...])


def swish_project(who, normed, q_own, s_own, pieces):
    t, d = normed.shape
    half = d // 2
    kd = HEADS * DK
    vd = HEADS * DV
    qn = kd // 256
    vn = vd // 256
    low = lambda j: (0, jnp.minimum(j, qn - 1))
    high = lambda j: (0, jnp.clip(j - qn, 0, vn - 1))
    return call(
        swish_kernel,
        (sds((t, kd), BF16), sds((t, vd), F32)),
        grid=(qn + vn,),
        in_specs=[
            SMEM,
            pl.BlockSpec((t, d), lambda j: (0, 0)),
            pl.BlockSpec((half, 256), low),
            pl.BlockSpec((half, 256), high),
        ]
        + [pl.BlockSpec((half // 4, 256), lambda j: (0, j))] * 4,
        out_specs=(pl.BlockSpec((t, 256), low), pl.BlockSpec((t, 256), high)),
        scratch_shapes=[pltpu.VMEM((d, 256), BF16)],
    )(who, normed, q_own, s_own, *pieces)


def mark_at(mrow, place):
    return mrow[0:1, place : place + 1]


def state_kernel(kv, pre, mcol, mrow, payload, passing):
    t = pre.shape[0]
    kd = HEADS * DK
    ones = lower_ones(WIDE)
    states = [jnp.zeros((DV, DK), F32) for _ in range(HEADS)]
    total = jnp.zeros((1, kd), F32)
    for i in range(t // WIDE):
        rows = slice(i * WIDE, (i + 1) * WIDE)
        cumul = split_sum(ones, log_decay(pre[rows, :]))
        end = cumul[WIDE - 1 : WIDE, :]
        total = total + end
        last = mark_at(mrow, (i + 1) * WIDE - 1)
        keys = kv[rows, 0:kd].astype(F32)
        tail = jnp.where(mcol[rows, :] == last, keys * jnp.exp(end - cumul), 0.0).astype(BF16)
        if i:
            keep = jnp.where(mark_at(mrow, i * WIDE - 1) == last, jnp.exp(end), 0.0)
        for h in range(HEADS):
            c = slice(h * DK, (h + 1) * DK)
            values = kv[rows, kd + h * DV : kd + (h + 1) * DV]
            update = tn(values, tail[:, c])
            states[h] = states[h] * keep[:, c] + update if i else update
    for h in range(HEADS):
        payload[h * DV : (h + 1) * DV, :] = states[h].astype(BF16)
    last = mark_at(mrow, t - 1)
    payload[HEADS * DV :, :] = jnp.broadcast_to(last, (16, DK)).astype(BF16)
    passes = jnp.where(mark_at(mrow, 0) == last, jnp.exp(total), 0.0)
    passing[...] = jnp.broadcast_to(passes, passing.shape)


def local_state(kv, pre, mcol, mrow):
    return call(
        state_kernel,
        (sds((HEADS * DV + 16, DK), BF16), sds((8, HEADS * DK), F32)), us=5)(kv, pre, mcol, mrow)


def mixer_kernel(
    who, x, small, q, kv, pre, swish, mcol, mrow, payload, own, r0, r1, r2, r3,
    mixed_out, states_out, gated_out, hidden_out, second_out, full,
):
    t, d = x.shape
    kd = HEADS * DK
    ones = lower_ones(WIDE)
    causal_rows = lax.broadcasted_iota(jnp.int32, (WIDE, WIDE), 0)
    causal_cols = lax.broadcasted_iota(jnp.int32, (WIDE, WIDE), 1)
    states = [payload[h * DV : (h + 1) * DV, :].astype(F32) for h in range(HEADS)]
    before = payload[HEADS * DV :, :].astype(F32)[0:1, 0:1]
    place_rows(who, full, own[...], [r[...] for r in (r0, r1, r2, r3)])
    for i in range(t // WIDE):
        rows = slice(i * WIDE, (i + 1) * WIDE)
        marks = mcol[rows, :]
        last = mark_at(mrow, (i + 1) * WIDE - 1)
        cumul = split_sum(ones, log_decay(pre[rows, :]))
        middle = cumul[SPAN - 1 : SPAN, :]
        end = cumul[WIDE - 1 : WIDE, :]
        queries = q[rows, :].astype(F32)
        keys = kv[rows, 0:kd].astype(F32)
        lifted = (queries * jnp.exp(cumul - middle)).astype(BF16)
        lowered = (keys * jnp.exp(middle - cumul)).astype(BF16)
        carried = jnp.where(marks == before, queries * jnp.exp(cumul), 0.0).astype(BF16)
        tail = jnp.where(marks == last, keys * jnp.exp(end - cumul), 0.0).astype(BF16)
        keep = jnp.where(before == last, jnp.exp(end), 0.0)
        causal = (causal_rows >= causal_cols) & (marks == mrow[0:1, rows])
        for h in range(HEADS):
            c = slice(h * DK, (h + 1) * DK)
            values = kv[rows, kd + h * DV : kd + (h + 1) * DV]
            low_state = states[h].astype(BF16)
            states_out[i, h] = low_state
            scores = jnp.where(causal, nt(lifted[:, c], lowered[:, c]), 0.0).astype(BF16)
            mixed_out[rows, h * DV : (h + 1) * DV] = nn(scores, values) + nt(
                carried[:, c], low_state
            )
            states[h] = states[h] * keep[:, c] + tn(values, tail[:, c])
        before = last
    gain = head_gain_of(small)
    for h in range(HEADS):
        c = slice(h * DV, (h + 1) * DV)
        mixed = mixed_out[:, c]
        scale = lax.rsqrt(jnp.mean(mixed * mixed, axis=-1, keepdims=True) + HEAD_FLOOR)
        pre_gate = swish[:, c]
        gated_out[:, c] = (mixed * scale * gain * (pre_gate * sigmoid(pre_gate))).astype(BF16)
    hidden = x[...].astype(F32) + nn(gated_out[...], full[...])
    hidden_out[...] = hidden
    mean_sq = jnp.mean(hidden * hidden, axis=-1, keepdims=True)
    second_out[...] = (
        hidden * lax.rsqrt(mean_sq + EPSILON) * row_of(small, ROW_FEED)
    ).astype(BF16)


def mixer(who, x, small, q, kv, pre, swish, mcol, mrow, payload, own, pieces):
    t, d = x.shape
    vd = HEADS * DV
    quarter = own.shape[0] // 4
    right = pl.BlockSpec((quarter, d), lambda i: (0, 0))
    whole = lambda a: pl.BlockSpec(a.shape, lambda i: (0,) * a.ndim)
    outs = (
        sds((t, vd), F32),
        sds((t // WIDE, HEADS, DV, DK), BF16),
        sds((t, vd), BF16),
        sds((t, d), F32),
        sds((t, d), BF16),
    )
    ins = (x, small, q, kv, pre, swish, mcol, mrow, payload, own)
    return call(
        mixer_kernel,
        outs,
        grid=(1,),
        in_specs=[SMEM] + [whole(a) for a in ins] + [right] * 4,
        out_specs=tuple(whole(a) for a in outs),
        scratch_shapes=[pltpu.VMEM((vd, d), BF16)], us=11)(who, *ins, *pieces)


def feed_kernel(
    who, second, cot, g0, g1, u0, u1, down, r0, r1, r2, r3, *rest, first, blocks
):
    if first:
        total_out, total_ds, keep, send, wg, wu, wd, sec_t, cot_t, sg_, su_, sd_ = rest
    else:
        in_out, in_ds, total_out, total_ds, keep, send, wg, wu, wd, sec_t, cot_t, sg_, su_, sd_ = rest
    j = pl.program_id(0)

    @pl.when(j == 0)
    def _():
        if first:
            total_out[...] = jnp.zeros_like(total_out)
            total_ds[...] = jnp.zeros_like(total_ds)
        else:
            total_out[...] = in_out[...]
            total_ds[...] = in_ds[...]
        sec_t[...] = second[...].T
        cot_t[...] = cot[...].T

    x = who[0]
    q = who[1]
    half = g0.shape[0]
    rows = pl.ds(pl.multiple_of(x * half, half), half)
    wg[rows, 0:128] = g0[...]
    wg[rows, 128:256] = g1[...]
    wu[rows, 0:128] = u0[...]
    wu[rows, 128:256] = u1[...]
    wd[pl.ds(pl.multiple_of(x * 128, 128), 128), :] = down[...]
    for k, r in enumerate((r0, r1, r2, r3)):
        at = q ^ k
        rows = pl.ds(pl.multiple_of((1 - x) * half + at * 128, 128), 128)
        wg[rows, :] = r[:, 0:256]
        wu[rows, :] = r[:, 256:512]
        wd[pl.ds(pl.multiple_of((1 - x) * 128, 128), 128), pl.ds(pl.multiple_of(at * 256, 256), 256)] = r[:, 512:768]
    gate = nn(second[...], wg[...])
    upward = nn(second[...], wu[...])
    d_inner = nt(cot[...], wd[...])
    sig = sigmoid(gate)
    silu = gate * sig
    inner = (silu * upward).astype(BF16)
    d_gate = (d_inner * upward * sig * (1.0 + gate * (1.0 - sig))).astype(BF16)
    d_up = (d_inner * silu).astype(BF16)
    total_out[...] += nn(inner, wd[...])
    total_ds[...] += nt(d_gate, wg[...]) + nt(d_up, wu[...])
    sg_[...] = nn(sec_t[...], d_gate).astype(BF16)
    su_[...] = nn(sec_t[...], d_up).astype(BF16)
    grad_down = tn(inner, cot[...]).astype(BF16)
    for part in range(2):
        for cb in range(4):
            at = part * half + cb * 128
            sd_[at : at + 128, :] = grad_down[part * 128 : (part + 1) * 128, cb * 256 : (cb + 1) * 256]
    cols = slice(0, 256)
    place_grads(who, keep, send, sg_, 0, cols)
    place_grads(who, keep, send, su_, 32, cols)
    place_grads(who, keep, send, sd_, 64, cols)


def feed(who, second, cot, gate_own, up_own, down_own, pieces, totals, start, blocks):
    t, d = second.shape
    half = d // 2
    ff = gate_own.shape[1]
    halves = ff // 256
    const = lambda j: (0, 0)
    first = totals is None
    left = pl.BlockSpec((half, 128), lambda j: (0, start + j))
    right = pl.BlockSpec((half, 128), lambda j: (0, halves + start + j))
    full = pl.BlockSpec((t, d), const)
    grads = pl.BlockSpec((2, 2, 4, 96, 256), lambda j: (0, 0, 0, 0, j))
    grads_shape = sds((2, 2, 4, 96, blocks * 256), BF16)
    return call(
        functools.partial(feed_kernel, first=first, blocks=blocks),
        (sds((t, d), F32), sds((t, d), F32), grads_shape, grads_shape),
        us=1 + 4.5 * blocks,
        grid=(blocks,),
        in_specs=[
            SMEM, full, full, left, right, left, right,
            pl.BlockSpec((128, d), lambda j: (start + j, 0)),
        ]
        + [pl.BlockSpec((half // 4, 768), lambda j: (0, j))] * 4
        + ([] if first else [full, full]),
        out_specs=(full, full, grads, grads),
        scratch_shapes=[
            pltpu.VMEM((d, 256), BF16),
            pltpu.VMEM((d, 256), BF16),
            pltpu.VMEM((256, d), BF16),
            pltpu.VMEM((d, t), BF16),
            pltpu.VMEM((d, t), BF16),
            pltpu.VMEM((d, 256), BF16),
            pltpu.VMEM((d, 256), BF16),
            pltpu.VMEM((d, 256), BF16),
        ],
    )(
        who, second, cot, gate_own, gate_own, up_own, up_own, down_own, *pieces,
        *(() if first else totals),
    )


def pack_kernel(who, g0, g1, u0, u1, down, out):
    out[:, 0:128] = g0[...]
    out[:, 128:256] = g1[...]
    out[:, 256:384] = u0[...]
    out[:, 384:512] = u1[...]
    out[:, 512:768] = down[...]


def pack_feed(who, gate_own, up_own, down_own, start, blocks):
    half, ff = gate_own.shape
    halves = ff // 256
    quarter = half // 4
    left = pl.BlockSpec((quarter, 128), lambda j, w: (w[1], start + j))
    right = pl.BlockSpec((quarter, 128), lambda j, w: (w[1], halves + start + j))
    return pl.pallas_call(
        pack_kernel,
        out_shape=sds((quarter, blocks * 768), BF16),
        cost_estimate=cost(blocks),
        grid_spec=pltpu.PrefetchScalarGridSpec(
            num_scalar_prefetch=1,
            grid=(blocks,),
            in_specs=[
                left, right, left, right,
                pl.BlockSpec((128, down_own.shape[1] // 4), lambda j, w: (start + j, w[1])),
            ],
            out_specs=pl.BlockSpec((quarter, 768), lambda j, w: (0, j)),
        ),
    )(who, gate_own, gate_own, up_own, up_own, down_own)


def mixer_back_kernel(
    who, small, d_second, hidden, cot, swish, mixed, q, pre, mcol, payload,
    own, r0, r1, r2, r3,
    d_hidden_out, low_out, d_swish_out, d_mixed_out, rows_out, back_out, full, d_gated,
):
    t, d = hidden.shape
    kd = HEADS * DK
    place_rows(who, full, own[...], [r[...] for r in (r0, r1, r2, r3)])
    values = hidden[...]
    upstream = d_second[...]
    scale = lax.rsqrt(jnp.mean(values * values, axis=-1, keepdims=True) + EPSILON)
    rows_out[...] = jnp.zeros_like(rows_out)
    rows_out[0:1, :] = jnp.sum(upstream * values * scale, axis=0, keepdims=True)
    scaled = upstream * row_of(small, ROW_FEED)
    mean = jnp.mean(scaled * values, axis=-1, keepdims=True)
    d_hidden = cot[...].astype(F32) + scale * scaled - values * (scale * scale * scale * mean)
    d_hidden_out[...] = d_hidden
    low_out[...] = d_hidden.astype(BF16)
    d_gated[...] = nt(low_out[...], full[...])
    gain = head_gain_of(small)
    grad_heads = jnp.zeros((1, DV), F32)
    for h in range(HEADS):
        c = slice(h * DV, (h + 1) * DV)
        values = mixed[:, c]
        scale = lax.rsqrt(jnp.mean(values * values, axis=-1, keepdims=True) + HEAD_FLOOR)
        pre_gate = swish[:, c]
        sig = sigmoid(pre_gate)
        up = d_gated[:, c]
        unit = values * scale
        d_swish_out[:, c] = (up * unit * gain * sig * (1.0 + pre_gate * (1.0 - sig))).astype(BF16)
        err = up * pre_gate * sig
        grad_heads = grad_heads + jnp.sum(err * unit, axis=0, keepdims=True)
        scaled = err * gain
        mean = jnp.mean(scaled * unit, axis=-1, keepdims=True)
        d_mixed_out[:, c] = (scale * (scaled - unit * mean)).astype(BF16)
    rows_out[1:2, 0:DV] = grad_heads
    ones = lower_ones(WIDE)
    before = payload[HEADS * DV :, :].astype(F32)[0:1, 0:1]
    base = jnp.zeros((1, kd), F32)
    sums = [jnp.zeros((DV, DK), F32) for _ in range(HEADS)]
    for i in range(t // WIDE):
        rows = slice(i * WIDE, (i + 1) * WIDE)
        cumul = split_sum(ones, log_decay(pre[rows, :])) + base
        base = cumul[WIDE - 1 : WIDE, :]
        queries = q[rows, :].astype(F32)
        carried = jnp.where(mcol[rows, :] == before, queries * jnp.exp(cumul), 0.0).astype(BF16)
        for h in range(HEADS):
            sums[h] = sums[h] + tn(
                d_mixed_out[rows, h * DV : (h + 1) * DV], carried[:, h * DK : (h + 1) * DK]
            )
    for h in range(HEADS):
        back_out[h * DV : (h + 1) * DV, :] = sums[h].astype(BF16)


def mixer_back(who, small, d_second, hidden, cot, swish, mixed, q, pre, mcol, payload, own, pieces):
    t, d = hidden.shape
    vd = HEADS * DV
    quarter = own.shape[0] // 4
    right = pl.BlockSpec((quarter, d), lambda i: (0, 0))
    whole = lambda a: pl.BlockSpec(a.shape, lambda i: (0,) * len(a.shape))
    outs = (
        sds((t, d), F32),
        sds((t, d), BF16),
        sds((t, vd), BF16),
        sds((t, vd), BF16),
        sds((8, d), F32),
        sds((HEADS * DV, DK), BF16),
    )
    ins = (small, d_second, hidden, cot, swish, mixed, q, pre, mcol, payload, own)
    return call(
        mixer_back_kernel,
        outs,
        grid=(1,),
        in_specs=[SMEM] + [whole(a) for a in ins] + [right] * 4,
        out_specs=tuple(whole(a) for a in outs),
        scratch_shapes=[pltpu.VMEM((vd, d), BF16), pltpu.VMEM((t, vd), F32)], us=11)(who, *ins, *pieces)


def gate_grads_kernel(who, normed, d_swish, gated, low, keep, send, scratch, left_t):
    j = pl.program_id(0)
    count = d_swish.shape[1]
    half = pl.num_programs(0) // 2

    @pl.when(j == 0)
    def _():
        left_t[...] = normed[...].T

    @pl.when(j == half)
    def _():
        left_t[...] = gated[...].T

    @pl.when(j < half)
    def _():
        scratch[...] = nn(left_t[...], d_swish[...]).astype(BF16)

    @pl.when(j >= half)
    def _():
        scratch[...] = nn(left_t[...], low[...]).astype(BF16)

    place_grads(who, keep, send, scratch, 0, slice(0, 256))


def gate_grads(who, normed, d_swish, gated, low):
    t, d = normed.shape
    n = d_swish.shape[1] // 256
    const = lambda j: (0, 0)
    shape = sds((2, 2, 4, 32, 2 * n * 256), BF16)
    spec = pl.BlockSpec((2, 2, 4, 32, 256), lambda j: (0, 0, 0, 0, j))
    return call(
        gate_grads_kernel,
        (shape, shape),
        grid=(2 * n,),
        in_specs=[
            SMEM,
            pl.BlockSpec((t, d), const),
            pl.BlockSpec((t, 256), lambda j: (0, jnp.minimum(j, n - 1))),
            pl.BlockSpec((t, d), const),
            pl.BlockSpec((t, 256), lambda j: (0, jnp.maximum(j - n, 0))),
        ],
        out_specs=(spec, spec),
        scratch_shapes=[pltpu.VMEM((d, 256), BF16), pltpu.VMEM((d, t), BF16)], us=9)(who, normed, d_swish, gated, low)


def recurrence_back_kernel(
    small, q, kv, pre, d_mixed, mcol, mrow, payload, states, entering,
    d_qkv, d_pre_out, d_narrow_out, bias_out,
):
    t = pre.shape[0]
    kd = HEADS * DK
    ones = lower_ones(WIDE)
    reverse = upper_ones(WIDE)
    causal_rows = lax.broadcasted_iota(jnp.int32, (WIDE, WIDE), 0)
    causal_cols = lax.broadcasted_iota(jnp.int32, (WIDE, WIDE), 1)
    grads = [entering[h * DV : (h + 1) * DV, :].astype(F32) for h in range(HEADS)]
    bias_sum = jnp.zeros((1, kd), F32)
    for i in reversed(range(t // WIDE)):
        rows = slice(i * WIDE, (i + 1) * WIDE)
        marks = mcol[rows, :]
        last = mark_at(mrow, (i + 1) * WIDE - 1)
        if i:
            before = mark_at(mrow, i * WIDE - 1)
        else:
            before = payload[HEADS * DV :, :].astype(F32)[0:1, 0:1]
        pre_here = pre[rows, :]
        cumul = split_sum(ones, log_decay(pre_here))
        middle = cumul[SPAN - 1 : SPAN, :]
        end = cumul[WIDE - 1 : WIDE, :]
        queries = q[rows, :].astype(F32)
        keys = kv[rows, 0:kd].astype(F32)
        lift = jnp.exp(cumul - middle)
        sink = jnp.exp(middle - cumul)
        rise = jnp.where(marks == before, jnp.exp(cumul), 0.0)
        fall = jnp.where(marks == last, jnp.exp(end - cumul), 0.0)
        lifted = (queries * lift).astype(BF16)
        lowered = (keys * sink).astype(BF16)
        carried = (queries * rise).astype(BF16)
        tail = (keys * fall).astype(BF16)
        keep = jnp.where(before == last, jnp.exp(end), 0.0)
        causal = (causal_rows >= causal_cols) & (marks == mrow[0:1, rows])
        slopes = []
        ends = []
        for h in range(HEADS):
            c = slice(h * DK, (h + 1) * DK)
            values = kv[rows, kd + h * DV : kd + (h + 1) * DV]
            up = d_mixed[rows, h * DV : (h + 1) * DV]
            state = states[i, h]
            grad = grads[h]
            low_grad = grad.astype(BF16)
            scores = jnp.where(causal, nt(lifted[:, c], lowered[:, c]), 0.0).astype(BF16)
            d_scores = jnp.where(causal, nt(up, values), 0.0).astype(BF16)
            d_lifted = nn(d_scores, lowered[:, c])
            d_lowered = tn(d_scores, lifted[:, c])
            d_carried = nn(up, state)
            d_tail = nn(values, low_grad)
            d_values = tn(scores, up) + nt(tail[:, c], low_grad)
            d_qkv[rows, c] = (d_lifted * lift[:, c] + d_carried * rise[:, c]).astype(BF16)
            d_qkv[rows, kd + h * DK : kd + (h + 1) * DK] = (
                d_lowered * sink[:, c] + d_tail * fall[:, c]
            ).astype(BF16)
            d_qkv[rows, 2 * kd + h * DV : 2 * kd + (h + 1) * DV] = d_values.astype(BF16)
            tail_term = tail[:, c].astype(F32) * d_tail
            slopes.append(
                lifted[:, c].astype(F32) * d_lifted
                - lowered[:, c].astype(F32) * d_lowered
                + carried[:, c].astype(F32) * d_carried
                - tail_term
            )
            kept = keep[:, c] * grad
            ends.append(
                jnp.sum(tail_term, axis=0, keepdims=True)
                + jnp.sum(kept * state.astype(F32), axis=0, keepdims=True)
            )
            grads[h] = kept + tn(up, carried[:, c])
        d_decay = split_sum(reverse, jnp.concatenate(slopes, axis=1)) + jnp.concatenate(ends, axis=1)
        d_pre = d_decay * sigmoid(-pre_here) / GATE_NORM
        bias_sum = bias_sum + jnp.sum(d_pre, axis=0, keepdims=True)
        d_pre_out[rows, :] = d_pre.astype(BF16)
    bias_out[...] = jnp.broadcast_to(bias_sum, bias_out.shape)
    d_narrow_out[...] = nt(d_pre_out[...], expand_of(small)).astype(BF16)


def recurrence_back(small, q, kv, pre, d_mixed, mcol, mrow, payload, states, entering):
    t = q.shape[0]
    width = q.shape[1] + kv.shape[1]
    return call(
        recurrence_back_kernel,
        (
            sds((t, width), BF16),
            sds(pre.shape, BF16),
            sds((t, 16), BF16),
            sds((8, HEADS * DK), F32),
        ), us=11)(small, q, kv, pre, d_mixed, mcol, mrow, payload, states, entering)


def input_back_kernel(
    who, x, small, d_hidden, d_qkv, d_swish, d_narrow, q_own, k_own, v_own, s_own,
    a0, a1, a2, a3, b0, b1, b2, b3, grad_input, mixer_out, total, full,
):
    j = pl.program_id(0)
    steps = pl.num_programs(0)

    @pl.when(j == 0)
    def _():
        total[...] = nn(d_narrow[...], small[0:ROW_EXPAND, :])

    first = [r[...] for r in (a0, a1, a2, a3)]
    other = [r[...] for r in (b0, b1, b2, b3)]

    @pl.when(j < 2)
    def _():
        place_rows(who, full, q_own[...], other)

    @pl.when((j >= 2) & (j < 4))
    def _():
        place_rows(who, full, k_own[...], first)

    @pl.when((j >= 4) & (j < 8))
    def _():
        place_rows(who, full, v_own[...], first)

    @pl.when(j >= 8)
    def _():
        place_rows(who, full, s_own[...], other)

    @pl.when(j < 8)
    def _():
        total[...] += nt(d_qkv[...], full[...])

    @pl.when(j >= 8)
    def _():
        total[...] += nt(d_swish[...], full[...])

    @pl.when(j == steps - 1)
    def _():
        values = x[...].astype(F32)
        upstream = total[...]
        scale = lax.rsqrt(jnp.mean(values * values, axis=-1, keepdims=True) + EPSILON)
        unit = values * scale
        mixer_out[...] = jnp.broadcast_to(
            jnp.sum(upstream * unit, axis=0, keepdims=True), mixer_out.shape
        )
        scaled = upstream * row_of(small, ROW_MIXER)
        mean = jnp.mean(scaled * unit, axis=-1, keepdims=True)
        grad_input[...] = (d_hidden[...] + scale * (scaled - unit * mean)).astype(BF16)


def input_back(who, x, small, d_hidden, d_qkv, d_swish, d_narrow, owns, pieces, gate_pieces):
    t, d = x.shape
    half = d // 2
    kd = HEADS * DK
    vd = HEADS * DV
    qn = kd // 256
    vn = vd // 256
    wn = 2 * qn + vn
    const = lambda j: (0, 0)
    beyond = lambda j: (0, jnp.where(j < wn, jnp.minimum(j, qn - 1), j - wn + qn))
    col = lambda low, count: (lambda j: (0, jnp.clip(j - low, 0, count - 1)))
    return call(
        input_back_kernel,
        (sds((t, d), BF16), sds((8, d), F32)),
        grid=(wn + vn,),
        in_specs=[
            SMEM,
            pl.BlockSpec((t, d), const),
            pl.BlockSpec(small.shape, const),
            pl.BlockSpec((t, d), const),
            pl.BlockSpec((t, 256), col(0, wn)),
            pl.BlockSpec((t, 256), col(wn, vn)),
            pl.BlockSpec((t, 16), const),
            pl.BlockSpec((half, 256), col(0, qn)),
            pl.BlockSpec((half, 256), col(qn, qn)),
            pl.BlockSpec((half, 256), col(2 * qn, vn)),
            pl.BlockSpec((half, 256), col(wn, vn)),
        ]
        + [pl.BlockSpec((half // 4, 256), col(qn, qn + vn))] * 4
        + [pl.BlockSpec((half // 4, 256), beyond)] * 4,
        out_specs=(pl.BlockSpec((t, d), const), pl.BlockSpec((8, d), const)),
        scratch_shapes=[pltpu.VMEM((t, d), F32), pltpu.VMEM((d, 256), BF16)], us=15)(who, x, small, d_hidden, d_qkv, d_swish, d_narrow, *owns, *pieces, *gate_pieces)


def late_grads_kernel(
    who, normed, d_qkv, d_narrow, narrow, d_pre, rows_in, bias_in,
    keep, send, scratch, strip, left_t, rows,
):
    t, d = normed.shape
    half = d // 2
    kd = HEADS * DK
    n = d_qkv.shape[1] // 256
    left_t[...] = normed[...].T
    for j in range(n):
        c = slice(j * 256, (j + 1) * 256)
        scratch[...] = nn(left_t[...], d_qkv[:, c]).astype(BF16)
        place_grads(who, keep, send, scratch, 0, c)
    rows[...] = jnp.zeros_like(rows)
    rows[LANE_FEED : LANE_FEED + 1, :] = rows_in[0:1, :]
    part = kd // 2
    rows[LANE_BIAS : LANE_BIAS + 1, 0:part] = bias_in[0:1, 0:part]
    rows[LANE_BIAS : LANE_BIAS + 1, half : half + part] = bias_in[0:1, part:kd]
    part = DV // 2
    rows[LANE_HEADS : LANE_HEADS + 1, 0:part] = rows_in[1:2, 0:part]
    rows[LANE_HEADS : LANE_HEADS + 1, half : half + part] = rows_in[1:2, part:DV]
    columns = rows[...].T
    squeeze = nn(left_t[...], d_narrow[...])
    expand = tn(d_pre[...], narrow[...])
    part = kd // 2
    strip[...] = columns.astype(BF16)
    strip[:, 0:16] = squeeze.astype(BF16)
    strip[0:part, LANE_EXPAND : LANE_EXPAND + 16] = expand[0:part].astype(BF16)
    strip[half : half + part, LANE_EXPAND : LANE_EXPAND + 16] = expand[part:kd].astype(BF16)
    place_grads(who, keep, send, strip, 0, slice(n * 256, n * 256 + 128))


def late_grads(who, normed, d_qkv, d_narrow, narrow, d_pre, rows_in, bias_in):
    t, d = normed.shape
    shape = sds((2, 2, 4, 32, d_qkv.shape[1] + 128), BF16)
    whole = lambda a: pl.BlockSpec(a.shape, lambda i: (0,) * len(a.shape))
    ins = (normed, d_qkv, d_narrow, narrow, d_pre, rows_in, bias_in)
    return call(
        late_grads_kernel,
        (shape, shape),
        us=10,
        grid=(1,),
        in_specs=[SMEM] + [whole(a) for a in ins],
        out_specs=(whole(shape), whole(shape)),
        scratch_shapes=[
            pltpu.VMEM((d, 256), BF16),
            pltpu.VMEM((d, 128), BF16),
            pltpu.VMEM((d, t), BF16),
            pltpu.VMEM((128, d), F32),
        ],
    )(who, *ins)


def settle_kernel(who, a, b, c, d, *outs):
    me = who[2]
    for k, part in enumerate((a, b, c, d)):
        for zz in range(4):
            rows = pl.ds(pl.multiple_of((me ^ (k * 4 + zz)) * 32, 32), 32)
            at = 0
            for out in outs:
                count = out.shape[1]
                out[rows, :] = part[zz, :, at : at + count].astype(F32)
                at += count


def settle(who, parts, half, widths):
    shapes = tuple(sds((half, width), F32) for width in widths)
    return call(settle_kernel, shapes, us=4, in_specs=[SMEM] + [VMEM] * 4)(who, *parts)


def feed_settle_kernel(who, a, b, c, d, *rest, first):
    gate, up, down = rest if first else rest[3:]
    h = pl.program_id(1)
    me = who[2]
    for k, part in enumerate((a, b, c, d)):
        for zz in range(4):
            block = me ^ (k * 4 + zz)
            rows = pl.ds(pl.multiple_of(block * 32, 32), 32)
            gate[rows, :] = part[zz, 0:32, :].astype(F32)
            up[rows, :] = part[zz, 32:64, :].astype(F32)
            at = pl.ds(pl.multiple_of((block % 4) * 32, 32), 32)
            cols = pl.ds(pl.multiple_of((block // 4) * 256 + h * 128, 128), 128)
            down[at, cols] = part[zz, 64:96, :].astype(F32)


def feed_settle(who, parts, before, start, blocks, half, ff, d):
    halves = ff // 256
    first = before is None
    shapes = (sds((half, ff), F32), sds((half, ff), F32), sds((ff // 2, d), F32))
    wide = pl.BlockSpec((half, 128), lambda j, h: (0, h * halves + start + j))
    tall = pl.BlockSpec((128, d), lambda j, h: (start + j, 0))
    any_spec = pl.BlockSpec(memory_space=pl.ANY)
    return call(
        functools.partial(feed_settle_kernel, first=first),
        shapes,
        us=2 * blocks,
        grid=(blocks, 2),
        in_specs=[SMEM]
        + [pl.BlockSpec((4, 96, 128), lambda j, h: (0, 0, 2 * j + h))] * 4
        + ([] if first else [any_spec] * 3),
        out_specs=(wide, wide, tall),
        input_output_aliases={} if first else {5: 0, 6: 1, 7: 2},
    )(who, *parts, *(() if first else before))


def added(*terms):
    total = terms[0].astype(F32)
    for term in terms[1:]:
        total = total + term.astype(F32)
    return total.astype(BF16)


def swap(v, bit):
    count = lax.axis_size("replica")
    return lax.ppermute(v, "replica", [(i, i ^ bit) for i in range(count)])


def cross(v):
    return lax.ppermute(v, "fsdp", [(0, 1), (1, 0)])


def tied(v, *after):
    return lax.optimization_barrier((v,) + after)[0]


def fenced(go, *jobs):
    work = lambda: tuple(job() for job in jobs)
    shapes = jax.eval_shape(work)
    blank = lambda: jax.tree.map(lambda a: jnp.zeros(a.shape, a.dtype), shapes)
    return lax.cond(go, work, blank)


class Chain:
    def __init__(self, keep, got):
        self.keep = keep
        self.got = got

    def to_y(self, now):
        return added(self.keep[0, 1], self.got[0, 1], tied(self.over, now)[1])

    def here(self, k, side):
        return self.keep[0, 0, k], self.got[0, 0, k], self.over[0, k], side[k]

    def to_near(self, now):
        side = tied(self.side, now)
        odd = slice(1, 4, 2)
        return added(*self.here(odd, side))

    def to_far(self, now):
        return added(*self.here(2, self.side), tied(self.near, now)[1])

    def to_line(self, now):
        side = tied(self.side, now)
        return [added(*self.here(k, side)) for k in range(1, 4)]

    def own_of_line(self, now):
        deep = tied(self.deep[0], now)
        self.own = added(*self.here(0, self.side), deep, *self.deep[1:])
        return self.own

    def own_of_far(self, now):
        self.own = added(*self.here(0, self.side), self.near[0], tied(self.far, now))
        return self.own

    def back_near(self, now):
        self.pair = jnp.stack([self.own, tied(self.far, now)])
        return self.pair

    def back_y(self, now):
        near = tied(self.near, now)
        self.line = jnp.stack([self.pair[0], near[0], self.pair[1], near[1]])
        return self.line

    def back_y_of_line(self, now):
        deep = tied(self.deep[0], now)
        self.line = jnp.stack([self.own, deep, *self.deep[1:]])
        return self.line


def over_core(keep, send):
    got = swap(send, 1)
    return got, added(keep[1], got[1])


def natural(keep, send):
    both = jnp.stack([keep, send])
    both = jnp.moveaxis(both, 0, 1)
    return both.reshape((2, 16) + keep.shape[3:])


def total_over(v, dim):
    v = lax.psum_scatter(v.astype(BF16), "fsdp", scatter_dimension=dim, tiled=True)
    return lax.psum(v, "replica").astype(F32)


def chain_join(earlier, later):
    factor_early, state_early, first_early, last_early = earlier
    factor_late, state_late, first_late, last_late = later
    joined = (first_late == last_early) | (last_early < 0) | (first_late < 0)
    linked = jnp.where(joined, factor_late, 0.0)
    return (
        linked * factor_early,
        linked[:, None] * state_early + state_late,
        jnp.where(first_early < 0, first_late, first_early),
        jnp.where(last_late < 0, last_early, last_late),
    )


def chained(payload, passing, first_mark):
    place = lax.axis_index("fsdp")
    own = (
        passing[0].reshape(HEADS, DK).astype(BF16),
        payload,
        first_mark.astype(BF16),
    )
    factors, payloads, firsts = [lax.all_gather(a, "fsdp") for a in own]
    rows = HEADS * DV

    def one(turn, carry):
        pick = lambda a: lax.dynamic_index_in_dim(a, turn, 0, False).astype(F32)
        factor, block, first = pick(factors), pick(payloads), pick(firsts)
        later = (factor, block[:rows].reshape(HEADS, DV, DK), first, block[rows, :1])
        earlier_factor, state, earlier_first, earlier_last = carry
        joined = (later[2] == earlier_last) | (earlier_last < 0)
        linked = jnp.where(joined, later[0], 0.0)
        return (
            linked * earlier_factor,
            linked[:, None, :] * state + later[1],
            jnp.where(earlier_first < 0, later[2], earlier_first),
            later[3],
        )

    none = -jnp.ones((1,), F32)
    start = (jnp.ones((HEADS, DK), F32), jnp.zeros((HEADS, DV, DK), F32), none, none)
    done = lax.fori_loop(0, place, one, start)
    marks = jnp.broadcast_to(done[3][:, None], (16, DK))
    return jnp.concatenate([done[1].reshape(rows, DK), marks]).astype(BF16)


def chained_back(back, passing, linked):
    count = lax.axis_size("fsdp")
    ahead = count - 1 - lax.axis_index("fsdp")
    factor = jnp.where(linked, passing[0], 0.0).reshape(HEADS, DK).astype(BF16)
    factors, backs = [lax.all_gather(a, "fsdp") for a in (factor, back)]

    def one(turn, grad):
        source = count - 1 - turn
        pick = lambda a: lax.dynamic_index_in_dim(a, source, 0, False).astype(F32)
        return pick(backs).reshape(HEADS, DV, DK) + pick(factors)[:, None, :] * grad

    grad = lax.fori_loop(0, ahead, one, jnp.zeros((HEADS, DV, DK), F32))
    return grad.reshape(HEADS * DV, DK).astype(BF16)


def on_device(
    inputs, segments, cotangent, mixer_gain, query_map, key_map, value_map, swish_map, squeeze,
    expand, forget_bias, head_gain, readout, feed_gain, gate_map, up_map, down_map,
):
    shards = lax.axis_size("fsdp")
    copies = lax.axis_size("replica")
    paired = shards == 2 and copies == 16
    t, d = inputs.shape
    kd, vd = HEADS * DK, HEADS * DV
    half = d // 2
    quarter = half // 4
    marks = segments[0].astype(F32)
    mcol, mrow = marks[:, None], marks[None, :]

    if paired:
        place = lax.axis_index("replica")
        core, side, deep = place % 2, (place // 2) % 2, place // 4
        x = lax.axis_index("fsdp")
        q = side * 2 + core
        who = jnp.stack([x, q, core * 8 + side * 4 + deep]).astype(jnp.int32)
    else:
        who = jnp.zeros((3,), jnp.int32)
        x = q = 0
        gather = lambda a, dim=0: lax.all_gather(a, "fsdp", axis=dim, tiled=True)
        query_map, key_map, value_map, swish_map, readout, gate_map, up_map, down_map = [
            gather(a)
            for a in (query_map, key_map, value_map, swish_map, readout, gate_map, up_map, down_map)
        ]
        mixer_gain, feed_gain, forget_bias, head_gain, squeeze = [
            gather(a) for a in (mixer_gain, feed_gain, forget_bias, head_gain, squeeze)
        ]
        expand = gather(expand, 1)

    def small_half(k):
        cut = lambda a, dim=0: lax.slice_in_dim(a, k * (a.shape[dim] // 2), (k + 1) * (a.shape[dim] // 2), axis=dim)
        return packed(cut(squeeze), cut(expand, 1), cut(mixer_gain), cut(feed_gain), cut(forget_bias), cut(head_gain))

    def packed(squeeze, expand, mixer_gain, feed_gain, forget_bias, head_gain):
        wide = lambda a: jnp.pad(a, ((0, 0), (0, half - a.shape[1])))
        mixed = jnp.concatenate([forget_bias, head_gain])[None]
        rows = [squeeze.T, wide(expand), mixer_gain[None], feed_gain[None], wide(mixed)]
        block = jnp.concatenate(rows)
        return jnp.pad(block, ((0, SMALL_ROWS - block.shape[0]), (0, 0)))

    ff = gate_map.shape[1]
    halves = ff // 256
    counts = chunk_blocks(halves)
    starts = [sum(counts[:i]) for i in range(len(counts))]

    def quarter_rows(a, k):
        return lax.dynamic_slice_in_dim(a, k * quarter, quarter, 0)

    if paired:
        return paired_device(
            who, x, q, mcol, mrow, inputs, cotangent, query_map, key_map, value_map, swish_map,
            readout, gate_map, up_map, down_map,
            packed(squeeze, expand, mixer_gain, feed_gain, forget_bias, head_gain),
            starts, counts,
        )
    small = jnp.concatenate([small_half(0), small_half(1)], axis=1)
    lower = lambda a: a[: a.shape[0] // 2]
    upper = lambda a: a[a.shape[0] // 2 :]
    share = lambda maps: tuple(
        jnp.concatenate([quarter_rows(upper(a), k) for a in maps], axis=1) for k in range(4)
    )
    kv_pieces = share((key_map, value_map))
    gate_pieces = share((query_map, swish_map))
    read_pieces = share((readout,))
    others = (upper(gate_map), upper(up_map), upper(down_map))
    feed_pieces = [
        tuple(
            pack_feed(jnp.full((3,), k, jnp.int32), *others, s, n) for k in range(4)
        )
        for s, n in zip(starts, counts)
    ]
    query_map, key_map, value_map, swish_map, readout, gate_map, up_map, down_map = [
        lower(a)
        for a in (query_map, key_map, value_map, swish_map, readout, gate_map, up_map, down_map)
    ]

    normed, kv, pre, narrow = project(who, inputs, small, key_map, value_map, kv_pieces)
    local, passing = local_state(kv, pre, mcol, mrow)
    payload = chained(local, passing, marks[:1])
    queries, swish = swish_project(who, normed, query_map, swish_map, gate_pieces)
    mixed, states, gated, hidden, second = mixer(
        who, inputs, small, queries, kv, pre, swish, mcol, mrow, payload, readout, read_pieces
    )

    totals = None
    feed_grads = []
    for s, n, pieces in zip(starts, counts, feed_pieces):
        *totals, keep, send = feed(
            who, second, cotangent, gate_map, up_map, down_map, pieces, totals, s, n
        )
        feed_grads.append((keep, send))
    output = (hidden + totals[0]).astype(BF16)

    d_hidden, low, d_swish, d_mixed, rows, back = mixer_back(
        who, small, totals[1], hidden, cotangent, swish, mixed, queries, pre, mcol, payload,
        readout, read_pieces,
    )
    linked = marks[0] == payload[HEADS * DV, 0].astype(F32)
    entering = chained_back(back, passing, linked)
    gate_grad = gate_grads(who, normed, d_swish, gated, low)
    d_qkv, d_pre, d_narrow, bias_row = recurrence_back(
        small, queries, kv, pre, d_mixed, mcol, mrow, payload, states, entering
    )
    grad_input, mixer_row = input_back(
        who, inputs, small, d_hidden, d_qkv, d_swish, d_narrow,
        (query_map, key_map, value_map, swish_map), kv_pieces, gate_pieces,
    )
    late_grad = late_grads(who, normed, d_qkv, d_narrow, narrow, d_pre, rows, bias_row)

    gates, ups, downs = [], [], []
    for (keep, send), n in zip(feed_grads, counts):
        block = natural(keep, send)
        sides = lambda k: block[:, :, 32 * k : 32 * (k + 1), :].reshape(d, n, 2, 128)
        gates.append(sides(0))
        ups.append(sides(1))
        part = block[:, :, 64:96, :].reshape(2, 4, 128, n, 256)
        downs.append(part.transpose(0, 3, 2, 1, 4).reshape(2, n * 128, d))
    whole = lambda parts: jnp.concatenate(parts, axis=1).transpose(0, 2, 1, 3).reshape(d, ff)
    grad_gate, grad_up = whole(gates), whole(ups)
    grad_down = jnp.concatenate(downs, axis=1).reshape(ff, d)
    flat = lambda pair: natural(*pair).reshape(d, -1)
    gate_flat, late_flat = flat(gate_grad), flat(late_grad)
    strip = late_flat[:, 2 * kd + vd :]
    joined = lambda lane, count: jnp.concatenate(
        [strip[:count, lane], strip[half : half + count, lane]]
    )
    part = kd // 2
    grad_expand = jnp.concatenate([strip[:part, 16:32], strip[half : half + part, 16:32]]).T
    results = (
        mixer_row[0], late_flat[:, :kd], late_flat[:, kd : 2 * kd],
        late_flat[:, 2 * kd : 2 * kd + vd],
        gate_flat[:, :vd], strip[:, :16], grad_expand, joined(LANE_BIAS, part),
        joined(LANE_HEADS, DV // 2), gate_flat[:, vd:], joined(LANE_FEED, half),
        grad_gate, grad_up, grad_down,
    )
    return (output, grad_input) + tuple(
        total_over(a, 1 if i == 6 else 0) for i, a in enumerate(results)
    )


def paired_device(
    who, x, q, mcol, mrow, inputs, cotangent, query_map, key_map, value_map, swish_map,
    readout, gate_map, up_map, down_map, small_own, starts, counts,
):
    t, d = inputs.shape
    half = d // 2
    quarter = half // 4
    kd = HEADS * DK
    ff = gate_map.shape[1]

    def share(maps):
        cut = lambda a: lax.dynamic_slice_in_dim(a, q * quarter, quarter, 0)
        return jnp.concatenate([cut(a) for a in maps], axis=1)

    def spread(first, *after):
        second = swap(first, 2)
        return (first, swap(first, 1), second, swap(second, 1))

    go = x < 2
    vd = HEADS * DV

    def together(*values):
        return lax.optimization_barrier(values)

    def core_step(grads, *after):
        keep, send = grads
        ((got, out),) = fenced(tied(go, *after), lambda: over_core(keep, send))
        return Chain(keep, got), out

    small_other = cross(small_own)
    kv_share = share((key_map, value_map))
    kv_first = cross(kv_share)
    gate_share = share((tied(query_map, kv_share), swish_map))
    read_share = share((tied(readout, kv_share),))
    feed_shares = [
        pack_feed(tied(who, gate_share, read_share), gate_map, up_map, down_map, s, n)
        for s, n in zip(starts, counts)
    ]
    kv_first, small_other, gate_share, read_share, *feed_shares = together(
        kv_first, small_other, gate_share, read_share, *feed_shares
    )
    kv_second, kv_third = swap(kv_first, 2), swap(kv_first, 1)
    gate_first = cross(gate_share)
    small = jnp.concatenate(
        [jnp.where(x == 0, small_own, small_other), jnp.where(x == 0, small_other, small_own)],
        axis=1,
    )
    gate_first, kv_second = together(gate_first, kv_second)
    kv_pieces = (kv_first, kv_third, kv_second, swap(kv_second, 1))
    gate_second, gate_third = swap(gate_first, 2), swap(gate_first, 1)
    read_first = cross(tied(read_share, gate_first))
    f0_first = cross(tied(feed_shares[0], gate_first))
    normed, kv, pre, narrow = project(
        tied(who, gate_first), inputs, small, key_map, value_map, kv_pieces
    )
    gate_second, read_first, normed = together(gate_second, read_first, normed)
    gate_fourth = swap(gate_second, 1)
    gate_pieces = (gate_first, gate_third, gate_second, gate_fourth)
    read_second, read_third = swap(read_first, 2), swap(read_first, 1)
    local, _ = local_state(kv, pre, mcol, tied(mrow, normed))
    payload, (queries, swish) = fenced(
        tied(go, local, gate_fourth, read_third),
        lambda: lax.ppermute(local, "fsdp", [(0, 1)]),
        lambda: swish_project(who, normed, query_map, swish_map, gate_pieces),
    )
    f0_first, read_second, swish = together(f0_first, read_second, swish)
    f0_second, f0_third = swap(f0_first, 2), swap(f0_first, 1)
    read_pieces = (read_first, read_third, read_second, swap(read_second, 1))
    f1_first = cross(tied(feed_shares[1], f0_first))
    mixed, states, gated, hidden, second = mixer(
        tied(who, swish), inputs, small, queries, kv, pre, swish, mcol, mrow, payload,
        readout, read_pieces,
    )
    f0_second, f1_first, hidden = together(f0_second, f1_first, hidden)
    f0_pieces = (f0_first, f0_third, f0_second, swap(f0_second, 1))
    f1_second, f1_third = swap(f1_first, 2), swap(f1_first, 1)
    f2_first = cross(tied(feed_shares[2], f1_first))

    def feed_part(i, pieces, totals, *after):
        *totals, keep, send = feed(
            tied(who, *after), second, cotangent, gate_map, up_map, down_map, pieces, totals,
            starts[i], counts[i],
        )
        return totals, (keep, send)

    totals, grads = feed_part(0, f0_pieces, None, hidden, f1_first)
    f0, out = core_step(grads, totals[0], f1_third)
    f2_first, f1_second, out = together(f2_first, f1_second, out)
    f0.over = cross(out)
    f1_pieces = (f1_first, f1_third, f1_second, swap(f1_second, 1))
    f2_second, f2_third = swap(f2_first, 2), swap(f2_first, 1)
    totals, grads = feed_part(1, f1_pieces, totals, out)
    f1, out = core_step(grads, totals[0], f2_second, f2_third)
    a = f0.to_y(out)
    a, out = together(a, out)
    f1.over = cross(out)
    f0.side = swap(a, 2)
    f2_pieces = (f2_first, f2_third, f2_second, swap(tied(f2_second, a), 1))
    totals, grads = feed_part(2, f2_pieces, totals, a)
    a = f0.to_near(totals[0])
    f0.near = swap(a, 4)
    keep, send = grads
    back_parts, (got, f2_out) = fenced(
        tied(go, a),
        lambda: mixer_back(
            who, small, totals[1], hidden, cotangent, swish, mixed, queries, pre, mcol, payload,
            readout, read_pieces,
        ),
        lambda: over_core(keep, send),
    )
    d_hidden, low, d_swish, d_mixed, rows, back = back_parts
    f2 = Chain(keep, got)
    a, b = f0.to_far(back), f1.to_y(back)
    a, b, back, out = together(a, b, back, f2_out)
    f2.over = cross(out)
    entering = lax.ppermute(back, "fsdp", [(1, 0)])
    f0.far = swap(a, 8)
    f1.side = swap(b, 2)
    keep, send = gate_grads(tied(who, a), normed, d_swish, gated, low)
    a = f0.own_of_far(keep)
    a, entering = together(a, entering)
    f0.far = swap(a, 8)
    (d_qkv, d_pre, d_narrow, bias_row), (got, g_out) = fenced(
        tied(go, a),
        lambda: recurrence_back(
            small, queries, kv, pre, d_mixed, mcol, mrow, payload, states, entering
        ),
        lambda: over_core(keep, send),
    )
    g = Chain(keep, got)
    a, b = f0.back_near(d_qkv), f1.to_near(d_qkv)
    a, b, out = together(a, b, g_out)
    f0.near, f1.near = swap(a, 4), swap(b, 4)
    g.over = cross(out)
    keep, send = late_grads(tied(who, a), normed, d_qkv, d_narrow, narrow, d_pre, rows, bias_row)
    a, b, c = f0.back_y(keep), f1.to_far(keep), f2.to_y(keep)
    a, b, c = together(a, b, c)
    f0.beside, f1.far, f2.side = swap(a, 2), swap(b, 8), swap(c, 2)
    (grad_input, mixer_row), (got, v_out) = fenced(
        tied(go, a),
        lambda: input_back(
            who, inputs, small, d_hidden, d_qkv, d_swish, d_narrow,
            (query_map, key_map, value_map, swish_map), kv_pieces, gate_pieces,
        ),
        lambda: over_core(keep, send),
    )
    v = Chain(keep, got)
    a, b, c = f1.own_of_far(mixer_row), f2.to_near(mixer_row), g.to_y(mixer_row)
    f0_beside, a, b, c, out, mixer_row = together(f0.beside, a, b, c, v_out, mixer_row)
    v.over = cross(out)
    f1.far, f2.near, g.side = swap(a, 8), swap(b, 4), swap(c, 2)
    f0_parts = (f0.line, f0_beside, swap(f0.line, 1), swap(f0_beside, 1))
    mixer_half = jnp.where(x == 0, mixer_row[:, :half], mixer_row[:, half:])
    mixer_half = mixer_half + cross(jnp.where(x == 0, mixer_row[:, half:], mixer_row[:, :half]))
    output = (tied(hidden, b) + totals[0]).astype(BF16)
    feeds = feed_settle(tied(who, output), f0_parts, None, starts[0], counts[0], half, ff, d)
    a, b, c = f1.back_near(feeds[0]), f2.to_far(feeds[0]), g.to_near(feeds[0])
    a, b, c, mixer_half = together(a, b, c, mixer_half)
    f1.near, f2.far, g.near = swap(a, 4), swap(b, 8), swap(c, 4)
    mixer_half = mixer_half + swap(mixer_half, 1)
    a, b, c, e = f1.back_y(a), f2.own_of_far(a), g.to_far(a), v.to_y(a)
    a, b, c, e, mixer_half = together(a, b, c, e, mixer_half)
    f1.beside, f2.far, g.far, v.side = swap(a, 2), swap(b, 8), swap(c, 8), swap(e, 2)
    mixer_half = mixer_half + swap(mixer_half, 2)
    a, b, c = f2.back_near(a), g.own_of_far(a), v.to_near(a)
    f1_beside, a, b, c, mixer_half = together(f1.beside, a, b, c, mixer_half)
    f2.near, g.far, v.near = swap(a, 4), swap(b, 8), swap(c, 4)
    f1_parts = (f1.line, f1_beside, swap(f1.line, 1), swap(f1_beside, 1))
    a, b, c = f2.back_y(a), g.back_near(a), v.to_far(a)
    a, b, c, mixer_half = together(a, b, c, mixer_half)
    f2.beside, g.near, v.far = swap(a, 2), swap(b, 4), swap(c, 8)
    feeds = feed_settle(tied(who, a), f1_parts, feeds, starts[1], counts[1], half, ff, d)
    b, c = g.back_y(feeds[0]), v.own_of_far(feeds[0])
    f2_beside, b, c, mixer_half = together(f2.beside, b, c, mixer_half)
    f2_parts = (f2.line, f2_beside, swap(f2.line, 1), swap(f2_beside, 1))
    g.beside, v.far = swap(b, 2), swap(c, 8)
    mixer_half = mixer_half + swap(mixer_half, 4)
    c = v.back_near(c)
    g_beside, c, mixer_half = together(g.beside, c, mixer_half)
    v.near = swap(c, 4)
    g_parts = (g.line, g_beside, swap(g.line, 1), swap(g_beside, 1))
    feeds = feed_settle(tied(who, c), f2_parts, feeds, starts[2], counts[2], half, ff, d)
    c = v.back_y(feeds[0])
    c, mixer_half = together(c, mixer_half)
    v.beside = swap(c, 2)
    mixer_half = mixer_half + swap(mixer_half, 8)
    grad_swish, grad_readout = settle(tied(who, c), g_parts, half, (vd, vd))
    v_beside = tied(v.beside, grad_swish)
    v_parts = (v.line, v_beside, swap(v.line, 1), swap(v_beside, 1))
    grad_query, grad_key, grad_value, strip = settle(
        tied(who, grad_swish), v_parts, half, (kd, kd, vd, 128)
    )
    grad_gate, grad_up, grad_down = feeds
    return (
        output, grad_input, mixer_half[0], grad_query, grad_key, grad_value, grad_swish,
        strip[:, :16], strip[: kd // 2, LANE_EXPAND : LANE_EXPAND + 16].T,
        strip[: kd // 2, LANE_BIAS], strip[: DV // 2, LANE_HEADS], grad_readout,
        strip[:, LANE_FEED], grad_gate, grad_up, grad_down,
    )


def chunk_blocks(halves):
    parts = 3
    base, extra = divmod(halves, parts)
    return [base + (1 if i >= parts - extra else 0) for i in range(parts)]


def solution(mesh):
    placed = (
        P(("replica", "fsdp"), None),
        P("replica", "fsdp"),
        P(("replica", "fsdp"), None),
        P("fsdp"),
        P("fsdp", None),
        P("fsdp", None),
        P("fsdp", None),
        P("fsdp", None),
        P("fsdp", None),
        P(None, "fsdp"),
        P("fsdp"),
        P("fsdp"),
        P("fsdp", None),
        P("fsdp"),
        P("fsdp", None),
        P("fsdp", None),
        P("fsdp", None),
    )
    return jax.shard_map(
        on_device,
        mesh=mesh,
        in_specs=placed,
        out_specs=(
            P(("replica", "fsdp"), None),
            P(("replica", "fsdp"), None),
            P("fsdp"),
            P("fsdp", None),
            P("fsdp", None),
            P("fsdp", None),
            P("fsdp", None),
            P("fsdp", None),
            P(None, "fsdp"),
            P("fsdp"),
            P("fsdp"),
            P("fsdp", None),
            P("fsdp"),
            P("fsdp", None),
            P("fsdp", None),
            P("fsdp", None),
        ),
        check_vma=False,
    )
```

```python
import functools

import jax
import jax.numpy as jnp
from jax import lax
from jax.experimental import pallas as pl
from jax.experimental.pallas import tpu as pltpu
from jax.sharding import PartitionSpec as P

HEADS = 4
DK = 128
DV = 256
SPAN = 64
WIDE = 2 * SPAN

EPSILON = 1e-06
HEAD_FLOOR = 16.0
GATE_NORM = 16.0

F32 = jnp.float32
BF16 = jnp.bfloat16
MIB = 1024 * 1024

ROW_EXPAND = 16
ROW_MIXER = 32
ROW_FEED = 33
ROW_MIXED = 34
SMALL_ROWS = 48
LANE_EXPAND = 16
LANE_FEED = 32
LANE_BIAS = 33
LANE_HEADS = 34
LANE_MIXER = 35


def nn(a, b):
    return lax.dot_general(a, b, (((1,), (0,)), ((), ())), preferred_element_type=F32)


def nt(a, b):
    return lax.dot_general(a, b, (((1,), (1,)), ((), ())), preferred_element_type=F32)


def tn(a, b):
    return lax.dot_general(a, b, (((0,), (0,)), ((), ())), preferred_element_type=F32)


def sigmoid(v):
    return 1.0 / (1.0 + jnp.exp(-v))


def cost(us):
    return pl.CostEstimate(
        flops=int(us * 1e7), bytes_accessed=int(us * 3.6e4), transcendentals=0
    )


def call(kernel, out_shape, us=5, vmem=30, **kw):
    return pl.pallas_call(
        kernel,
        out_shape=out_shape,
        cost_estimate=cost(us),
        compiler_params=pltpu.CompilerParams(vmem_limit_bytes=vmem * MIB),
        **kw,
    )


def sds(shape, dtype):
    return jax.ShapeDtypeStruct(shape, dtype)


SMEM = pl.BlockSpec(memory_space=pltpu.SMEM)
VMEM = pl.BlockSpec(memory_space=pltpu.VMEM)


def split_sum(ones, values):
    high = values.astype(BF16)
    rest = values - high.astype(F32)
    middle = rest.astype(BF16)
    low = (rest - middle.astype(F32)).astype(BF16)
    return nn(ones, high) + nn(ones, middle) + nn(ones, low)


def lower_ones(size):
    rows = lax.broadcasted_iota(jnp.int32, (size, size), 0)
    cols = lax.broadcasted_iota(jnp.int32, (size, size), 1)
    return (rows >= cols).astype(F32).astype(BF16)


def upper_ones(size):
    rows = lax.broadcasted_iota(jnp.int32, (size, size), 0)
    cols = lax.broadcasted_iota(jnp.int32, (size, size), 1)
    return (rows <= cols).astype(F32).astype(BF16)


def log_decay(pre):
    return (jnp.minimum(pre, 0.0) - jnp.log1p(jnp.exp(-jnp.abs(pre)))) / GATE_NORM


def row_of(small_ref, row):
    return small_ref[ROW_MIXER:SMALL_ROWS, :].astype(F32)[row - ROW_MIXER : row - ROW_MIXER + 1, :]


def expand_of(small_ref):
    half = small_ref.shape[1] // 2
    quarter = half // 2
    part = small_ref[ROW_EXPAND:ROW_MIXER, :]
    return jnp.concatenate([part[:, :quarter], part[:, half : half + quarter]], axis=1)


def bias_of(small_ref):
    half = small_ref.shape[1] // 2
    quarter = half // 2
    row = row_of(small_ref, ROW_MIXED)
    return jnp.concatenate([row[:, :quarter], row[:, half : half + quarter]], axis=1)


def head_gain_of(small_ref):
    half = small_ref.shape[1] // 2
    at = half // 2
    count = DV // 2
    row = row_of(small_ref, ROW_MIXED)
    return jnp.concatenate([row[:, at : at + count], row[:, half + at : half + at + count]], axis=1)


def place_rows(who_ref, full_ref, own, pieces):
    x = who_ref[0]
    q = who_ref[1] & (len(pieces) - 1)
    half = own.shape[0]
    rows = pieces[0].shape[0]
    full_ref[pl.ds(pl.multiple_of(x * half, half), half), :] = own
    for k in range(len(pieces)):
        at = (1 - x) * half + (q ^ k) * rows
        full_ref[pl.ds(pl.multiple_of(at, rows), rows), :] = pieces[k]


def place_grads(who_ref, keep_ref, send_ref, scratch_ref, row, cols, rows=32):
    x = who_ref[0]
    me = who_ref[2]
    half = scratch_ref.shape[0] // 2
    for core, out_ref in ((0, keep_ref), (1, send_ref)):
        for xx in range(2):
            for yy in range(2):
                for zz in range(4):
                    block = me ^ (core * 8 + yy * 4 + zz)
                    at = pl.multiple_of((x ^ xx) * half + block * rows, rows)
                    out_ref[xx, yy, zz, row : row + rows, cols] = scratch_ref[pl.ds(at, rows), :]


def project_kernel(
    who, x, small, k_own, v_own, r0, r1, r2, r3, normed, kv, pre, narrow_out, full
):
    j = pl.program_id(0)

    @pl.when(j == 0)
    def _():
        tokens = x[...].astype(F32)
        mean_sq = jnp.mean(tokens * tokens, axis=-1, keepdims=True)
        normed[...] = (
            tokens * lax.rsqrt(mean_sq + EPSILON) * row_of(small, ROW_MIXER)
        ).astype(BF16)
        narrow = nt(normed[...], small[0:ROW_EXPAND, :]).astype(BF16)
        narrow_out[...] = narrow
        pre[...] = nn(narrow, expand_of(small)) + bias_of(small)

    pieces = [r[...] for r in (r0, r1, r2, r3)]

    @pl.when(j < 2)
    def _():
        place_rows(who, full, k_own[...], pieces)

    @pl.when(j >= 2)
    def _():
        place_rows(who, full, v_own[...], pieces)

    kv[...] = nn(normed[...], full[...]).astype(BF16)


def project(who, x, small, k_own, v_own, pieces):
    t, d = x.shape
    half = d // 2
    kd = HEADS * DK
    vd = HEADS * DV
    width = kd + vd
    const = lambda j: (0, 0)
    qn = kd // 256
    vn = vd // 256
    return call(
        project_kernel,
        (sds((t, d), BF16), sds((t, width), BF16), sds((t, kd), F32), sds((t, 16), BF16)),
        grid=(width // 256,),
        in_specs=[
            SMEM,
            pl.BlockSpec((t, d), const),
            pl.BlockSpec(small.shape, const),
            pl.BlockSpec((half, 256), lambda j: (0, jnp.minimum(j, qn - 1))),
            pl.BlockSpec((half, 256), lambda j: (0, jnp.clip(j - qn, 0, vn - 1))),
        ]
        + [pl.BlockSpec((half // 4, 256), lambda j: (0, j))] * 4,
        out_specs=(
            pl.BlockSpec((t, d), const),
            pl.BlockSpec((t, 256), lambda j: (0, j)),
            pl.BlockSpec((t, kd), const),
            pl.BlockSpec((t, 16), const),
        ),
        scratch_shapes=[pltpu.VMEM((d, 256), BF16)],
    )(who, x, small, k_own, v_own, *pieces)


def swish_kernel(who, normed, q_own, s_own, r0, r1, r2, r3, queries, swish, full):
    j = pl.program_id(0)
    pieces = [r[...] for r in (r0, r1, r2, r3)]

    @pl.when(j < 2)
    def _():
        place_rows(who, full, q_own[...], pieces)
        queries[...] = nn(normed[...], full[...]).astype(BF16)

    @pl.when(j >= 2)
    def _():
        place_rows(who, full, s_own[...], pieces)
        swish[...] = nn(normed[...], full[...])


def swish_project(who, normed, q_own, s_own, pieces):
    t, d = normed.shape
    half = d // 2
    kd = HEADS * DK
    vd = HEADS * DV
    qn = kd // 256
    vn = vd // 256
    low = lambda j: (0, jnp.minimum(j, qn - 1))
    high = lambda j: (0, jnp.clip(j - qn, 0, vn - 1))
    return call(
        swish_kernel,
        (sds((t, kd), BF16), sds((t, vd), F32)),
        grid=(qn + vn,),
        in_specs=[
            SMEM,
            pl.BlockSpec((t, d), lambda j: (0, 0)),
            pl.BlockSpec((half, 256), low),
            pl.BlockSpec((half, 256), high),
        ]
        + [pl.BlockSpec((half // 4, 256), lambda j: (0, j))] * 4,
        out_specs=(pl.BlockSpec((t, 256), low), pl.BlockSpec((t, 256), high)),
        scratch_shapes=[pltpu.VMEM((d, 256), BF16)],
    )(who, normed, q_own, s_own, *pieces)


def mark_at(mrow, place):
    return mrow[0:1, place : place + 1]


def state_kernel(kv, pre, mcol, mrow, payload, passing):
    t = pre.shape[0]
    kd = HEADS * DK
    ones = lower_ones(WIDE)
    states = [jnp.zeros((DV, DK), F32) for _ in range(HEADS)]
    total = jnp.zeros((1, kd), F32)
    for i in range(t // WIDE):
        rows = slice(i * WIDE, (i + 1) * WIDE)
        cumul = split_sum(ones, log_decay(pre[rows, :]))
        end = cumul[WIDE - 1 : WIDE, :]
        total = total + end
        last = mark_at(mrow, (i + 1) * WIDE - 1)
        keys = kv[rows, 0:kd].astype(F32)
        tail = jnp.where(mcol[rows, :] == last, keys * jnp.exp(end - cumul), 0.0).astype(BF16)
        if i:
            keep = jnp.where(mark_at(mrow, i * WIDE - 1) == last, jnp.exp(end), 0.0)
        for h in range(HEADS):
            c = slice(h * DK, (h + 1) * DK)
            values = kv[rows, kd + h * DV : kd + (h + 1) * DV]
            update = tn(values, tail[:, c])
            states[h] = states[h] * keep[:, c] + update if i else update
    for h in range(HEADS):
        payload[h * DV : (h + 1) * DV, :] = states[h].astype(BF16)
    last = mark_at(mrow, t - 1)
    payload[HEADS * DV :, :] = jnp.broadcast_to(last, (16, DK)).astype(BF16)
    passes = jnp.where(mark_at(mrow, 0) == last, jnp.exp(total), 0.0)
    passing[...] = jnp.broadcast_to(passes, passing.shape)


def local_state(kv, pre, mcol, mrow):
    return call(
        state_kernel,
        (sds((HEADS * DV + 16, DK), BF16), sds((8, HEADS * DK), F32)), us=5)(kv, pre, mcol, mrow)


def mixer_kernel(
    small, q, kv, pre, swish, mcol, mrow, payload, mixed_out, states_out, gated_out
):
    t = q.shape[0]
    kd = HEADS * DK
    ones = lower_ones(WIDE)
    causal_rows = lax.broadcasted_iota(jnp.int32, (WIDE, WIDE), 0)
    causal_cols = lax.broadcasted_iota(jnp.int32, (WIDE, WIDE), 1)
    states = [payload[h * DV : (h + 1) * DV, :].astype(F32) for h in range(HEADS)]
    before = payload[HEADS * DV :, :].astype(F32)[0:1, 0:1]
    for i in range(t // WIDE):
        rows = slice(i * WIDE, (i + 1) * WIDE)
        marks = mcol[rows, :]
        last = mark_at(mrow, (i + 1) * WIDE - 1)
        cumul = split_sum(ones, log_decay(pre[rows, :]))
        middle = cumul[SPAN - 1 : SPAN, :]
        end = cumul[WIDE - 1 : WIDE, :]
        queries = q[rows, :].astype(F32)
        keys = kv[rows, 0:kd].astype(F32)
        lifted = (queries * jnp.exp(cumul - middle)).astype(BF16)
        lowered = (keys * jnp.exp(middle - cumul)).astype(BF16)
        carried = jnp.where(marks == before, queries * jnp.exp(cumul), 0.0).astype(BF16)
        tail = jnp.where(marks == last, keys * jnp.exp(end - cumul), 0.0).astype(BF16)
        keep = jnp.where(before == last, jnp.exp(end), 0.0)
        causal = (causal_rows >= causal_cols) & (marks == mrow[0:1, rows])
        for h in range(HEADS):
            c = slice(h * DK, (h + 1) * DK)
            values = kv[rows, kd + h * DV : kd + (h + 1) * DV]
            low_state = states[h].astype(BF16)
            states_out[i, h] = low_state
            scores = jnp.where(causal, nt(lifted[:, c], lowered[:, c]), 0.0).astype(BF16)
            mixed_out[rows, h * DV : (h + 1) * DV] = nn(scores, values) + nt(
                carried[:, c], low_state
            )
            states[h] = states[h] * keep[:, c] + tn(values, tail[:, c])
        before = last
    gain = head_gain_of(small)
    for h in range(HEADS):
        c = slice(h * DV, (h + 1) * DV)
        mixed = mixed_out[:, c]
        scale = lax.rsqrt(jnp.mean(mixed * mixed, axis=-1, keepdims=True) + HEAD_FLOOR)
        pre_gate = swish[:, c]
        gated_out[:, c] = (mixed * scale * gain * (pre_gate * sigmoid(pre_gate))).astype(BF16)


def mixer(small, q, kv, pre, swish, mcol, mrow, payload):
    t = q.shape[0]
    vd = HEADS * DV
    outs = (
        sds((t, vd), F32),
        sds((t // WIDE, HEADS, DV, DK), BF16),
        sds((t, vd), BF16),
    )
    return call(mixer_kernel, outs, us=8)(small, q, kv, pre, swish, mcol, mrow, payload)


def reader_kernel(who, x, small, gated, own, r0, r1, hidden_out, second_out, full):
    place_rows(who, full, own[...], [r0[...], r1[...]])
    hidden = x[...].astype(F32) + nn(gated[...], full[...])
    hidden_out[...] = hidden
    mean_sq = jnp.mean(hidden * hidden, axis=-1, keepdims=True)
    second_out[...] = (
        hidden * lax.rsqrt(mean_sq + EPSILON) * row_of(small, ROW_FEED)
    ).astype(BF16)


def reader(who, x, small, gated, own, pieces):
    t, d = x.shape
    ins = (x, small, gated, own, *pieces)
    return call(
        reader_kernel,
        (sds((t, d), F32), sds((t, d), BF16)),
        us=3,
        in_specs=[SMEM] + [VMEM] * len(ins),
        scratch_shapes=[pltpu.VMEM((gated.shape[1], d), BF16)],
    )(who, *ins)


def feed_kernel(
    who, second, cot, g0, g1, u0, u1, down, r0, r1, r2, r3,
    part_out, part_ds, keep, send, wg, wu, wd, sec_t, sg_, su_, sd_, total_out, total_ds,
):
    j = pl.program_id(0)

    @pl.when(j == 0)
    def _():
        total_out[...] = jnp.zeros_like(total_out)
        total_ds[...] = jnp.zeros_like(total_ds)
        sec_t[...] = second[...].T

    x = who[0]
    q = who[1]
    half = g0.shape[0]
    rows = pl.ds(pl.multiple_of(x * half, half), half)
    wg[rows, 0:128] = g0[...]
    wg[rows, 128:256] = g1[...]
    wu[rows, 0:128] = u0[...]
    wu[rows, 128:256] = u1[...]
    wd[pl.ds(pl.multiple_of(x * 128, 128), 128), :] = down[...]
    for k, r in enumerate((r0, r1, r2, r3)):
        at = q ^ k
        rows = pl.ds(pl.multiple_of((1 - x) * half + at * 128, 128), 128)
        wg[rows, :] = r[:, 0:256]
        wu[rows, :] = r[:, 256:512]
        wd[pl.ds(pl.multiple_of((1 - x) * 128, 128), 128), pl.ds(pl.multiple_of(at * 256, 256), 256)] = r[:, 512:768]
    gate = nn(second[...], wg[...])
    upward = nn(second[...], wu[...])
    d_inner = nt(cot[...], wd[...])
    sig = sigmoid(gate)
    silu = gate * sig
    inner = (silu * upward).astype(BF16)
    d_gate = (d_inner * upward * sig * (1.0 + gate * (1.0 - sig))).astype(BF16)
    d_up = (d_inner * silu).astype(BF16)
    total_out[...] += nn(inner, wd[...])
    total_ds[...] += nt(d_gate, wg[...]) + nt(d_up, wu[...])
    sg_[...] = nn(sec_t[...], d_gate).astype(BF16)
    su_[...] = nn(sec_t[...], d_up).astype(BF16)
    grad_down = tn(inner, cot[...]).astype(BF16)
    for part in range(2):
        for cb in range(4):
            at = part * half + cb * 128
            sd_[at : at + 128, :] = grad_down[part * 128 : (part + 1) * 128, cb * 256 : (cb + 1) * 256]
    cols = slice(0, 256)
    place_grads(who, keep, send, sg_, 0, cols)
    place_grads(who, keep, send, su_, 32, cols)
    place_grads(who, keep, send, sd_, 64, cols)

    @pl.when(j == pl.num_programs(0) - 1)
    def _():
        part_out[...] = total_out[...].astype(BF16)
        part_ds[...] = total_ds[...].astype(BF16)


def feed(who, second, cot, gate_own, up_own, down_own, pieces, start, blocks):
    t, d = second.shape
    half = d // 2
    ff = gate_own.shape[1]
    halves = ff // 256
    left = pl.BlockSpec((half, 128), lambda j: (0, start + j))
    right = pl.BlockSpec((half, 128), lambda j: (0, halves + start + j))
    full = pl.BlockSpec((t, d), lambda j: (0, 0))
    grads = pl.BlockSpec((2, 2, 4, 96, 256), lambda j: (0, 0, 0, 0, j))
    grads_shape = sds((2, 2, 4, 96, blocks * 256), BF16)
    return call(
        feed_kernel,
        (sds((t, d), BF16), sds((t, d), BF16), grads_shape, grads_shape),
        us=1 + 4.5 * blocks,
        vmem=56,
        grid=(blocks,),
        in_specs=[
            SMEM, full, full, left, right, left, right,
            pl.BlockSpec((128, d), lambda j: (start + j, 0)),
        ]
        + [pl.BlockSpec((half // 4, 768), lambda j: (0, j))] * 4,
        out_specs=(full, full, grads, grads),
        scratch_shapes=[
            pltpu.VMEM((d, 256), BF16),
            pltpu.VMEM((d, 256), BF16),
            pltpu.VMEM((256, d), BF16),
            pltpu.VMEM((d, t), BF16),
            pltpu.VMEM((d, 256), BF16),
            pltpu.VMEM((d, 256), BF16),
            pltpu.VMEM((d, 256), BF16),
            pltpu.VMEM((t, d), F32),
            pltpu.VMEM((t, d), F32),
        ],
    )(who, second, cot, gate_own, gate_own, up_own, up_own, down_own, *pieces)


def pack_kernel(who, g0, g1, u0, u1, down, out):
    out[:, 0:128] = g0[...]
    out[:, 128:256] = g1[...]
    out[:, 256:384] = u0[...]
    out[:, 384:512] = u1[...]
    out[:, 512:768] = down[...]


def pack_feed(who, gate_own, up_own, down_own, start, blocks):
    half, ff = gate_own.shape
    halves = ff // 256
    quarter = half // 4
    left = pl.BlockSpec((quarter, 128), lambda j, w: (w[1], start + j))
    right = pl.BlockSpec((quarter, 128), lambda j, w: (w[1], halves + start + j))
    return pl.pallas_call(
        pack_kernel,
        out_shape=sds((quarter, blocks * 768), BF16),
        cost_estimate=cost(blocks),
        grid_spec=pltpu.PrefetchScalarGridSpec(
            num_scalar_prefetch=1,
            grid=(blocks,),
            in_specs=[
                left, right, left, right,
                pl.BlockSpec((128, down_own.shape[1] // 4), lambda j, w: (start + j, w[1])),
            ],
            out_specs=pl.BlockSpec((quarter, 768), lambda j, w: (0, j)),
        ),
    )(who, gate_own, gate_own, up_own, up_own, down_own)


def mixer_back_kernel(
    who, small, s0, s1, s2, hidden, cot, swish, mixed, q, pre, mcol, payload,
    own, r0, r1,
    d_hidden_out, low_out, d_swish_out, d_mixed_out, rows_out, back_out, full, d_gated,
):
    t, d = hidden.shape
    kd = HEADS * DK
    place_rows(who, full, own[...], [r0[...], r1[...]])
    values = hidden[...]
    upstream = s0[...].astype(F32) + s1[...].astype(F32) + s2[...].astype(F32)
    scale = lax.rsqrt(jnp.mean(values * values, axis=-1, keepdims=True) + EPSILON)
    rows_out[...] = jnp.zeros_like(rows_out)
    rows_out[0:1, :] = jnp.sum(upstream * values * scale, axis=0, keepdims=True)
    scaled = upstream * row_of(small, ROW_FEED)
    mean = jnp.mean(scaled * values, axis=-1, keepdims=True)
    d_hidden = cot[...].astype(F32) + scale * scaled - values * (scale * scale * scale * mean)
    d_hidden_out[...] = d_hidden
    low_out[...] = d_hidden.astype(BF16)
    d_gated[...] = nt(low_out[...], full[...])
    gain = head_gain_of(small)
    grad_heads = jnp.zeros((1, DV), F32)
    for h in range(HEADS):
        c = slice(h * DV, (h + 1) * DV)
        values = mixed[:, c]
        scale = lax.rsqrt(jnp.mean(values * values, axis=-1, keepdims=True) + HEAD_FLOOR)
        pre_gate = swish[:, c]
        sig = sigmoid(pre_gate)
        up = d_gated[:, c]
        unit = values * scale
        d_swish_out[:, c] = (up * unit * gain * sig * (1.0 + pre_gate * (1.0 - sig))).astype(BF16)
        err = up * pre_gate * sig
        grad_heads = grad_heads + jnp.sum(err * unit, axis=0, keepdims=True)
        scaled = err * gain
        mean = jnp.mean(scaled * unit, axis=-1, keepdims=True)
        d_mixed_out[:, c] = (scale * (scaled - unit * mean)).astype(BF16)
    rows_out[1:2, 0:DV] = grad_heads
    ones = lower_ones(WIDE)
    before = payload[HEADS * DV :, :].astype(F32)[0:1, 0:1]
    base = jnp.zeros((1, kd), F32)
    sums = [jnp.zeros((DV, DK), F32) for _ in range(HEADS)]
    for i in range(t // WIDE):
        rows = slice(i * WIDE, (i + 1) * WIDE)
        cumul = split_sum(ones, log_decay(pre[rows, :])) + base
        base = cumul[WIDE - 1 : WIDE, :]
        queries = q[rows, :].astype(F32)
        carried = jnp.where(mcol[rows, :] == before, queries * jnp.exp(cumul), 0.0).astype(BF16)
        for h in range(HEADS):
            sums[h] = sums[h] + tn(
                d_mixed_out[rows, h * DV : (h + 1) * DV], carried[:, h * DK : (h + 1) * DK]
            )
    for h in range(HEADS):
        back_out[h * DV : (h + 1) * DV, :] = sums[h].astype(BF16)


def mixer_back(who, small, d_second, hidden, cot, swish, mixed, q, pre, mcol, payload, own, pieces):
    t, d = hidden.shape
    vd = HEADS * DV
    whole = lambda a: pl.BlockSpec(a.shape, lambda i: (0,) * len(a.shape))
    outs = (
        sds((t, d), F32),
        sds((t, d), BF16),
        sds((t, vd), BF16),
        sds((t, vd), BF16),
        sds((8, d), F32),
        sds((HEADS * DV, DK), BF16),
    )
    ins = (small, *d_second, hidden, cot, swish, mixed, q, pre, mcol, payload, own, *pieces)
    return call(
        mixer_back_kernel,
        outs,
        grid=(1,),
        in_specs=[SMEM] + [whole(a) for a in ins],
        out_specs=tuple(whole(a) for a in outs),
        scratch_shapes=[pltpu.VMEM((vd, d), BF16), pltpu.VMEM((t, vd), F32)], us=11)(who, *ins)


def gate_grads_kernel(who, normed, d_swish, gated, low, keep, send, scratch, left_t):
    j = pl.program_id(0)
    count = d_swish.shape[1]
    half = pl.num_programs(0) // 2

    @pl.when(j == 0)
    def _():
        left_t[...] = normed[...].T

    @pl.when(j == half)
    def _():
        left_t[...] = gated[...].T

    @pl.when(j < half)
    def _():
        scratch[...] = nn(left_t[...], d_swish[...]).astype(BF16)

    @pl.when(j >= half)
    def _():
        scratch[...] = nn(left_t[...], low[...]).astype(BF16)

    place_grads(who, keep, send, scratch, 0, slice(0, 256))


def gate_grads(who, normed, d_swish, gated, low):
    t, d = normed.shape
    n = d_swish.shape[1] // 256
    const = lambda j: (0, 0)
    shape = sds((2, 2, 4, 32, 2 * n * 256), BF16)
    spec = pl.BlockSpec((2, 2, 4, 32, 256), lambda j: (0, 0, 0, 0, j))
    return call(
        gate_grads_kernel,
        (shape, shape),
        grid=(2 * n,),
        in_specs=[
            SMEM,
            pl.BlockSpec((t, d), const),
            pl.BlockSpec((t, 256), lambda j: (0, jnp.minimum(j, n - 1))),
            pl.BlockSpec((t, d), const),
            pl.BlockSpec((t, 256), lambda j: (0, jnp.maximum(j - n, 0))),
        ],
        out_specs=(spec, spec),
        scratch_shapes=[pltpu.VMEM((d, 256), BF16), pltpu.VMEM((d, t), BF16)], us=9)(who, normed, d_swish, gated, low)


def recurrence_back_kernel(
    small, q, kv, pre, d_mixed, mcol, mrow, payload, states, entering,
    d_qkv, d_pre_out, d_narrow_out, bias_out,
):
    t = pre.shape[0]
    kd = HEADS * DK
    ones = lower_ones(WIDE)
    reverse = upper_ones(WIDE)
    causal_rows = lax.broadcasted_iota(jnp.int32, (WIDE, WIDE), 0)
    causal_cols = lax.broadcasted_iota(jnp.int32, (WIDE, WIDE), 1)
    grads = [entering[h * DV : (h + 1) * DV, :].astype(F32) for h in range(HEADS)]
    bias_sum = jnp.zeros((1, kd), F32)
    for i in reversed(range(t // WIDE)):
        rows = slice(i * WIDE, (i + 1) * WIDE)
        marks = mcol[rows, :]
        last = mark_at(mrow, (i + 1) * WIDE - 1)
        if i:
            before = mark_at(mrow, i * WIDE - 1)
        else:
            before = payload[HEADS * DV :, :].astype(F32)[0:1, 0:1]
        pre_here = pre[rows, :]
        cumul = split_sum(ones, log_decay(pre_here))
        middle = cumul[SPAN - 1 : SPAN, :]
        end = cumul[WIDE - 1 : WIDE, :]
        queries = q[rows, :].astype(F32)
        keys = kv[rows, 0:kd].astype(F32)
        lift = jnp.exp(cumul - middle)
        sink = jnp.exp(middle - cumul)
        rise = jnp.where(marks == before, jnp.exp(cumul), 0.0)
        fall = jnp.where(marks == last, jnp.exp(end - cumul), 0.0)
        lifted = (queries * lift).astype(BF16)
        lowered = (keys * sink).astype(BF16)
        carried = (queries * rise).astype(BF16)
        tail = (keys * fall).astype(BF16)
        keep = jnp.where(before == last, jnp.exp(end), 0.0)
        causal = (causal_rows >= causal_cols) & (marks == mrow[0:1, rows])
        slopes = []
        ends = []
        for h in range(HEADS):
            c = slice(h * DK, (h + 1) * DK)
            values = kv[rows, kd + h * DV : kd + (h + 1) * DV]
            up = d_mixed[rows, h * DV : (h + 1) * DV]
            state = states[i, h]
            grad = grads[h]
            low_grad = grad.astype(BF16)
            scores = jnp.where(causal, nt(lifted[:, c], lowered[:, c]), 0.0).astype(BF16)
            d_scores = jnp.where(causal, nt(up, values), 0.0).astype(BF16)
            d_lifted = nn(d_scores, lowered[:, c])
            d_lowered = tn(d_scores, lifted[:, c])
            d_carried = nn(up, state)
            d_tail = nn(values, low_grad)
            d_values = tn(scores, up) + nt(tail[:, c], low_grad)
            d_qkv[rows, c] = (d_lifted * lift[:, c] + d_carried * rise[:, c]).astype(BF16)
            d_qkv[rows, kd + h * DK : kd + (h + 1) * DK] = (
                d_lowered * sink[:, c] + d_tail * fall[:, c]
            ).astype(BF16)
            d_qkv[rows, 2 * kd + h * DV : 2 * kd + (h + 1) * DV] = d_values.astype(BF16)
            tail_term = tail[:, c].astype(F32) * d_tail
            slopes.append(
                lifted[:, c].astype(F32) * d_lifted
                - lowered[:, c].astype(F32) * d_lowered
                + carried[:, c].astype(F32) * d_carried
                - tail_term
            )
            kept = keep[:, c] * grad
            ends.append(
                jnp.sum(tail_term, axis=0, keepdims=True)
                + jnp.sum(kept * state.astype(F32), axis=0, keepdims=True)
            )
            grads[h] = kept + tn(up, carried[:, c])
        d_decay = split_sum(reverse, jnp.concatenate(slopes, axis=1)) + jnp.concatenate(ends, axis=1)
        d_pre = d_decay * sigmoid(-pre_here) / GATE_NORM
        bias_sum = bias_sum + jnp.sum(d_pre, axis=0, keepdims=True)
        d_pre_out[rows, :] = d_pre.astype(BF16)
    bias_out[...] = jnp.broadcast_to(bias_sum, bias_out.shape)
    d_narrow_out[...] = nt(d_pre_out[...], expand_of(small)).astype(BF16)


def recurrence_back(small, q, kv, pre, d_mixed, mcol, mrow, payload, states, entering):
    t = q.shape[0]
    width = q.shape[1] + kv.shape[1]
    return call(
        recurrence_back_kernel,
        (
            sds((t, width), BF16),
            sds(pre.shape, BF16),
            sds((t, 16), BF16),
            sds((8, HEADS * DK), F32),
        ), us=11)(small, q, kv, pre, d_mixed, mcol, mrow, payload, states, entering)


def input_back_kernel(
    who, x, small, d_hidden, d_qkv, d_swish, d_narrow, q_own, k_own, v_own, s_own,
    a0, a1, a2, a3, b0, b1, b2, b3, grad_input, mixer_out, total, full,
):
    j = pl.program_id(0)
    steps = pl.num_programs(0)

    @pl.when(j == 0)
    def _():
        total[...] = nn(d_narrow[...], small[0:ROW_EXPAND, :])

    first = [r[...] for r in (a0, a1, a2, a3)]
    other = [r[...] for r in (b0, b1, b2, b3)]

    @pl.when(j < 2)
    def _():
        place_rows(who, full, q_own[...], other)

    @pl.when((j >= 2) & (j < 4))
    def _():
        place_rows(who, full, k_own[...], first)

    @pl.when((j >= 4) & (j < 8))
    def _():
        place_rows(who, full, v_own[...], first)

    @pl.when(j >= 8)
    def _():
        place_rows(who, full, s_own[...], other)

    @pl.when(j < 8)
    def _():
        total[...] += nt(d_qkv[...], full[...])

    @pl.when(j >= 8)
    def _():
        total[...] += nt(d_swish[...], full[...])

    @pl.when(j == steps - 1)
    def _():
        values = x[...].astype(F32)
        upstream = total[...]
        scale = lax.rsqrt(jnp.mean(values * values, axis=-1, keepdims=True) + EPSILON)
        unit = values * scale
        mixer_out[...] = jnp.broadcast_to(
            jnp.sum(upstream * unit, axis=0, keepdims=True), mixer_out.shape
        )
        scaled = upstream * row_of(small, ROW_MIXER)
        mean = jnp.mean(scaled * unit, axis=-1, keepdims=True)
        grad_input[...] = (d_hidden[...] + scale * (scaled - unit * mean)).astype(BF16)


def input_back(who, x, small, d_hidden, d_qkv, d_swish, d_narrow, owns, pieces, gate_pieces):
    t, d = x.shape
    half = d // 2
    kd = HEADS * DK
    vd = HEADS * DV
    qn = kd // 256
    vn = vd // 256
    wn = 2 * qn + vn
    const = lambda j: (0, 0)
    beyond = lambda j: (0, jnp.where(j < wn, jnp.minimum(j, qn - 1), j - wn + qn))
    col = lambda low, count: (lambda j: (0, jnp.clip(j - low, 0, count - 1)))
    return call(
        input_back_kernel,
        (sds((t, d), BF16), sds((8, d), F32)),
        grid=(wn + vn,),
        in_specs=[
            SMEM,
            pl.BlockSpec((t, d), const),
            pl.BlockSpec(small.shape, const),
            pl.BlockSpec((t, d), const),
            pl.BlockSpec((t, 256), col(0, wn)),
            pl.BlockSpec((t, 256), col(wn, vn)),
            pl.BlockSpec((t, 16), const),
            pl.BlockSpec((half, 256), col(0, qn)),
            pl.BlockSpec((half, 256), col(qn, qn)),
            pl.BlockSpec((half, 256), col(2 * qn, vn)),
            pl.BlockSpec((half, 256), col(wn, vn)),
        ]
        + [pl.BlockSpec((half // 4, 256), col(qn, qn + vn))] * 4
        + [pl.BlockSpec((half // 4, 256), beyond)] * 4,
        out_specs=(pl.BlockSpec((t, d), const), pl.BlockSpec((8, d), const)),
        scratch_shapes=[pltpu.VMEM((t, d), F32), pltpu.VMEM((d, 256), BF16)], us=15)(who, x, small, d_hidden, d_qkv, d_swish, d_narrow, *owns, *pieces, *gate_pieces)


def late_grads_kernel(
    who, normed, d_qkv, d_narrow, narrow, d_pre, rows_in, bias_in, mixer_in,
    keep, send, scratch, strip, left_t, rows,
):
    t, d = normed.shape
    half = d // 2
    kd = HEADS * DK
    n = d_qkv.shape[1] // 256
    left_t[...] = normed[...].T
    for j in range(n):
        c = slice(j * 256, (j + 1) * 256)
        scratch[...] = nn(left_t[...], d_qkv[:, c]).astype(BF16)
        place_grads(who, keep, send, scratch, 0, c)
    rows[...] = jnp.zeros_like(rows)
    rows[LANE_FEED : LANE_FEED + 1, :] = rows_in[0:1, :]
    rows[LANE_MIXER : LANE_MIXER + 1, :] = mixer_in[0:1, :]
    part = kd // 2
    rows[LANE_BIAS : LANE_BIAS + 1, 0:part] = bias_in[0:1, 0:part]
    rows[LANE_BIAS : LANE_BIAS + 1, half : half + part] = bias_in[0:1, part:kd]
    part = DV // 2
    rows[LANE_HEADS : LANE_HEADS + 1, 0:part] = rows_in[1:2, 0:part]
    rows[LANE_HEADS : LANE_HEADS + 1, half : half + part] = rows_in[1:2, part:DV]
    columns = rows[...].T
    squeeze = nn(left_t[...], d_narrow[...])
    expand = tn(d_pre[...], narrow[...])
    part = kd // 2
    strip[...] = columns.astype(BF16)
    strip[:, 0:16] = squeeze.astype(BF16)
    strip[0:part, LANE_EXPAND : LANE_EXPAND + 16] = expand[0:part].astype(BF16)
    strip[half : half + part, LANE_EXPAND : LANE_EXPAND + 16] = expand[part:kd].astype(BF16)
    place_grads(who, keep, send, strip, 0, slice(n * 256, n * 256 + 128))


def late_grads(who, normed, d_qkv, d_narrow, narrow, d_pre, rows_in, bias_in, mixer_in):
    t, d = normed.shape
    shape = sds((2, 2, 4, 32, d_qkv.shape[1] + 128), BF16)
    whole = lambda a: pl.BlockSpec(a.shape, lambda i: (0,) * len(a.shape))
    ins = (normed, d_qkv, d_narrow, narrow, d_pre, rows_in, bias_in, mixer_in)
    return call(
        late_grads_kernel,
        (shape, shape),
        us=10,
        grid=(1,),
        in_specs=[SMEM] + [whole(a) for a in ins],
        out_specs=(whole(shape), whole(shape)),
        scratch_shapes=[
            pltpu.VMEM((d, 256), BF16),
            pltpu.VMEM((d, 128), BF16),
            pltpu.VMEM((d, t), BF16),
            pltpu.VMEM((128, d), F32),
        ],
    )(who, *ins)


def settle_kernel(who, a, b, c, d, *outs):
    me = who[2]
    for k, part in enumerate((a, b, c, d)):
        for zz in range(4):
            rows = pl.ds(pl.multiple_of((me ^ (k * 4 + zz)) * 32, 32), 32)
            at = 0
            for out in outs:
                count = out.shape[1]
                out[rows, :] = part[zz, :, at : at + count].astype(F32)
                at += count


def settle(who, parts, half, widths):
    shapes = tuple(sds((half, width), F32) for width in widths)
    return call(settle_kernel, shapes, us=4, in_specs=[SMEM] + [VMEM] * 4)(who, *parts)


def feed_settle_kernel(who, a, b, c, d, *rest, first):
    gate, up, down = rest if first else rest[3:]
    h = pl.program_id(1)
    me = who[2]
    for k, part in enumerate((a, b, c, d)):
        for zz in range(4):
            block = me ^ (k * 4 + zz)
            rows = pl.ds(pl.multiple_of(block * 32, 32), 32)
            gate[rows, :] = part[zz, 0:32, :].astype(F32)
            up[rows, :] = part[zz, 32:64, :].astype(F32)
            at = pl.ds(pl.multiple_of((block % 4) * 32, 32), 32)
            cols = pl.ds(pl.multiple_of((block // 4) * 256 + h * 128, 128), 128)
            down[at, cols] = part[zz, 64:96, :].astype(F32)


def feed_settle(who, parts, before, start, blocks, half, ff, d):
    halves = ff // 256
    first = before is None
    shapes = (sds((half, ff), F32), sds((half, ff), F32), sds((ff // 2, d), F32))
    wide = pl.BlockSpec((half, 128), lambda j, h: (0, h * halves + start + j))
    tall = pl.BlockSpec((128, d), lambda j, h: (start + j, 0))
    any_spec = pl.BlockSpec(memory_space=pl.ANY)
    return call(
        functools.partial(feed_settle_kernel, first=first),
        shapes,
        us=2 * blocks,
        grid=(blocks, 2),
        in_specs=[SMEM]
        + [pl.BlockSpec((4, 96, 128), lambda j, h: (0, 0, 2 * j + h))] * 4
        + ([] if first else [any_spec] * 3),
        out_specs=(wide, wide, tall),
        input_output_aliases={} if first else {5: 0, 6: 1, 7: 2},
    )(who, *parts, *(() if first else before))


def added(*terms):
    total = terms[0].astype(F32)
    for term in terms[1:]:
        total = total + term.astype(F32)
    return total.astype(BF16)


def summed(first, *rest):
    for term in rest:
        first = first + term.astype(F32)
    return first.astype(BF16)


def swap(v, bit):
    count = lax.axis_size("replica")
    return lax.ppermute(v, "replica", [(i, i ^ bit) for i in range(count)])


def cross(v):
    return lax.ppermute(v, "fsdp", [(0, 1), (1, 0)])


def tied(v, *after):
    return lax.optimization_barrier((v,) + after)[0]


def fenced(go, *jobs):
    work = lambda: tuple(job() for job in jobs)
    shapes = jax.eval_shape(work)
    blank = lambda: jax.tree.map(lambda a: jnp.zeros(a.shape, a.dtype), shapes)
    return lax.cond(go, work, blank)


class Part:
    def __init__(self, keep, got):
        self.keep = keep
        self.got = got


class Chain:
    def __init__(self, *parts):
        self.parts = parts

    def blocks(self, y, k, *more):
        at, sums = 0, []
        for part in self.parts:
            width = part.keep.shape[-1]
            cut = [a[..., at : at + width] for a in more]
            sums.append(added(part.keep[0, y, k], part.got[0, y, k], part.over[y, k], *cut))
            at += width
        return sums[0] if len(sums) == 1 else jnp.concatenate(sums, axis=-1)

    def to_y(self, now):
        last = self.parts[-1]
        last.over = tied(last.over, now)
        return self.blocks(1, slice(None))

    def to_near(self, now):
        side = tied(self.side, now)
        odd = slice(1, 4, 2)
        return self.blocks(0, odd, side[odd])

    def to_far(self, now):
        return self.blocks(0, 2, self.side[2], tied(self.near, now)[1])

    def own_of_far(self, now):
        self.own = self.blocks(0, 0, self.side[0], self.near[0], tied(self.far, now))
        return self.own

    def back_near(self, now):
        self.pair = jnp.stack([self.own, tied(self.far, now)])
        return self.pair

    def back_y(self, now):
        near = tied(self.near, now)
        self.line = jnp.stack([self.pair[0], near[0], self.pair[1], near[1]])
        return self.line

    def gathered(self, now):
        beside = tied(self.beside, now)
        return (self.line, beside, swap(self.line, 1), swap(beside, 1))


def over_core(keep, send):
    got = swap(send, 1)
    return got, added(keep[1], got[1])


def natural(keep, send):
    both = jnp.stack([keep, send])
    both = jnp.moveaxis(both, 0, 1)
    return both.reshape((2, 16) + keep.shape[3:])


def total_over(v, dim):
    v = lax.psum_scatter(v.astype(BF16), "fsdp", scatter_dimension=dim, tiled=True)
    return lax.psum(v, "replica").astype(F32)


def chain_join(earlier, later):
    factor_early, state_early, first_early, last_early = earlier
    factor_late, state_late, first_late, last_late = later
    joined = (first_late == last_early) | (last_early < 0) | (first_late < 0)
    linked = jnp.where(joined, factor_late, 0.0)
    return (
        linked * factor_early,
        linked[:, None] * state_early + state_late,
        jnp.where(first_early < 0, first_late, first_early),
        jnp.where(last_late < 0, last_early, last_late),
    )


def chained(payload, passing, first_mark):
    place = lax.axis_index("fsdp")
    own = (
        passing[0].reshape(HEADS, DK).astype(BF16),
        payload,
        first_mark.astype(BF16),
    )
    factors, payloads, firsts = [lax.all_gather(a, "fsdp") for a in own]
    rows = HEADS * DV

    def one(turn, carry):
        pick = lambda a: lax.dynamic_index_in_dim(a, turn, 0, False).astype(F32)
        factor, block, first = pick(factors), pick(payloads), pick(firsts)
        later = (factor, block[:rows].reshape(HEADS, DV, DK), first, block[rows, :1])
        earlier_factor, state, earlier_first, earlier_last = carry
        joined = (later[2] == earlier_last) | (earlier_last < 0)
        linked = jnp.where(joined, later[0], 0.0)
        return (
            linked * earlier_factor,
            linked[:, None, :] * state + later[1],
            jnp.where(earlier_first < 0, later[2], earlier_first),
            later[3],
        )

    none = -jnp.ones((1,), F32)
    start = (jnp.ones((HEADS, DK), F32), jnp.zeros((HEADS, DV, DK), F32), none, none)
    done = lax.fori_loop(0, place, one, start)
    marks = jnp.broadcast_to(done[3][:, None], (16, DK))
    return jnp.concatenate([done[1].reshape(rows, DK), marks]).astype(BF16)


def chained_back(back, passing, linked):
    count = lax.axis_size("fsdp")
    ahead = count - 1 - lax.axis_index("fsdp")
    factor = jnp.where(linked, passing[0], 0.0).reshape(HEADS, DK).astype(BF16)
    factors, backs = [lax.all_gather(a, "fsdp") for a in (factor, back)]

    def one(turn, grad):
        source = count - 1 - turn
        pick = lambda a: lax.dynamic_index_in_dim(a, source, 0, False).astype(F32)
        return pick(backs).reshape(HEADS, DV, DK) + pick(factors)[:, None, :] * grad

    grad = lax.fori_loop(0, ahead, one, jnp.zeros((HEADS, DV, DK), F32))
    return grad.reshape(HEADS * DV, DK).astype(BF16)


def on_device(
    inputs, segments, cotangent, mixer_gain, query_map, key_map, value_map, swish_map, squeeze,
    expand, forget_bias, head_gain, readout, feed_gain, gate_map, up_map, down_map,
):
    shards = lax.axis_size("fsdp")
    copies = lax.axis_size("replica")
    paired = shards == 2 and copies == 16
    t, d = inputs.shape
    kd, vd = HEADS * DK, HEADS * DV
    half = d // 2
    quarter = half // 4
    marks = segments[0].astype(F32)
    mcol, mrow = marks[:, None], marks[None, :]

    if paired:
        place = lax.axis_index("replica")
        core, side, deep = place % 2, (place // 2) % 2, place // 4
        x = lax.axis_index("fsdp")
        q = side * 2 + core
        who = jnp.stack([x, q, core * 8 + side * 4 + deep]).astype(jnp.int32)
    else:
        who = jnp.zeros((3,), jnp.int32)
        x = q = 0
        gather = lambda a, dim=0: lax.all_gather(a, "fsdp", axis=dim, tiled=True)
        query_map, key_map, value_map, swish_map, readout, gate_map, up_map, down_map = [
            gather(a)
            for a in (query_map, key_map, value_map, swish_map, readout, gate_map, up_map, down_map)
        ]
        mixer_gain, feed_gain, forget_bias, head_gain, squeeze = [
            gather(a) for a in (mixer_gain, feed_gain, forget_bias, head_gain, squeeze)
        ]
        expand = gather(expand, 1)

    def small_half(k):
        cut = lambda a, dim=0: lax.slice_in_dim(a, k * (a.shape[dim] // 2), (k + 1) * (a.shape[dim] // 2), axis=dim)
        return packed(cut(squeeze), cut(expand, 1), cut(mixer_gain), cut(feed_gain), cut(forget_bias), cut(head_gain))

    def packed(squeeze, expand, mixer_gain, feed_gain, forget_bias, head_gain):
        wide = lambda a: jnp.pad(a, ((0, 0), (0, half - a.shape[1])))
        mixed = jnp.concatenate([forget_bias, head_gain])[None]
        rows = [squeeze.T, wide(expand), mixer_gain[None], feed_gain[None], wide(mixed)]
        block = jnp.concatenate(rows)
        return jnp.pad(block, ((0, SMALL_ROWS - block.shape[0]), (0, 0)))

    ff = gate_map.shape[1]
    halves = ff // 256
    counts = chunk_blocks(halves)
    starts = [sum(counts[:i]) for i in range(len(counts))]

    def quarter_rows(a, k):
        return lax.dynamic_slice_in_dim(a, k * quarter, quarter, 0)

    if paired:
        return paired_device(
            who, x, q, mcol, mrow, inputs, cotangent, query_map, key_map, value_map, swish_map,
            readout, gate_map, up_map, down_map,
            packed(squeeze, expand, mixer_gain, feed_gain, forget_bias, head_gain),
            starts, counts,
        )
    small = jnp.concatenate([small_half(0), small_half(1)], axis=1)
    lower = lambda a: a[: a.shape[0] // 2]
    upper = lambda a: a[a.shape[0] // 2 :]
    share = lambda maps: tuple(
        jnp.concatenate([quarter_rows(upper(a), k) for a in maps], axis=1) for k in range(4)
    )
    kv_pieces = share((key_map, value_map))
    gate_pieces = share((query_map, swish_map))
    read_pieces = (upper(readout)[: half // 2], upper(readout)[half // 2 :])
    others = (upper(gate_map), upper(up_map), upper(down_map))
    feed_pieces = [
        tuple(
            pack_feed(jnp.full((3,), k, jnp.int32), *others, s, n) for k in range(4)
        )
        for s, n in zip(starts, counts)
    ]
    query_map, key_map, value_map, swish_map, readout, gate_map, up_map, down_map = [
        lower(a)
        for a in (query_map, key_map, value_map, swish_map, readout, gate_map, up_map, down_map)
    ]

    normed, kv, pre, narrow = project(who, inputs, small, key_map, value_map, kv_pieces)
    local, passing = local_state(kv, pre, mcol, mrow)
    payload = chained(local, passing, marks[:1])
    queries, swish = swish_project(who, normed, query_map, swish_map, gate_pieces)
    mixed, states, gated = mixer(small, queries, kv, pre, swish, mcol, mrow, payload)
    hidden, second = reader(who, inputs, small, gated, readout, read_pieces)

    feed_grads, out_parts, second_parts = [], [], []
    for s, n, pieces in zip(starts, counts, feed_pieces):
        out_part, second_part, keep, send = feed(
            who, second, cotangent, gate_map, up_map, down_map, pieces, s, n
        )
        out_parts.append(out_part)
        second_parts.append(second_part)
        feed_grads.append((keep, send))
    output = summed(hidden, *out_parts)

    d_hidden, low, d_swish, d_mixed, rows, back = mixer_back(
        who, small, second_parts, hidden, cotangent, swish, mixed, queries, pre, mcol, payload,
        readout, read_pieces,
    )
    linked = marks[0] == payload[HEADS * DV, 0].astype(F32)
    entering = chained_back(back, passing, linked)
    gate_grad = gate_grads(who, normed, d_swish, gated, low)
    d_qkv, d_pre, d_narrow, bias_row = recurrence_back(
        small, queries, kv, pre, d_mixed, mcol, mrow, payload, states, entering
    )
    grad_input, mixer_row = input_back(
        who, inputs, small, d_hidden, d_qkv, d_swish, d_narrow,
        (query_map, key_map, value_map, swish_map), kv_pieces, gate_pieces,
    )
    late_grad = late_grads(
        who, normed, d_qkv, d_narrow, narrow, d_pre, rows, bias_row, mixer_row
    )

    gates, ups, downs = [], [], []
    for (keep, send), n in zip(feed_grads, counts):
        block = natural(keep, send)
        sides = lambda k: block[:, :, 32 * k : 32 * (k + 1), :].reshape(d, n, 2, 128)
        gates.append(sides(0))
        ups.append(sides(1))
        part = block[:, :, 64:96, :].reshape(2, 4, 128, n, 256)
        downs.append(part.transpose(0, 3, 2, 1, 4).reshape(2, n * 128, d))
    whole = lambda parts: jnp.concatenate(parts, axis=1).transpose(0, 2, 1, 3).reshape(d, ff)
    grad_gate, grad_up = whole(gates), whole(ups)
    grad_down = jnp.concatenate(downs, axis=1).reshape(ff, d)
    flat = lambda pair: natural(*pair).reshape(d, -1)
    gate_flat, late_flat = flat(gate_grad), flat(late_grad)
    strip = late_flat[:, 2 * kd + vd :]
    joined = lambda lane, count: jnp.concatenate(
        [strip[:count, lane], strip[half : half + count, lane]]
    )
    part = kd // 2
    grad_expand = jnp.concatenate([strip[:part, 16:32], strip[half : half + part, 16:32]]).T
    results = (
        joined(LANE_MIXER, half), late_flat[:, :kd], late_flat[:, kd : 2 * kd],
        late_flat[:, 2 * kd : 2 * kd + vd],
        gate_flat[:, :vd], strip[:, :16], grad_expand, joined(LANE_BIAS, part),
        joined(LANE_HEADS, DV // 2), gate_flat[:, vd:], joined(LANE_FEED, half),
        grad_gate, grad_up, grad_down,
    )
    return (output, grad_input) + tuple(
        total_over(a, 1 if i == 6 else 0) for i, a in enumerate(results)
    )


def paired_device(
    who, x, q, mcol, mrow, inputs, cotangent, query_map, key_map, value_map, swish_map,
    readout, gate_map, up_map, down_map, small_own, starts, counts,
):
    t, d = inputs.shape
    half = d // 2
    quarter = half // 4
    kd = HEADS * DK
    ff = gate_map.shape[1]

    def share(maps):
        cut = lambda a: lax.dynamic_slice_in_dim(a, q * quarter, quarter, 0)
        return jnp.concatenate([cut(a) for a in maps], axis=1)

    def spread(first, *after):
        second = swap(first, 2)
        return (first, swap(first, 1), second, swap(second, 1))

    go = x < 2
    vd = HEADS * DV

    def together(*values):
        return lax.optimization_barrier(values)

    def core_step(grads, *after):
        keep, send = grads
        ((got, out),) = fenced(tied(go, send, *after), lambda: over_core(keep, send))
        return Part(keep, got), out

    small_other = cross(small_own)
    kv_share = share((key_map, value_map))
    kv_first = cross(kv_share)
    gate_share = share((tied(query_map, kv_share), swish_map))
    read_share = lax.dynamic_slice_in_dim(tied(readout, kv_share), (q % 2) * (half // 2), half // 2, 0)
    def pack(i, *after):
        return pack_feed(tied(who, *after), gate_map, up_map, down_map, starts[i], counts[i])

    feed_shares = [pack(0, gate_share, read_share)]
    kv_first, small_other, gate_share, read_share, feed_shares[0] = together(
        kv_first, small_other, gate_share, read_share, feed_shares[0]
    )
    kv_second, kv_third = swap(kv_first, 2), swap(kv_first, 1)
    gate_first = cross(gate_share)
    small = jnp.concatenate(
        [jnp.where(x == 0, small_own, small_other), jnp.where(x == 0, small_other, small_own)],
        axis=1,
    )
    feed_shares += [pack(1, kv_first), pack(2, kv_first)]
    gate_first, kv_second, kv_third, *feed_shares = together(
        gate_first, kv_second, kv_third, *feed_shares
    )
    kv_pieces = (kv_first, kv_third, kv_second, swap(kv_second, 1))
    gate_second, gate_third = swap(gate_first, 2), swap(gate_first, 1)
    f0_first = cross(tied(feed_shares[0], gate_first))
    normed, kv, pre, narrow = project(
        tied(who, gate_first), inputs, small, key_map, value_map, kv_pieces
    )
    gate_second, f0_first, normed = together(gate_second, f0_first, normed)
    gate_fourth = swap(gate_second, 1)
    gate_pieces = (gate_first, gate_third, gate_second, gate_fourth)
    f0_third = swap(f0_first, 1)
    read_first = cross(tied(read_share, f0_first))
    local, _ = local_state(kv, pre, mcol, tied(mrow, normed))
    payload, (queries, swish), f0_second = fenced(
        tied(go, local, gate_fourth, f0_third),
        lambda: lax.ppermute(local, "fsdp", [(0, 1)]),
        lambda: swish_project(who, normed, query_map, swish_map, gate_pieces),
        lambda: swap(f0_first, 2),
    )
    read_first, swish = together(read_first, swish)
    read_pieces = (read_first, swap(read_first, 1))
    f0_pieces = (f0_first, f0_third, f0_second, swap(f0_second, 1))
    f1_first = cross(tied(feed_shares[1], read_first))
    mixed, states, gated = mixer(
        tied(small, swish), queries, kv, pre, swish, mcol, mrow, payload
    )
    hidden, second = reader(tied(who, gated, f0_pieces[3]), inputs, small, gated, readout, read_pieces)
    f1_first, hidden = together(f1_first, hidden)
    f1_second, f1_third = swap(f1_first, 2), swap(f1_first, 1)
    f2_first = cross(tied(feed_shares[2], f1_first))

    def feed_part(i, pieces, *after):
        out_part, second_part, keep, send = feed(
            tied(who, *after), second, cotangent, gate_map, up_map, down_map, pieces, starts[i],
            counts[i],
        )
        out_parts.append(out_part)
        second_parts.append(second_part)
        return keep, send

    out_parts, second_parts = [], []
    grads = feed_part(0, f0_pieces, hidden, f1_first)
    part0, out = core_step(grads, f1_third)
    f2_first, f1_second, out = together(f2_first, f1_second, out)
    part0.over = cross(out)
    f1_pieces = (f1_first, f1_third, f1_second, swap(f1_second, 1))
    f2_second, f2_third = swap(f2_first, 2), swap(f2_first, 1)
    grads = feed_part(1, f1_pieces, out)
    part1, out = core_step(grads, f2_second, f2_third)
    f0, f1 = Chain(part0), Chain(part1)
    a = f0.to_y(out)
    a, out = together(a, out)
    part1.over = cross(out)
    f0.side = swap(a, 2)
    f2_pieces = (f2_first, f2_third, f2_second, swap(tied(f2_second, a), 1))
    keep, send = feed_part(2, f2_pieces, a)
    a = f0.to_near(keep)
    f0.near = swap(a, 4)
    back_parts, (got, f2_out) = fenced(
        tied(go, a),
        lambda: mixer_back(
            who, small, second_parts, hidden, cotangent, swish, mixed, queries, pre, mcol,
            payload, readout, read_pieces,
        ),
        lambda: over_core(keep, send),
    )
    d_hidden, low, d_swish, d_mixed, rows, back = back_parts
    part2 = Part(keep, got)
    f2 = Chain(part2)
    a, b = f0.to_far(back), f1.to_y(back)
    a, b, back, f2_out = together(a, b, back, f2_out)
    part2.over = cross(f2_out)
    entering = lax.ppermute(back, "fsdp", [(1, 0)])
    f0.far = swap(a, 8)
    f1.side = swap(b, 2)
    keep, send = gate_grads(tied(who, a), normed, d_swish, gated, low)
    a = f0.own_of_far(keep)
    a, entering = together(a, entering)
    f0.far = swap(a, 8)
    (d_qkv, d_pre, d_narrow, bias_row), (got, g_out) = fenced(
        tied(go, a),
        lambda: recurrence_back(
            small, queries, kv, pre, d_mixed, mcol, mrow, payload, states, entering
        ),
        lambda: over_core(keep, send),
    )
    part_g = Part(keep, got)
    g = Chain(part_g)
    a, b = f0.back_near(d_qkv), f1.to_near(d_qkv)
    a, b, g_out = together(a, b, g_out)
    part_g.over = cross(g_out)
    f0.near, f1.near = swap(a, 4), swap(b, 4)
    grad_input, mixer_row = input_back(
        tied(who, a), inputs, small, d_hidden, d_qkv, d_swish, d_narrow,
        (query_map, key_map, value_map, swish_map), kv_pieces, gate_pieces,
    )
    a, b, c = f0.back_y(mixer_row), f1.to_far(mixer_row), f2.to_y(mixer_row)
    a, b, c = together(a, b, c)
    f2.side, f1.far, a0 = swap(c, 2), swap(b, 8), a
    grads = late_grads(
        tied(who, a), normed, d_qkv, d_narrow, narrow, d_pre, rows, bias_row, mixer_row
    )
    a = f1.own_of_far(grads[0])
    part_v, v_out = core_step(grads, a)
    v = Chain(part_v)
    a, line0, v_out = together(a, a0, v_out)
    f1.far = swap(a, 8)
    part_v.over = cross(v_out)
    now = f2.to_near(v_out)
    f2.near = swap(now, 4)
    now = g.to_y(now)
    g.side = swap(now, 2)
    now = f1.back_near(now)
    f1.near = swap(now, 4)
    f0.beside = swap(tied(line0, now), 2)
    now = f2.to_far(now)
    f2.far = swap(now, 8)
    output = summed(tied(hidden, now), *out_parts)
    now = v.to_y(output)
    v.side = swap(now, 2)
    now = f2.own_of_far(now)
    f2.far = swap(now, 8)
    now = g.to_near(now)
    g.near = swap(now, 4)
    now = f1.back_y(now)
    f1.beside = swap(now, 2)
    f0_parts = f0.gathered(now)
    feeds = feed_settle(tied(who, now), f0_parts, None, starts[0], counts[0], half, ff, d)
    now = f2.back_near(feeds[0])
    f2.near = swap(now, 4)
    now = g.to_far(now)
    g.far = swap(now, 8)
    now = v.to_near(now)
    v.near = swap(now, 4)
    now = f2.back_y(now)
    f2.beside = swap(now, 2)
    now = g.own_of_far(now)
    g.far = swap(now, 8)
    now = v.to_far(now)
    v.far = swap(now, 8)
    f1_parts = f1.gathered(now)
    now = g.back_near(now)
    g.near = swap(now, 4)
    now = v.own_of_far(now)
    v.far = swap(now, 8)
    feeds = feed_settle(tied(who, now), f1_parts, feeds, starts[1], counts[1], half, ff, d)
    now = v.back_near(feeds[0])
    v.near = swap(now, 4)
    now = g.back_y(now)
    g.beside = swap(now, 2)
    now = v.back_y(now)
    v.beside = swap(now, 2)
    f2_parts = f2.gathered(now)
    feeds = feed_settle(tied(who, now), f2_parts, feeds, starts[2], counts[2], half, ff, d)
    g_parts = g.gathered(feeds[0])
    v_parts = v.gathered(feeds[0])
    grad_swish, grad_readout = settle(tied(who, feeds[0]), g_parts, half, (vd, vd))
    grad_query, grad_key, grad_value, strip = settle(
        tied(who, grad_swish), v_parts, half, (kd, kd, vd, 128)
    )
    grad_gate, grad_up, grad_down = feeds
    return (
        output, grad_input, strip[:, LANE_MIXER], grad_query, grad_key, grad_value, grad_swish,
        strip[:, :16], strip[: kd // 2, LANE_EXPAND : LANE_EXPAND + 16].T,
        strip[: kd // 2, LANE_BIAS], strip[: DV // 2, LANE_HEADS], grad_readout,
        strip[:, LANE_FEED], grad_gate, grad_up, grad_down,
    )


def chunk_blocks(halves):
    parts = 3
    base, extra = divmod(halves, parts)
    return [base + (1 if i >= parts - extra else 0) for i in range(parts)]


def solution(mesh):
    placed = (
        P(("replica", "fsdp"), None),
        P("replica", "fsdp"),
        P(("replica", "fsdp"), None),
        P("fsdp"),
        P("fsdp", None),
        P("fsdp", None),
        P("fsdp", None),
        P("fsdp", None),
        P("fsdp", None),
        P(None, "fsdp"),
        P("fsdp"),
        P("fsdp"),
        P("fsdp", None),
        P("fsdp"),
        P("fsdp", None),
        P("fsdp", None),
        P("fsdp", None),
    )
    return jax.shard_map(
        on_device,
        mesh=mesh,
        in_specs=placed,
        out_specs=(
            P(("replica", "fsdp"), None),
            P(("replica", "fsdp"), None),
            P("fsdp"),
            P("fsdp", None),
            P("fsdp", None),
            P("fsdp", None),
            P("fsdp", None),
            P("fsdp", None),
            P(None, "fsdp"),
            P("fsdp"),
            P("fsdp"),
            P("fsdp", None),
            P("fsdp"),
            P("fsdp", None),
            P("fsdp", None),
            P("fsdp", None),
        ),
        check_vma=False,
    )
```

```python
import functools

import jax
import jax.numpy as jnp
from jax import lax
from jax.experimental import pallas as pl
from jax.experimental.pallas import tpu as pltpu
from jax.sharding import PartitionSpec as P

HEADS = 4
DK = 128
DV = 256
SPAN = 64
WIDE = 2 * SPAN

EPSILON = 1e-06
HEAD_FLOOR = 16.0
GATE_NORM = 16.0

F32 = jnp.float32
BF16 = jnp.bfloat16
MIB = 1024 * 1024

ROW_EXPAND = 16
ROW_MIXER = 32
ROW_FEED = 33
ROW_MIXED = 34
SMALL_ROWS = 48
LANE_EXPAND = 16
LANE_FEED = 32
LANE_BIAS = 33
LANE_HEADS = 34
LANE_MIXER = 35


def nn(a, b):
    return lax.dot_general(a, b, (((1,), (0,)), ((), ())), preferred_element_type=F32)


def nt(a, b):
    return lax.dot_general(a, b, (((1,), (1,)), ((), ())), preferred_element_type=F32)


def tn(a, b):
    return lax.dot_general(a, b, (((0,), (0,)), ((), ())), preferred_element_type=F32)


def sigmoid(v):
    return 1.0 / (1.0 + jnp.exp(-v))


def cost(us):
    return pl.CostEstimate(
        flops=int(us * 1e7), bytes_accessed=int(us * 3.6e4), transcendentals=0
    )


def call(kernel, out_shape, us=5, vmem=30, **kw):
    return pl.pallas_call(
        kernel,
        out_shape=out_shape,
        cost_estimate=cost(us),
        compiler_params=pltpu.CompilerParams(vmem_limit_bytes=vmem * MIB),
        **kw,
    )


def sds(shape, dtype):
    return jax.ShapeDtypeStruct(shape, dtype)


SMEM = pl.BlockSpec(memory_space=pltpu.SMEM)
VMEM = pl.BlockSpec(memory_space=pltpu.VMEM)


def split_sum(ones, values):
    high = values.astype(BF16)
    rest = values - high.astype(F32)
    middle = rest.astype(BF16)
    low = (rest - middle.astype(F32)).astype(BF16)
    return nn(ones, high) + nn(ones, middle) + nn(ones, low)


def lower_ones(size):
    rows = lax.broadcasted_iota(jnp.int32, (size, size), 0)
    cols = lax.broadcasted_iota(jnp.int32, (size, size), 1)
    return (rows >= cols).astype(F32).astype(BF16)


def upper_ones(size):
    rows = lax.broadcasted_iota(jnp.int32, (size, size), 0)
    cols = lax.broadcasted_iota(jnp.int32, (size, size), 1)
    return (rows <= cols).astype(F32).astype(BF16)


def log_decay(pre):
    return (jnp.minimum(pre, 0.0) - jnp.log1p(jnp.exp(-jnp.abs(pre)))) / GATE_NORM


def row_of(small_ref, row):
    return small_ref[ROW_MIXER:SMALL_ROWS, :].astype(F32)[row - ROW_MIXER : row - ROW_MIXER + 1, :]


def expand_of(small_ref):
    half = small_ref.shape[1] // 2
    quarter = half // 2
    part = small_ref[ROW_EXPAND:ROW_MIXER, :]
    return jnp.concatenate([part[:, :quarter], part[:, half : half + quarter]], axis=1)


def bias_of(small_ref):
    half = small_ref.shape[1] // 2
    quarter = half // 2
    row = row_of(small_ref, ROW_MIXED)
    return jnp.concatenate([row[:, :quarter], row[:, half : half + quarter]], axis=1)


def head_gain_of(small_ref):
    half = small_ref.shape[1] // 2
    at = half // 2
    count = DV // 2
    row = row_of(small_ref, ROW_MIXED)
    return jnp.concatenate([row[:, at : at + count], row[:, half + at : half + at + count]], axis=1)


def place_rows(who_ref, full_ref, own, pieces, number=1):
    x = who_ref[0]
    q = who_ref[number]
    half = own.shape[0]
    rows = pieces[0].shape[0]
    full_ref[pl.ds(pl.multiple_of(x * half, half), half), :] = own
    for k in range(len(pieces)):
        at = (1 - x) * half + (q ^ k) * rows
        full_ref[pl.ds(pl.multiple_of(at, rows), rows), :] = pieces[k]


def place_grads(who_ref, outs, scratch_ref, row, cols, rows=32):
    x = who_ref[0]
    me = who_ref[2]
    half = scratch_ref.shape[0] // 2
    keep, send_own, send_over = outs
    for core in range(2):
        for xx in range(2):
            out = (keep.at[xx], (send_own, send_over)[xx])[core]
            for yy in range(2):
                for zz in range(4):
                    block = me ^ (core * 8 + yy * 4 + zz)
                    at = pl.multiple_of((x ^ xx) * half + block * rows, rows)
                    out[yy, zz, row : row + rows, cols] = scratch_ref[pl.ds(at, rows), :]


def grads_out(rows, width, block=None, index=None):
    shapes = [(2, 2, 4, rows, width), (2, 4, rows, width), (2, 4, rows, width)]
    block = block or width
    index = index or (lambda *a: 0)
    specs = [
        pl.BlockSpec((*shape[:-1], block), lambda *a, n=len(shape): (0,) * (n - 1) + (index(*a),))
        for shape in shapes
    ]
    return [sds(shape, BF16) for shape in shapes], specs


def project_kernel(
    who, x, small, k_own, v_own, r0, r1, r2, r3, normed, kv, pre, narrow_out, full
):
    j = pl.program_id(0)

    @pl.when(j == 0)
    def _():
        tokens = x[...].astype(F32)
        mean_sq = jnp.mean(tokens * tokens, axis=-1, keepdims=True)
        normed[...] = (
            tokens * lax.rsqrt(mean_sq + EPSILON) * row_of(small, ROW_MIXER)
        ).astype(BF16)
        narrow = nt(normed[...], small[0:ROW_EXPAND, :]).astype(BF16)
        narrow_out[...] = narrow
        pre[...] = nn(narrow, expand_of(small)) + bias_of(small)

    pieces = [r[...] for r in (r0, r1, r2, r3)]

    @pl.when(j == 0)
    def _():
        place_rows(who, full, k_own[...], pieces)

    @pl.when(j >= 1)
    def _():
        place_rows(who, full, v_own[...], pieces)

    kv[...] = nn(normed[...], full[...]).astype(BF16)


def project(who, x, small, k_own, v_own, pieces):
    t, d = x.shape
    half = d // 2
    wide = HEADS * DK
    vn = HEADS * DV // wide
    const = lambda j: (0, 0)
    return call(
        project_kernel,
        (sds((t, d), BF16), sds((t, (1 + vn) * wide), BF16), sds((t, wide), F32), sds((t, 16), BF16)),
        grid=(1 + vn,),
        in_specs=[
            SMEM,
            pl.BlockSpec((t, d), const),
            pl.BlockSpec(small.shape, const),
            pl.BlockSpec((half, wide), const),
            pl.BlockSpec((half, wide), lambda j: (0, jnp.maximum(j - 1, 0))),
        ]
        + [pl.BlockSpec((half // 4, wide), lambda j: (0, j))] * 4,
        out_specs=(
            pl.BlockSpec((t, d), const),
            pl.BlockSpec((t, wide), lambda j: (0, j)),
            pl.BlockSpec((t, wide), const),
            pl.BlockSpec((t, 16), const),
        ),
        scratch_shapes=[pltpu.VMEM((d, wide), BF16)],
    )(who, x, small, k_own, v_own, *pieces)


def swish_kernel(who, normed, q_own, s_own, r0, r1, r2, r3, queries, swish, full):
    j = pl.program_id(0)
    pieces = [r[...] for r in (r0, r1, r2, r3)]

    @pl.when(j == 0)
    def _():
        place_rows(who, full, q_own[...], pieces)
        queries[...] = nn(normed[...], full[...]).astype(BF16)

    @pl.when(j >= 1)
    def _():
        place_rows(who, full, s_own[...], pieces)
        swish[...] = nn(normed[...], full[...])


def swish_project(who, normed, q_own, s_own, pieces):
    t, d = normed.shape
    half = d // 2
    wide = HEADS * DK
    vn = HEADS * DV // wide
    const = lambda j: (0, 0)
    high = lambda j: (0, jnp.maximum(j - 1, 0))
    return call(
        swish_kernel,
        (sds((t, wide), BF16), sds((t, vn * wide), F32)),
        grid=(1 + vn,),
        in_specs=[
            SMEM,
            pl.BlockSpec((t, d), const),
            pl.BlockSpec((half, wide), const),
            pl.BlockSpec((half, wide), high),
        ]
        + [pl.BlockSpec((half // 4, wide), lambda j: (0, j))] * 4,
        out_specs=(pl.BlockSpec((t, wide), const), pl.BlockSpec((t, wide), high)),
        scratch_shapes=[pltpu.VMEM((d, wide), BF16)],
    )(who, normed, q_own, s_own, *pieces)


def mark_at(mrow, place):
    return mrow[0:1, place : place + 1]


def state_kernel(kv, pre, mcol, mrow, payload, passing):
    t = pre.shape[0]
    kd = HEADS * DK
    ones = lower_ones(WIDE)
    states = [jnp.zeros((DV, DK), F32) for _ in range(HEADS)]
    total = jnp.zeros((1, kd), F32)
    for i in range(t // WIDE):
        rows = slice(i * WIDE, (i + 1) * WIDE)
        cumul = split_sum(ones, log_decay(pre[rows, :]))
        end = cumul[WIDE - 1 : WIDE, :]
        total = total + end
        last = mark_at(mrow, (i + 1) * WIDE - 1)
        keys = kv[rows, 0:kd].astype(F32)
        tail = jnp.where(mcol[rows, :] == last, keys * jnp.exp(end - cumul), 0.0).astype(BF16)
        if i:
            keep = jnp.where(mark_at(mrow, i * WIDE - 1) == last, jnp.exp(end), 0.0)
        for h in range(HEADS):
            c = slice(h * DK, (h + 1) * DK)
            values = kv[rows, kd + h * DV : kd + (h + 1) * DV]
            update = tn(values, tail[:, c])
            states[h] = states[h] * keep[:, c] + update if i else update
    for h in range(HEADS):
        payload[h * DV : (h + 1) * DV, :] = states[h].astype(BF16)
    last = mark_at(mrow, t - 1)
    payload[HEADS * DV :, :] = jnp.broadcast_to(last, (16, DK)).astype(BF16)
    passes = jnp.where(mark_at(mrow, 0) == last, jnp.exp(total), 0.0)
    passing[...] = jnp.broadcast_to(passes, passing.shape)


def local_state(kv, pre, mcol, mrow):
    return call(
        state_kernel,
        (sds((HEADS * DV + 16, DK), BF16), sds((8, HEADS * DK), F32)), us=5)(kv, pre, mcol, mrow)


def mixer_kernel(
    small, q, kv, pre, swish, mcol, mrow, payload, mixed_out, states_out, gated_out
):
    t = q.shape[0]
    kd = HEADS * DK
    ones = lower_ones(WIDE)
    causal_rows = lax.broadcasted_iota(jnp.int32, (WIDE, WIDE), 0)
    causal_cols = lax.broadcasted_iota(jnp.int32, (WIDE, WIDE), 1)
    states = [payload[h * DV : (h + 1) * DV, :].astype(F32) for h in range(HEADS)]
    before = payload[HEADS * DV :, :].astype(F32)[0:1, 0:1]
    for i in range(t // WIDE):
        rows = slice(i * WIDE, (i + 1) * WIDE)
        marks = mcol[rows, :]
        last = mark_at(mrow, (i + 1) * WIDE - 1)
        cumul = split_sum(ones, log_decay(pre[rows, :]))
        middle = cumul[SPAN - 1 : SPAN, :]
        end = cumul[WIDE - 1 : WIDE, :]
        queries = q[rows, :].astype(F32)
        keys = kv[rows, 0:kd].astype(F32)
        lifted = (queries * jnp.exp(cumul - middle)).astype(BF16)
        lowered = (keys * jnp.exp(middle - cumul)).astype(BF16)
        carried = jnp.where(marks == before, queries * jnp.exp(cumul), 0.0).astype(BF16)
        tail = jnp.where(marks == last, keys * jnp.exp(end - cumul), 0.0).astype(BF16)
        keep = jnp.where(before == last, jnp.exp(end), 0.0)
        causal = (causal_rows >= causal_cols) & (marks == mrow[0:1, rows])
        for h in range(HEADS):
            c = slice(h * DK, (h + 1) * DK)
            values = kv[rows, kd + h * DV : kd + (h + 1) * DV]
            low_state = states[h].astype(BF16)
            states_out[i, h] = low_state
            scores = jnp.where(causal, nt(lifted[:, c], lowered[:, c]), 0.0).astype(BF16)
            mixed_out[rows, h * DV : (h + 1) * DV] = nn(scores, values) + nt(
                carried[:, c], low_state
            )
            states[h] = states[h] * keep[:, c] + tn(values, tail[:, c])
        before = last
    gain = head_gain_of(small)
    for h in range(HEADS):
        c = slice(h * DV, (h + 1) * DV)
        mixed = mixed_out[:, c]
        scale = lax.rsqrt(jnp.mean(mixed * mixed, axis=-1, keepdims=True) + HEAD_FLOOR)
        pre_gate = swish[:, c]
        gated_out[:, c] = (mixed * scale * gain * (pre_gate * sigmoid(pre_gate))).astype(BF16)


def mixer(small, q, kv, pre, swish, mcol, mrow, payload):
    t = q.shape[0]
    vd = HEADS * DV
    outs = (
        sds((t, vd), F32),
        sds((t // WIDE, HEADS, DV, DK), BF16),
        sds((t, vd), BF16),
    )
    return call(mixer_kernel, outs, us=8)(small, q, kv, pre, swish, mcol, mrow, payload)


def reader_kernel(
    who, x, small, gated, own, r0, r1, r2, r3, hidden_out, second_out, full
):
    place_rows(who, full, own[...], [r[...] for r in (r0, r1, r2, r3)], 3)
    hidden = x[...].astype(F32) + nn(gated[...], full[...])
    hidden_out[...] = hidden
    mean_sq = jnp.mean(hidden * hidden, axis=-1, keepdims=True)
    second_out[...] = (
        hidden * lax.rsqrt(mean_sq + EPSILON) * row_of(small, ROW_FEED)
    ).astype(BF16)


def reader(who, x, small, gated, own, pieces):
    t, d = x.shape
    ins = (x, small, gated, own, *pieces)
    return call(
        reader_kernel,
        (sds((t, d), F32), sds((t, d), BF16)),
        us=3,
        in_specs=[SMEM] + [VMEM] * len(ins),
        scratch_shapes=[pltpu.VMEM((gated.shape[1], d), BF16)],
    )(who, *ins)


def feed_kernel(
    who, second, cot, g0, g1, u0, u1, down, r0, r1, r2, r3,
    part_out, part_ds, keep, send_own, send_over, wg, wu, wd, sec_t, sg_, su_, sd_, total_out, total_ds,
):
    j = pl.program_id(0)

    @pl.when(j == 0)
    def _():
        total_out[...] = jnp.zeros_like(total_out)
        total_ds[...] = jnp.zeros_like(total_ds)
        sec_t[...] = second[...].T

    x = who[0]
    q = who[1]
    half = g0.shape[0]
    rows = pl.ds(pl.multiple_of(x * half, half), half)
    wg[rows, 0:128] = g0[...]
    wg[rows, 128:256] = g1[...]
    wu[rows, 0:128] = u0[...]
    wu[rows, 128:256] = u1[...]
    wd[pl.ds(pl.multiple_of(x * 128, 128), 128), :] = down[...]
    for k, r in enumerate((r0, r1, r2, r3)):
        at = q ^ k
        rows = pl.ds(pl.multiple_of((1 - x) * half + at * 128, 128), 128)
        wg[rows, :] = r[:, 0:256]
        wu[rows, :] = r[:, 256:512]
        wd[pl.ds(pl.multiple_of((1 - x) * 128, 128), 128), pl.ds(pl.multiple_of(at * 256, 256), 256)] = r[:, 512:768]
    gate = nn(second[...], wg[...])
    upward = nn(second[...], wu[...])
    d_inner = nt(cot[...], wd[...])
    sig = sigmoid(gate)
    silu = gate * sig
    inner = (silu * upward).astype(BF16)
    d_gate = (d_inner * upward * sig * (1.0 + gate * (1.0 - sig))).astype(BF16)
    d_up = (d_inner * silu).astype(BF16)
    total_out[...] += nn(inner, wd[...])
    total_ds[...] += nt(d_gate, wg[...]) + nt(d_up, wu[...])
    sg_[...] = nn(sec_t[...], d_gate).astype(BF16)
    su_[...] = nn(sec_t[...], d_up).astype(BF16)
    grad_down = tn(inner, cot[...]).astype(BF16)
    for part in range(2):
        for cb in range(4):
            at = part * half + cb * 128
            sd_[at : at + 128, :] = grad_down[part * 128 : (part + 1) * 128, cb * 256 : (cb + 1) * 256]
    cols = slice(0, 256)
    outs = (keep, send_own, send_over)
    place_grads(who, outs, sg_, 0, cols)
    place_grads(who, outs, su_, 32, cols)
    place_grads(who, outs, sd_, 64, cols)

    @pl.when(j == pl.num_programs(0) - 1)
    def _():
        part_out[...] = total_out[...].astype(BF16)
        part_ds[...] = total_ds[...].astype(BF16)


def feed(who, second, cot, gate_own, up_own, down_own, pieces, start, blocks):
    t, d = second.shape
    half = d // 2
    ff = gate_own.shape[1]
    halves = ff // 256
    left = pl.BlockSpec((half, 128), lambda j: (0, start + j))
    right = pl.BlockSpec((half, 128), lambda j: (0, halves + start + j))
    full = pl.BlockSpec((t, d), lambda j: (0, 0))
    shapes, specs = grads_out(96, blocks * 256, 256, lambda j: j)
    return call(
        feed_kernel,
        (sds((t, d), BF16), sds((t, d), BF16), *shapes),
        us=1 + 4.5 * blocks,
        vmem=56,
        grid=(blocks,),
        in_specs=[
            SMEM, full, full, left, right, left, right,
            pl.BlockSpec((128, d), lambda j: (start + j, 0)),
        ]
        + [pl.BlockSpec((half // 4, 768), lambda j: (0, j))] * 4,
        out_specs=(full, full, *specs),
        scratch_shapes=[
            pltpu.VMEM((d, 256), BF16),
            pltpu.VMEM((d, 256), BF16),
            pltpu.VMEM((256, d), BF16),
            pltpu.VMEM((d, t), BF16),
            pltpu.VMEM((d, 256), BF16),
            pltpu.VMEM((d, 256), BF16),
            pltpu.VMEM((d, 256), BF16),
            pltpu.VMEM((t, d), F32),
            pltpu.VMEM((t, d), F32),
        ],
    )(who, second, cot, gate_own, gate_own, up_own, up_own, down_own, *pieces)


def pack_kernel(who, g0, g1, u0, u1, down, out):
    out[:, 0:128] = g0[...]
    out[:, 128:256] = g1[...]
    out[:, 256:384] = u0[...]
    out[:, 384:512] = u1[...]
    out[:, 512:768] = down[...]


def pack_feed(who, gate_own, up_own, down_own, start, blocks):
    half, ff = gate_own.shape
    halves = ff // 256
    quarter = half // 4
    left = pl.BlockSpec((quarter, 128), lambda j, w: (w[1], start + j))
    right = pl.BlockSpec((quarter, 128), lambda j, w: (w[1], halves + start + j))
    return pl.pallas_call(
        pack_kernel,
        out_shape=sds((quarter, blocks * 768), BF16),
        cost_estimate=cost(blocks),
        grid_spec=pltpu.PrefetchScalarGridSpec(
            num_scalar_prefetch=1,
            grid=(blocks,),
            in_specs=[
                left, right, left, right,
                pl.BlockSpec((128, down_own.shape[1] // 4), lambda j, w: (start + j, w[1])),
            ],
            out_specs=pl.BlockSpec((quarter, 768), lambda j, w: (0, j)),
        ),
    )(who, gate_own, gate_own, up_own, up_own, down_own)


def mixer_back_kernel(
    who, small, s0, s1, s2, hidden, cot, swish, mixed, q, pre, mcol, payload,
    own, r0, r1, r2, r3,
    d_hidden_out, low_out, d_swish_out, d_mixed_out, rows_out, back_out, full, d_gated,
):
    t, d = hidden.shape
    kd = HEADS * DK
    place_rows(who, full, own[...], [r[...] for r in (r0, r1, r2, r3)], 3)
    values = hidden[...]
    upstream = s0[...].astype(F32) + s1[...].astype(F32) + s2[...].astype(F32)
    scale = lax.rsqrt(jnp.mean(values * values, axis=-1, keepdims=True) + EPSILON)
    rows_out[...] = jnp.zeros_like(rows_out)
    rows_out[0:1, :] = jnp.sum(upstream * values * scale, axis=0, keepdims=True)
    scaled = upstream * row_of(small, ROW_FEED)
    mean = jnp.mean(scaled * values, axis=-1, keepdims=True)
    d_hidden = cot[...].astype(F32) + scale * scaled - values * (scale * scale * scale * mean)
    d_hidden_out[...] = d_hidden
    low_out[...] = d_hidden.astype(BF16)
    d_gated[...] = nt(low_out[...], full[...])
    gain = head_gain_of(small)
    grad_heads = jnp.zeros((1, DV), F32)
    for h in range(HEADS):
        c = slice(h * DV, (h + 1) * DV)
        values = mixed[:, c]
        scale = lax.rsqrt(jnp.mean(values * values, axis=-1, keepdims=True) + HEAD_FLOOR)
        pre_gate = swish[:, c]
        sig = sigmoid(pre_gate)
        up = d_gated[:, c]
        unit = values * scale
        d_swish_out[:, c] = (up * unit * gain * sig * (1.0 + pre_gate * (1.0 - sig))).astype(BF16)
        err = up * pre_gate * sig
        grad_heads = grad_heads + jnp.sum(err * unit, axis=0, keepdims=True)
        scaled = err * gain
        mean = jnp.mean(scaled * unit, axis=-1, keepdims=True)
        d_mixed_out[:, c] = (scale * (scaled - unit * mean)).astype(BF16)
    rows_out[1:2, 0:DV] = grad_heads
    ones = lower_ones(WIDE)
    before = payload[HEADS * DV :, :].astype(F32)[0:1, 0:1]
    base = jnp.zeros((1, kd), F32)
    sums = [jnp.zeros((DV, DK), F32) for _ in range(HEADS)]
    for i in range(t // WIDE):
        rows = slice(i * WIDE, (i + 1) * WIDE)
        cumul = split_sum(ones, log_decay(pre[rows, :])) + base
        base = cumul[WIDE - 1 : WIDE, :]
        queries = q[rows, :].astype(F32)
        carried = jnp.where(mcol[rows, :] == before, queries * jnp.exp(cumul), 0.0).astype(BF16)
        for h in range(HEADS):
            sums[h] = sums[h] + tn(
                d_mixed_out[rows, h * DV : (h + 1) * DV], carried[:, h * DK : (h + 1) * DK]
            )
    for h in range(HEADS):
        back_out[h * DV : (h + 1) * DV, :] = sums[h].astype(BF16)


def mixer_back(who, small, d_second, hidden, cot, swish, mixed, q, pre, mcol, payload, own, pieces):
    t, d = hidden.shape
    vd = HEADS * DV
    whole = lambda a: pl.BlockSpec(a.shape, lambda i: (0,) * len(a.shape))
    outs = (
        sds((t, d), F32),
        sds((t, d), BF16),
        sds((t, vd), BF16),
        sds((t, vd), BF16),
        sds((8, d), F32),
        sds((HEADS * DV, DK), BF16),
    )
    ins = (small, *d_second, hidden, cot, swish, mixed, q, pre, mcol, payload, own, *pieces)
    return call(
        mixer_back_kernel,
        outs,
        grid=(1,),
        in_specs=[SMEM] + [whole(a) for a in ins],
        out_specs=tuple(whole(a) for a in outs),
        scratch_shapes=[pltpu.VMEM((vd, d), BF16), pltpu.VMEM((t, vd), F32)], us=11)(who, *ins)


def gate_grads_kernel(
    who, normed, d_swish, gated, low, keep, send_own, send_over, scratch, left_t
):
    j = pl.program_id(0)
    count = d_swish.shape[1]
    half = pl.num_programs(0) // 2

    @pl.when(j == 0)
    def _():
        left_t[...] = normed[...].T

    @pl.when(j == half)
    def _():
        left_t[...] = gated[...].T

    @pl.when(j < half)
    def _():
        scratch[...] = nn(left_t[...], d_swish[...]).astype(BF16)

    @pl.when(j >= half)
    def _():
        scratch[...] = nn(left_t[...], low[...]).astype(BF16)

    place_grads(who, (keep, send_own, send_over), scratch, 0, slice(0, 256))


def gate_grads(who, normed, d_swish, gated, low):
    t, d = normed.shape
    n = d_swish.shape[1] // 256
    const = lambda j: (0, 0)
    shapes, specs = grads_out(32, 2 * n * 256, 256, lambda j: j)
    return call(
        gate_grads_kernel,
        shapes,
        grid=(2 * n,),
        in_specs=[
            SMEM,
            pl.BlockSpec((t, d), const),
            pl.BlockSpec((t, 256), lambda j: (0, jnp.minimum(j, n - 1))),
            pl.BlockSpec((t, d), const),
            pl.BlockSpec((t, 256), lambda j: (0, jnp.maximum(j - n, 0))),
        ],
        out_specs=specs,
        scratch_shapes=[pltpu.VMEM((d, 256), BF16), pltpu.VMEM((d, t), BF16)], us=9)(who, normed, d_swish, gated, low)


def recurrence_back_kernel(
    small, q, kv, pre, d_mixed, mcol, mrow, payload, states, entering,
    d_qkv, d_pre_out, d_narrow_out, bias_out,
):
    t = pre.shape[0]
    kd = HEADS * DK
    ones = lower_ones(WIDE)
    reverse = upper_ones(WIDE)
    causal_rows = lax.broadcasted_iota(jnp.int32, (WIDE, WIDE), 0)
    causal_cols = lax.broadcasted_iota(jnp.int32, (WIDE, WIDE), 1)
    grads = [entering[h * DV : (h + 1) * DV, :].astype(F32) for h in range(HEADS)]
    bias_sum = jnp.zeros((1, kd), F32)
    for i in reversed(range(t // WIDE)):
        rows = slice(i * WIDE, (i + 1) * WIDE)
        marks = mcol[rows, :]
        last = mark_at(mrow, (i + 1) * WIDE - 1)
        if i:
            before = mark_at(mrow, i * WIDE - 1)
        else:
            before = payload[HEADS * DV :, :].astype(F32)[0:1, 0:1]
        pre_here = pre[rows, :]
        cumul = split_sum(ones, log_decay(pre_here))
        middle = cumul[SPAN - 1 : SPAN, :]
        end = cumul[WIDE - 1 : WIDE, :]
        queries = q[rows, :].astype(F32)
        keys = kv[rows, 0:kd].astype(F32)
        lift = jnp.exp(cumul - middle)
        sink = jnp.exp(middle - cumul)
        rise = jnp.where(marks == before, jnp.exp(cumul), 0.0)
        fall = jnp.where(marks == last, jnp.exp(end - cumul), 0.0)
        lifted = (queries * lift).astype(BF16)
        lowered = (keys * sink).astype(BF16)
        carried = (queries * rise).astype(BF16)
        tail = (keys * fall).astype(BF16)
        keep = jnp.where(before == last, jnp.exp(end), 0.0)
        causal = (causal_rows >= causal_cols) & (marks == mrow[0:1, rows])
        slopes = []
        ends = []
        for h in range(HEADS):
            c = slice(h * DK, (h + 1) * DK)
            values = kv[rows, kd + h * DV : kd + (h + 1) * DV]
            up = d_mixed[rows, h * DV : (h + 1) * DV]
            state = states[i, h]
            grad = grads[h]
            low_grad = grad.astype(BF16)
            scores = jnp.where(causal, nt(lifted[:, c], lowered[:, c]), 0.0).astype(BF16)
            d_scores = jnp.where(causal, nt(up, values), 0.0).astype(BF16)
            d_lifted = nn(d_scores, lowered[:, c])
            d_lowered = tn(d_scores, lifted[:, c])
            d_carried = nn(up, state)
            d_tail = nn(values, low_grad)
            d_values = tn(scores, up) + nt(tail[:, c], low_grad)
            d_qkv[rows, c] = (d_lifted * lift[:, c] + d_carried * rise[:, c]).astype(BF16)
            d_qkv[rows, kd + h * DK : kd + (h + 1) * DK] = (
                d_lowered * sink[:, c] + d_tail * fall[:, c]
            ).astype(BF16)
            d_qkv[rows, 2 * kd + h * DV : 2 * kd + (h + 1) * DV] = d_values.astype(BF16)
            tail_term = tail[:, c].astype(F32) * d_tail
            slopes.append(
                lifted[:, c].astype(F32) * d_lifted
                - lowered[:, c].astype(F32) * d_lowered
                + carried[:, c].astype(F32) * d_carried
                - tail_term
            )
            kept = keep[:, c] * grad
            ends.append(
                jnp.sum(tail_term, axis=0, keepdims=True)
                + jnp.sum(kept * state.astype(F32), axis=0, keepdims=True)
            )
            grads[h] = kept + tn(up, carried[:, c])
        d_decay = split_sum(reverse, jnp.concatenate(slopes, axis=1)) + jnp.concatenate(ends, axis=1)
        d_pre = d_decay * sigmoid(-pre_here) / GATE_NORM
        bias_sum = bias_sum + jnp.sum(d_pre, axis=0, keepdims=True)
        d_pre_out[rows, :] = d_pre.astype(BF16)
    bias_out[...] = jnp.broadcast_to(bias_sum, bias_out.shape)
    d_narrow_out[...] = nt(d_pre_out[...], expand_of(small)).astype(BF16)


def recurrence_back(small, q, kv, pre, d_mixed, mcol, mrow, payload, states, entering):
    t = q.shape[0]
    width = q.shape[1] + kv.shape[1]
    return call(
        recurrence_back_kernel,
        (
            sds((t, width), BF16),
            sds(pre.shape, BF16),
            sds((t, 16), BF16),
            sds((8, HEADS * DK), F32),
        ), us=11)(small, q, kv, pre, d_mixed, mcol, mrow, payload, states, entering)


def input_back_kernel(
    who, x, small, d_hidden, d_qkv, d_swish, d_narrow, q_own, k_own, v_own, s_own,
    a0, a1, a2, a3, b0, b1, b2, b3, grad_input, mixer_out, total, full,
):
    j = pl.program_id(0)
    steps = pl.num_programs(0)
    first = [r[...] for r in (a0, a1, a2, a3)]
    other = [r[...] for r in (b0, b1, b2, b3)]

    @pl.when(j == 0)
    def _():
        place_rows(who, full, q_own[...], other)
        total[...] = nn(d_narrow[...], small[0:ROW_EXPAND, :]) + nt(d_qkv[...], full[...])

    @pl.when(j == 1)
    def _():
        place_rows(who, full, k_own[...], first)

    @pl.when((j >= 2) & (j < 4))
    def _():
        place_rows(who, full, v_own[...], first)

    @pl.when((j >= 1) & (j < 4))
    def _():
        total[...] += nt(d_qkv[...], full[...])

    @pl.when(j >= 4)
    def _():
        place_rows(who, full, s_own[...], other)
        total[...] += nt(d_swish[...], full[...])

    @pl.when(j == steps - 1)
    def _():
        values = x[...].astype(F32)
        upstream = total[...]
        scale = lax.rsqrt(jnp.mean(values * values, axis=-1, keepdims=True) + EPSILON)
        unit = values * scale
        mixer_out[...] = jnp.broadcast_to(
            jnp.sum(upstream * unit, axis=0, keepdims=True), mixer_out.shape
        )
        scaled = upstream * row_of(small, ROW_MIXER)
        mean = jnp.mean(scaled * unit, axis=-1, keepdims=True)
        grad_input[...] = (d_hidden[...] + scale * (scaled - unit * mean)).astype(BF16)


def input_back(who, x, small, d_hidden, d_qkv, d_swish, d_narrow, owns, pieces, gate_pieces):
    t, d = x.shape
    half = d // 2
    wide = HEADS * DK
    vn = HEADS * DV // wide
    const = lambda j: (0, 0)
    col = lambda low, count: (lambda j: (0, jnp.clip(j - low, 0, count - 1)))
    beyond = lambda j: (0, jnp.clip(j - 1 - vn, 0, vn))
    return call(
        input_back_kernel,
        (sds((t, d), BF16), sds((8, d), F32)),
        us=10,
        grid=(2 + 2 * vn,),
        in_specs=[
            SMEM,
            pl.BlockSpec((t, d), const),
            pl.BlockSpec(small.shape, const),
            pl.BlockSpec((t, d), const),
            pl.BlockSpec((t, wide), col(0, 2 + vn)),
            pl.BlockSpec((t, wide), col(2 + vn, vn)),
            pl.BlockSpec((t, 16), const),
            pl.BlockSpec((half, wide), const),
            pl.BlockSpec((half, wide), const),
            pl.BlockSpec((half, wide), col(2, vn)),
            pl.BlockSpec((half, wide), col(2 + vn, vn)),
        ]
        + [pl.BlockSpec((half // 4, wide), col(1, 1 + vn))] * 4
        + [pl.BlockSpec((half // 4, wide), beyond)] * 4,
        out_specs=(pl.BlockSpec((t, d), const), pl.BlockSpec((8, d), const)),
        scratch_shapes=[pltpu.VMEM((t, d), F32), pltpu.VMEM((d, wide), BF16)],
    )(who, x, small, d_hidden, d_qkv, d_swish, d_narrow, *owns, *pieces, *gate_pieces)


def late_grads_kernel(
    who, normed, d_qkv, d_narrow, narrow, d_pre, rows_in, bias_in, mixer_in,
    keep, send_own, send_over, scratch, strip, left_t, rows,
):
    t, d = normed.shape
    half = d // 2
    kd = HEADS * DK
    n = d_qkv.shape[1] // 256
    left_t[...] = normed[...].T
    for j in range(n):
        c = slice(j * 256, (j + 1) * 256)
        scratch[...] = nn(left_t[...], d_qkv[:, c]).astype(BF16)
        place_grads(who, (keep, send_own, send_over), scratch, 0, c)
    rows[...] = jnp.zeros_like(rows)
    rows[LANE_FEED : LANE_FEED + 1, :] = rows_in[0:1, :]
    rows[LANE_MIXER : LANE_MIXER + 1, :] = mixer_in[0:1, :]
    part = kd // 2
    rows[LANE_BIAS : LANE_BIAS + 1, 0:part] = bias_in[0:1, 0:part]
    rows[LANE_BIAS : LANE_BIAS + 1, half : half + part] = bias_in[0:1, part:kd]
    part = DV // 2
    rows[LANE_HEADS : LANE_HEADS + 1, 0:part] = rows_in[1:2, 0:part]
    rows[LANE_HEADS : LANE_HEADS + 1, half : half + part] = rows_in[1:2, part:DV]
    columns = rows[...].T
    squeeze = nn(left_t[...], d_narrow[...])
    expand = tn(d_pre[...], narrow[...])
    part = kd // 2
    strip[...] = columns.astype(BF16)
    strip[:, 0:16] = squeeze.astype(BF16)
    strip[0:part, LANE_EXPAND : LANE_EXPAND + 16] = expand[0:part].astype(BF16)
    strip[half : half + part, LANE_EXPAND : LANE_EXPAND + 16] = expand[part:kd].astype(BF16)
    place_grads(who, (keep, send_own, send_over), strip, 0, slice(n * 256, n * 256 + 128))


def late_grads(who, normed, d_qkv, d_narrow, narrow, d_pre, rows_in, bias_in, mixer_in):
    t, d = normed.shape
    shapes, specs = grads_out(32, d_qkv.shape[1] + 128)
    whole = lambda a: pl.BlockSpec(a.shape, lambda i: (0,) * len(a.shape))
    ins = (normed, d_qkv, d_narrow, narrow, d_pre, rows_in, bias_in, mixer_in)
    return call(
        late_grads_kernel,
        shapes,
        us=10,
        grid=(1,),
        in_specs=[SMEM] + [whole(a) for a in ins],
        out_specs=specs,
        scratch_shapes=[
            pltpu.VMEM((d, 256), BF16),
            pltpu.VMEM((d, 128), BF16),
            pltpu.VMEM((d, t), BF16),
            pltpu.VMEM((128, d), F32),
        ],
    )(who, *ins)


def settle_kernel(who, a, b, c, d, *outs):
    me = who[2]
    for k, part in enumerate((a, b, c, d)):
        for zz in range(4):
            rows = pl.ds(pl.multiple_of((me ^ (k * 4 + zz)) * 32, 32), 32)
            at = 0
            for out in outs:
                count = out.shape[1]
                out[rows, :] = part[zz, :, at : at + count].astype(F32)
                at += count


def last_settle_kernel(
    who, a, b, c, d, query, key, value, squeeze, expand, feed, bias, heads, mixer, strip
):
    me = who[2]
    wide = query.shape[1] + key.shape[1] + value.shape[1]
    for k, part in enumerate((a, b, c, d)):
        for zz in range(4):
            rows = pl.ds(pl.multiple_of((me ^ (k * 4 + zz)) * 32, 32), 32)
            at = 0
            for out in (query, key, value):
                count = out.shape[1]
                out[rows, :] = part[zz, :, at : at + count].astype(F32)
                at += count
            strip[rows, :] = part[zz, :, wide:].astype(F32)
    turned = strip[...].T
    squeeze[...] = turned[0:16, :]
    expand[...] = strip[0 : expand.shape[0], LANE_EXPAND : LANE_EXPAND + 16]
    feed[...] = turned[LANE_FEED : LANE_FEED + 1, :]
    bias[...] = turned[LANE_BIAS : LANE_BIAS + 1, 0 : bias.shape[1]]
    heads[...] = turned[LANE_HEADS : LANE_HEADS + 1, 0 : heads.shape[1]]
    mixer[...] = turned[LANE_MIXER : LANE_MIXER + 1, :]


def last_settle(who, parts, half):
    kd, vd = HEADS * DK, HEADS * DV
    shapes = [(half, kd), (half, kd), (half, vd), (16, half), (kd // 2, 16)]
    shapes += [(1, half), (1, kd // 2), (1, DV // 2), (1, half)]
    return call(
        last_settle_kernel,
        [sds(shape, F32) for shape in shapes],
        in_specs=[SMEM] + [VMEM] * 4,
        scratch_shapes=[pltpu.VMEM((half, 128), F32)],
    )(who, *parts)


def settle(who, parts, half, widths):
    shapes = tuple(sds((half, width), F32) for width in widths)
    return call(settle_kernel, shapes, us=4, in_specs=[SMEM] + [VMEM] * 4)(who, *parts)


def feed_settle_kernel(who, a, b, c, d, *rest, first):
    gate, up, down = rest if first else rest[3:]
    h = pl.program_id(1)
    me = who[2]
    for k, part in enumerate((a, b, c, d)):
        for zz in range(4):
            block = me ^ (k * 4 + zz)
            rows = pl.ds(pl.multiple_of(block * 32, 32), 32)
            gate[rows, :] = part[zz, 0:32, :].astype(F32)
            up[rows, :] = part[zz, 32:64, :].astype(F32)
            at = pl.ds(pl.multiple_of((block % 4) * 32, 32), 32)
            cols = pl.ds(pl.multiple_of((block // 4) * 256 + h * 128, 128), 128)
            down[at, cols] = part[zz, 64:96, :].astype(F32)


def feed_settle(who, parts, before, start, blocks, half, ff, d):
    halves = ff // 256
    first = before is None
    shapes = (sds((half, ff), F32), sds((half, ff), F32), sds((ff // 2, d), F32))
    wide = pl.BlockSpec((half, 128), lambda j, h: (0, h * halves + start + j))
    tall = pl.BlockSpec((128, d), lambda j, h: (start + j, 0))
    any_spec = pl.BlockSpec(memory_space=pl.ANY)
    return call(
        functools.partial(feed_settle_kernel, first=first),
        shapes,
        us=2 * blocks,
        grid=(blocks, 2),
        in_specs=[SMEM]
        + [pl.BlockSpec((4, 96, 128), lambda j, h: (0, 0, 2 * j + h))] * 4
        + ([] if first else [any_spec] * 3),
        out_specs=(wide, wide, tall),
        input_output_aliases={} if first else {5: 0, 6: 1, 7: 2},
    )(who, *parts, *(() if first else before))


def added(*terms):
    total = terms[0].astype(F32)
    for term in terms[1:]:
        total = total + term.astype(F32)
    return total.astype(BF16)


def summed(first, *rest):
    for term in rest:
        first = first + term.astype(F32)
    return first.astype(BF16)


def swap(v, bit):
    count = lax.axis_size("replica")
    return lax.ppermute(v, "replica", [(i, i ^ bit) for i in range(count)])


def cross(v):
    return lax.ppermute(v, "fsdp", [(0, 1), (1, 0)])


def tied(v, *after):
    return lax.optimization_barrier((v,) + after)[0]


def fenced(go, *jobs):
    work = lambda: tuple(job() for job in jobs)
    shapes = jax.eval_shape(work)
    blank = lambda: jax.tree.map(lambda a: jnp.zeros(a.shape, a.dtype), shapes)
    return lax.cond(go, work, blank)


class Part:
    def __init__(self, keep, got):
        self.keep = keep
        self.got = got


class Chain:
    def __init__(self, *parts):
        self.parts = parts

    def blocks(self, y, k, *more):
        at, sums = 0, []
        for part in self.parts:
            width = part.keep.shape[-1]
            cut = [a[..., at : at + width] for a in more]
            sums.append(added(part.keep[0, y, k], part.got[y, k], part.over[y, k], *cut))
            at += width
        return sums[0] if len(sums) == 1 else jnp.concatenate(sums, axis=-1)

    def to_y(self, now):
        last = self.parts[-1]
        last.over = tied(last.over, now)
        return self.blocks(1, slice(None))

    def to_near(self, now):
        side = tied(self.side, now)
        odd = slice(1, 4, 2)
        return self.blocks(0, odd, side[odd])

    def to_far(self, now):
        return self.blocks(0, 2, self.side[2], tied(self.near, now)[1])

    def own_of_far(self, now):
        self.own = self.blocks(0, 0, self.side[0], self.near[0], tied(self.far, now))
        return self.own

    def back_near(self, now):
        self.pair = jnp.stack([self.own, tied(self.far, now)])
        return self.pair

    def back_y(self, now):
        near = tied(self.near, now)
        self.line = jnp.stack([self.pair[0], near[0], self.pair[1], near[1]])
        return self.line

    def gathered(self, now):
        beside = tied(self.beside, now)
        return (self.line, beside, swap(tied(self.line, beside), 1), swap(beside, 1))


def over_core(keep, send_over):
    return added(keep[1], swap(send_over, 1))


def natural(keep, send_own, send_over):
    both = jnp.stack([keep, jnp.stack([send_own, send_over])])
    both = jnp.moveaxis(both, 0, 1)
    return both.reshape((2, 16) + keep.shape[3:])


def total_over(v, dim):
    v = lax.psum_scatter(v.astype(BF16), "fsdp", scatter_dimension=dim, tiled=True)
    return lax.psum(v, "replica").astype(F32)


def chain_join(earlier, later):
    factor_early, state_early, first_early, last_early = earlier
    factor_late, state_late, first_late, last_late = later
    joined = (first_late == last_early) | (last_early < 0) | (first_late < 0)
    linked = jnp.where(joined, factor_late, 0.0)
    return (
        linked * factor_early,
        linked[:, None] * state_early + state_late,
        jnp.where(first_early < 0, first_late, first_early),
        jnp.where(last_late < 0, last_early, last_late),
    )


def chained(payload, passing, first_mark):
    place = lax.axis_index("fsdp")
    own = (
        passing[0].reshape(HEADS, DK).astype(BF16),
        payload,
        first_mark.astype(BF16),
    )
    factors, payloads, firsts = [lax.all_gather(a, "fsdp") for a in own]
    rows = HEADS * DV

    def one(turn, carry):
        pick = lambda a: lax.dynamic_index_in_dim(a, turn, 0, False).astype(F32)
        factor, block, first = pick(factors), pick(payloads), pick(firsts)
        later = (factor, block[:rows].reshape(HEADS, DV, DK), first, block[rows, :1])
        earlier_factor, state, earlier_first, earlier_last = carry
        joined = (later[2] == earlier_last) | (earlier_last < 0)
        linked = jnp.where(joined, later[0], 0.0)
        return (
            linked * earlier_factor,
            linked[:, None, :] * state + later[1],
            jnp.where(earlier_first < 0, later[2], earlier_first),
            later[3],
        )

    none = -jnp.ones((1,), F32)
    start = (jnp.ones((HEADS, DK), F32), jnp.zeros((HEADS, DV, DK), F32), none, none)
    done = lax.fori_loop(0, place, one, start)
    marks = jnp.broadcast_to(done[3][:, None], (16, DK))
    return jnp.concatenate([done[1].reshape(rows, DK), marks]).astype(BF16)


def chained_back(back, passing, linked):
    count = lax.axis_size("fsdp")
    ahead = count - 1 - lax.axis_index("fsdp")
    factor = jnp.where(linked, passing[0], 0.0).reshape(HEADS, DK).astype(BF16)
    factors, backs = [lax.all_gather(a, "fsdp") for a in (factor, back)]

    def one(turn, grad):
        source = count - 1 - turn
        pick = lambda a: lax.dynamic_index_in_dim(a, source, 0, False).astype(F32)
        return pick(backs).reshape(HEADS, DV, DK) + pick(factors)[:, None, :] * grad

    grad = lax.fori_loop(0, ahead, one, jnp.zeros((HEADS, DV, DK), F32))
    return grad.reshape(HEADS * DV, DK).astype(BF16)


def on_device(
    inputs, segments, cotangent, mixer_gain, query_map, key_map, value_map, swish_map, squeeze,
    expand, forget_bias, head_gain, readout, feed_gain, gate_map, up_map, down_map,
):
    shards = lax.axis_size("fsdp")
    copies = lax.axis_size("replica")
    paired = shards == 2 and copies == 16
    t, d = inputs.shape
    kd, vd = HEADS * DK, HEADS * DV
    half = d // 2
    quarter = half // 4
    marks = segments[0].astype(F32)
    mcol, mrow = marks[:, None], marks[None, :]

    if paired:
        place = lax.axis_index("replica")
        core, side, deep = place % 2, (place // 2) % 2, place // 4
        x = lax.axis_index("fsdp")
        q = side * 2 + core
        q_deep = (deep % 2) * 2 + core
        who = jnp.stack([x, q, core * 8 + side * 4 + deep, q_deep]).astype(jnp.int32)
    else:
        who = jnp.zeros((4,), jnp.int32)
        x = q = 0
        gather = lambda a, dim=0: lax.all_gather(a, "fsdp", axis=dim, tiled=True)
        query_map, key_map, value_map, swish_map, readout, gate_map, up_map, down_map = [
            gather(a)
            for a in (query_map, key_map, value_map, swish_map, readout, gate_map, up_map, down_map)
        ]
        mixer_gain, feed_gain, forget_bias, head_gain, squeeze = [
            gather(a) for a in (mixer_gain, feed_gain, forget_bias, head_gain, squeeze)
        ]
        expand = gather(expand, 1)

    def small_half(k):
        cut = lambda a, dim=0: lax.slice_in_dim(a, k * (a.shape[dim] // 2), (k + 1) * (a.shape[dim] // 2), axis=dim)
        return packed(cut(squeeze), cut(expand, 1), cut(mixer_gain), cut(feed_gain), cut(forget_bias), cut(head_gain))

    def packed(squeeze, expand, mixer_gain, feed_gain, forget_bias, head_gain):
        wide = lambda a: jnp.pad(a, ((0, 0), (0, half - a.shape[1])))
        mixed = jnp.concatenate([forget_bias, head_gain])[None]
        rows = [squeeze.T, wide(expand), mixer_gain[None], feed_gain[None], wide(mixed)]
        block = jnp.concatenate(rows)
        return jnp.pad(block, ((0, SMALL_ROWS - block.shape[0]), (0, 0)))

    ff = gate_map.shape[1]
    halves = ff // 256
    counts = chunk_blocks(halves)
    starts = [sum(counts[:i]) for i in range(len(counts))]

    def quarter_rows(a, k):
        return lax.dynamic_slice_in_dim(a, k * quarter, quarter, 0)

    if paired:
        return paired_device(
            who, x, q, q_deep, mcol, mrow, inputs, cotangent, query_map, key_map, value_map, swish_map,
            readout, gate_map, up_map, down_map,
            packed(squeeze, expand, mixer_gain, feed_gain, forget_bias, head_gain),
            starts, counts,
        )
    small = jnp.concatenate([small_half(0), small_half(1)], axis=1)
    lower = lambda a: a[: a.shape[0] // 2]
    upper = lambda a: a[a.shape[0] // 2 :]
    share = lambda maps: tuple(
        jnp.concatenate([quarter_rows(upper(a), k) for a in maps], axis=1) for k in range(4)
    )
    kv_pieces = share((key_map, value_map))
    gate_pieces = share((query_map, swish_map))
    read_pieces = share((readout,))
    others = (upper(gate_map), upper(up_map), upper(down_map))
    feed_pieces = [
        tuple(
            pack_feed(jnp.full((4,), k, jnp.int32), *others, s, n) for k in range(4)
        )
        for s, n in zip(starts, counts)
    ]
    query_map, key_map, value_map, swish_map, readout, gate_map, up_map, down_map = [
        lower(a)
        for a in (query_map, key_map, value_map, swish_map, readout, gate_map, up_map, down_map)
    ]

    normed, kv, pre, narrow = project(who, inputs, small, key_map, value_map, kv_pieces)
    local, passing = local_state(kv, pre, mcol, mrow)
    payload = chained(local, passing, marks[:1])
    queries, swish = swish_project(who, normed, query_map, swish_map, gate_pieces)
    mixed, states, gated = mixer(small, queries, kv, pre, swish, mcol, mrow, payload)
    hidden, second = reader(who, inputs, small, gated, readout, read_pieces)

    feed_grads, out_parts, second_parts = [], [], []
    for s, n, pieces in zip(starts, counts, feed_pieces):
        out_part, second_part, *grads = feed(
            who, second, cotangent, gate_map, up_map, down_map, pieces, s, n
        )
        out_parts.append(out_part)
        second_parts.append(second_part)
        feed_grads.append(grads)
    output = summed(hidden, *out_parts)

    d_hidden, low, d_swish, d_mixed, rows, back = mixer_back(
        who, small, second_parts, hidden, cotangent, swish, mixed, queries, pre, mcol, payload,
        readout, read_pieces,
    )
    linked = marks[0] == payload[HEADS * DV, 0].astype(F32)
    entering = chained_back(back, passing, linked)
    gate_grad = gate_grads(who, normed, d_swish, gated, low)
    d_qkv, d_pre, d_narrow, bias_row = recurrence_back(
        small, queries, kv, pre, d_mixed, mcol, mrow, payload, states, entering
    )
    grad_input, mixer_row = input_back(
        who, inputs, small, d_hidden, d_qkv, d_swish, d_narrow,
        (query_map, key_map, value_map, swish_map), kv_pieces, gate_pieces,
    )
    late_grad = late_grads(
        who, normed, d_qkv, d_narrow, narrow, d_pre, rows, bias_row, mixer_row
    )

    gates, ups, downs = [], [], []
    for grads, n in zip(feed_grads, counts):
        block = natural(*grads)
        sides = lambda k: block[:, :, 32 * k : 32 * (k + 1), :].reshape(d, n, 2, 128)
        gates.append(sides(0))
        ups.append(sides(1))
        part = block[:, :, 64:96, :].reshape(2, 4, 128, n, 256)
        downs.append(part.transpose(0, 3, 2, 1, 4).reshape(2, n * 128, d))
    whole = lambda parts: jnp.concatenate(parts, axis=1).transpose(0, 2, 1, 3).reshape(d, ff)
    grad_gate, grad_up = whole(gates), whole(ups)
    grad_down = jnp.concatenate(downs, axis=1).reshape(ff, d)
    flat = lambda pair: natural(*pair).reshape(d, -1)
    gate_flat, late_flat = flat(gate_grad), flat(late_grad)
    strip = late_flat[:, 2 * kd + vd :]
    joined = lambda lane, count: jnp.concatenate(
        [strip[:count, lane], strip[half : half + count, lane]]
    )
    part = kd // 2
    grad_expand = jnp.concatenate([strip[:part, 16:32], strip[half : half + part, 16:32]]).T
    results = (
        joined(LANE_MIXER, half), late_flat[:, :kd], late_flat[:, kd : 2 * kd],
        late_flat[:, 2 * kd : 2 * kd + vd],
        gate_flat[:, :vd], strip[:, :16], grad_expand, joined(LANE_BIAS, part),
        joined(LANE_HEADS, DV // 2), gate_flat[:, vd:], joined(LANE_FEED, half),
        grad_gate, grad_up, grad_down,
    )
    return (output, grad_input) + tuple(
        total_over(a, 1 if i == 6 else 0) for i, a in enumerate(results)
    )


def paired_device(
    who, x, q, q_deep, mcol, mrow, inputs, cotangent, query_map, key_map, value_map, swish_map,
    readout, gate_map, up_map, down_map, small_own, starts, counts,
):
    t, d = inputs.shape
    half = d // 2
    quarter = half // 4
    kd = HEADS * DK
    ff = gate_map.shape[1]

    def share(maps):
        cut = lambda a: lax.dynamic_slice_in_dim(a, q * quarter, quarter, 0)
        return jnp.concatenate([cut(a) for a in maps], axis=1)

    def spread(first, *after):
        second = swap(first, 2)
        return (first, swap(first, 1), second, swap(second, 1))

    go = x < 2
    vd = HEADS * DV

    def together(*values):
        return lax.optimization_barrier(values)

    def core_step(grads, *after, weights=()):
        keep, send_own, send_over = grads
        out, *swapped = fenced(
            tied(go, send_over, *after),
            lambda: over_core(keep, send_over),
            *((lambda v=v: swap(v, 1)) for v in weights),
        )
        return Part(keep, swap(tied(send_own, out), 1)), out, *swapped

    small_other = cross(small_own)
    kv_share = share((key_map, value_map))
    kv_first = cross(kv_share)
    gate_share = share((tied(query_map, kv_share), swish_map))
    read_share = lax.dynamic_slice_in_dim(tied(readout, kv_share), q_deep * quarter, quarter, 0)
    def pack(i, *after):
        return pack_feed(tied(who, *after), gate_map, up_map, down_map, starts[i], counts[i])

    feed_shares = [pack(0, gate_share, read_share)]
    kv_first, small_other, gate_share, read_share, feed_shares[0] = together(
        kv_first, small_other, gate_share, read_share, feed_shares[0]
    )
    kv_second, kv_third = swap(kv_first, 2), swap(kv_first, 1)
    gate_first = cross(gate_share)
    small = jnp.concatenate(
        [jnp.where(x == 0, small_own, small_other), jnp.where(x == 0, small_other, small_own)],
        axis=1,
    )
    feed_shares += [pack(1, kv_first), pack(2, kv_first)]
    gate_first, kv_second, kv_third, *feed_shares = together(
        gate_first, kv_second, kv_third, *feed_shares
    )
    kv_pieces = (kv_first, kv_third, kv_second, swap(kv_second, 1))
    gate_second, gate_third = swap(gate_first, 2), swap(gate_first, 1)
    f0_first = cross(tied(feed_shares[0], gate_first))
    normed, kv, pre, narrow = project(
        tied(who, gate_first), inputs, small, key_map, value_map, kv_pieces
    )
    local, _ = local_state(kv, pre, mcol, tied(mrow, normed))
    gate_second, f0_first, local = together(gate_second, f0_first, local)
    gate_fourth, f0_third = together(swap(gate_second, 1), swap(f0_first, 1))
    gate_pieces = (gate_first, gate_third, gate_second, gate_fourth)
    payload, (queries, swish), read_first, f0_second = fenced(
        tied(go, local, gate_fourth, f0_third),
        lambda: lax.ppermute(local, "fsdp", [(0, 1)]),
        lambda: swish_project(who, normed, query_map, swish_map, gate_pieces),
        lambda: cross(read_share),
        lambda: swap(f0_first, 2),
    )
    f0_fourth = swap(f0_second, 1)
    f0_pieces = (f0_first, f0_third, f0_second, f0_fourth)
    read_second, read_third = swap(read_first, 4), swap(read_first, 1)
    f1_first = cross(tied(feed_shares[1], swish))
    mixed, states, gated = mixer(
        tied(small, swish), queries, kv, pre, swish, mcol, mrow, payload
    )
    gated, read_second, read_third, f0_fourth = together(
        gated, read_second, read_third, f0_fourth
    )
    f0_pieces = (f0_first, f0_third, f0_second, f0_fourth)
    read_pieces = (read_first, read_third, read_second, swap(read_second, 1))
    hidden, second = reader(tied(who, gated), inputs, small, gated, readout, read_pieces)
    f1_first, hidden = together(f1_first, hidden)
    f1_second, f1_third = swap(f1_first, 2), swap(f1_first, 1)
    f2_first = cross(tied(feed_shares[2], f1_first))

    def feed_part(i, pieces, *after):
        out_part, second_part, *grads = feed(
            tied(who, *after), second, cotangent, gate_map, up_map, down_map, pieces, starts[i],
            counts[i],
        )
        out_parts.append(out_part)
        second_parts.append(second_part)
        return grads

    out_parts, second_parts = [], []
    grads = feed_part(0, f0_pieces, hidden)
    part0, out, f1_fourth = core_step(grads, f1_third, f1_second, weights=(f1_second,))
    f1_pieces = (f1_first, f1_third, f1_second, f1_fourth)
    f2_first, out = together(f2_first, out)
    part0.over = cross(out)
    f2_second, f2_third = swap(f2_first, 2), swap(f2_first, 1)
    grads = feed_part(1, f1_pieces, out)
    part1, out, f2_fourth = core_step(grads, f2_second, f2_third, weights=(f2_second,))
    f2_pieces = (f2_first, f2_third, f2_second, f2_fourth)
    f0, f1 = Chain(part0), Chain(part1)
    a = f0.to_y(out)
    a, out = together(a, out)
    part1.over = cross(out)
    f0.side = swap(a, 2)
    keep, send_own, send_over = feed_part(2, f2_pieces, a)
    a = f0.to_near(keep)
    f0.near = swap(a, 4)
    back_parts, f2_out, got = fenced(
        tied(go, a),
        lambda: mixer_back(
            who, small, second_parts, hidden, cotangent, swish, mixed, queries, pre, mcol,
            payload, readout, read_pieces,
        ),
        lambda: over_core(keep, send_over),
        lambda: swap(send_own, 1),
    )
    d_hidden, low, d_swish, d_mixed, rows, back = back_parts
    part2 = Part(keep, got)
    f2 = Chain(part2)
    a, b = f0.to_far(back), f1.to_y(back)
    a, b, back, f2_out = together(a, b, back, f2_out)
    part2.over = cross(f2_out)
    entering = lax.ppermute(back, "fsdp", [(1, 0)])
    f0.far = swap(a, 8)
    f1.side = swap(b, 2)
    keep, send_own, send_over = gate_grads(tied(who, a), normed, d_swish, gated, low)
    a = f0.own_of_far(keep)
    a, entering = together(a, entering)
    f0.far = swap(a, 8)
    (d_qkv, d_pre, d_narrow, bias_row), g_out, got = fenced(
        tied(go, a),
        lambda: recurrence_back(
            small, queries, kv, pre, d_mixed, mcol, mrow, payload, states, entering
        ),
        lambda: over_core(keep, send_over),
        lambda: swap(send_own, 1),
    )
    part_g = Part(keep, got)
    g = Chain(part_g)
    a, b = f0.back_near(d_qkv), f1.to_near(d_qkv)
    a, b, g_out = together(a, b, g_out)
    part_g.over = cross(g_out)
    f0.near, f1.near = swap(a, 4), swap(b, 4)
    grad_input, mixer_row = input_back(
        tied(who, a), inputs, small, d_hidden, d_qkv, d_swish, d_narrow,
        (query_map, key_map, value_map, swish_map), kv_pieces, gate_pieces,
    )
    a, b, c = f0.back_y(mixer_row), f1.to_far(mixer_row), f2.to_y(mixer_row)
    a, b, c = together(a, b, c)
    f2.side, f1.far, a0 = swap(c, 2), swap(b, 8), a
    grads = late_grads(
        tied(who, a), normed, d_qkv, d_narrow, narrow, d_pre, rows, bias_row, mixer_row
    )
    c = g.to_y(grads[0])
    part_v, v_out = core_step(grads, c)
    v = Chain(part_v)
    a, b = f1.own_of_far(v_out), f2.to_near(v_out)
    a, b, c, line0, v_out = together(a, b, c, a0, v_out)
    part_v.over = cross(v_out)
    f1.far, f2.near, g.side = swap(a, 8), swap(b, 4), swap(c, 2)
    now = f1.back_near(c)
    f1.near = swap(now, 4)
    f0.beside = swap(tied(line0, now), 2)
    now = f2.to_far(now)
    f2.far = swap(now, 8)
    now = g.to_near(now)
    g.near = swap(now, 4)
    output = summed(tied(hidden, now), *out_parts)
    now = f2.own_of_far(output)
    f2.far = swap(now, 8)
    now = v.to_y(now)
    v.side = swap(now, 2)
    now = f1.back_y(now)
    f1.beside = swap(now, 2)
    now = g.to_far(now)
    g.far = swap(now, 8)
    now = f2.back_near(now)
    f2.near = swap(now, 4)
    f0_parts = f0.gathered(now)
    feeds = feed_settle(tied(who, now), f0_parts, None, starts[0], counts[0], half, ff, d)
    now = v.to_near(feeds[0])
    v.near = swap(now, 4)
    now = g.own_of_far(now)
    g.far = swap(now, 8)
    now = f2.back_y(now)
    f2.beside = swap(now, 2)
    now = v.to_far(now)
    v.far = swap(now, 8)
    now = g.back_near(now)
    g.near = swap(now, 4)
    now = v.own_of_far(now)
    v.far = swap(now, 8)
    f1_parts = f1.gathered(now)
    feeds = feed_settle(tied(who, now), f1_parts, feeds, starts[1], counts[1], half, ff, d)
    now = v.back_near(feeds[0])
    v.near = swap(now, 4)
    now = g.back_y(now)
    g.beside = swap(now, 2)
    f2_parts = f2.gathered(now)
    now = v.back_y(now)
    v.beside = swap(now, 2)
    feeds = feed_settle(tied(who, now), f2_parts, feeds, starts[2], counts[2], half, ff, d)
    g_parts = g.gathered(feeds[0])
    grad_swish, grad_readout = settle(tied(who, feeds[0]), g_parts, half, (vd, vd))
    v_parts = v.gathered(grad_swish)
    grad_query, grad_key, grad_value, squeeze_t, expand_t, *small_grads = last_settle(
        tied(who, grad_swish), v_parts, half
    )
    grad_feed, grad_bias, grad_heads, grad_mixer = [a[0] for a in small_grads]
    grad_gate, grad_up, grad_down = feeds
    return (
        output, grad_input, grad_mixer, grad_query, grad_key, grad_value, grad_swish,
        squeeze_t.T, expand_t.T, grad_bias, grad_heads, grad_readout, grad_feed,
        grad_gate, grad_up, grad_down,
    )


def chunk_blocks(halves):
    parts = 3
    base, extra = divmod(halves, parts)
    return [base + (1 if i >= parts - extra else 0) for i in range(parts)]


def solution(mesh):
    placed = (
        P(("replica", "fsdp"), None),
        P("replica", "fsdp"),
        P(("replica", "fsdp"), None),
        P("fsdp"),
        P("fsdp", None),
        P("fsdp", None),
        P("fsdp", None),
        P("fsdp", None),
        P("fsdp", None),
        P(None, "fsdp"),
        P("fsdp"),
        P("fsdp"),
        P("fsdp", None),
        P("fsdp"),
        P("fsdp", None),
        P("fsdp", None),
        P("fsdp", None),
    )
    return jax.shard_map(
        on_device,
        mesh=mesh,
        in_specs=placed,
        out_specs=(
            P(("replica", "fsdp"), None),
            P(("replica", "fsdp"), None),
            P("fsdp"),
            P("fsdp", None),
            P("fsdp", None),
            P("fsdp", None),
            P("fsdp", None),
            P("fsdp", None),
            P(None, "fsdp"),
            P("fsdp"),
            P("fsdp"),
            P("fsdp", None),
            P("fsdp"),
            P("fsdp", None),
            P("fsdp", None),
            P("fsdp", None),
        ),
        check_vma=False,
    )
```
